256 devices in a mesh: group: 8 (over x_hi, y), fsdp: 32 (over z, x_lo, core).
Axes of the slice: x: 4 (x_hi: 2, x_lo: 2; x = x_hi * 2 + x_lo), y: 4, z: 8, core: 2. Of those that a mesh axis runs over, the one named last changes fastest.
Arguments:
- hidden: bfloat16 [8, 4096, 2048], P('group', 'fsdp'), may hold values from -10 to 10
- gain: float32 [8, 2048], P('group'), may hold values from 0.5 to 4
- weights: float32 [8, 2048, 2560], P('group', 'fsdp'), may hold values from -0.088388348 to 0.088388348
- momentum: float32 [8, 2048, 2560], P('group', 'fsdp'), may hold values from -6 to 6
- cotangent: bfloat16 [8, 4096, 2048], P('group', 'fsdp'), may hold values from -0.75 to 0.75
- segment: int32 [8, 4096], P('group', 'fsdp'), may hold values from 0 to 2, never falling along the last dimension, each value on 1 to 3072 neighbouring positions
- distance: int32 [1], replicated, may hold values from 0 to 1023
Outputs:
- attn_out: bfloat16 [8, 4096, 2048], P('group', 'fsdp')
- new_weights: float32 [8, 2048, 2560], P('group', 'fsdp')
- new_momentum: float32 [8, 2048, 2560], P('group', 'fsdp')
The draws below stay inside these ranges and needn't reach their ends.
All inputs are finite; a program needn't handle non-finite values.
Results may differ from the reference program's by a relative error of at most 0.03.
Values may be sent and summed in bfloat16 or wider, within the bound.
No kernel may reach another device: no remote copies, remote signals or barrier semaphores. Data moves between devices by JAX's collectives and lax.ppermute only.
A program may use at most 128 MiB of HBM per device.

```python
import math
import jax
import jax.numpy as jnp
import numpy as np
from jax import lax

D = 2048
QUERY_HEADS = 16
KEY_VALUE_HEADS = 4
HEAD_SIZE = 64
DEVICE_TOKENS = 128
DOCS = 3
GROUPS = 8
GROUP_LENGTH = 4096
QKVO = 2560


def draw_gain(key, part):
    key = jax.random.fold_in(key, 11)
    return jax.random.uniform(key, (GROUPS, D), jnp.float32, 0.6, 1.6)


def draw_hidden(key, part):
    key = jax.random.fold_in(key, 21)
    noise_key = jax.random.fold_in(key, 0)
    base = jax.random.normal(noise_key, (GROUPS, GROUP_LENGTH, D), jnp.float32)
    return jnp.clip(base, -6.0, 6.0).astype(jnp.bfloat16)


def draw_weights(key, part):
    key = jax.random.fold_in(key, 23)
    base = jax.random.normal(key, (GROUPS, D, QKVO), jnp.float32) * D ** (-0.5)
    bound = 4.0 * D ** (-0.5)
    return jnp.clip(base, -bound, bound)


def level_of(stream_key, dims, cuts, low, top_value):
    def one(axis_at, shards_of):
        draws = jax.random.uniform(jax.random.fold_in(jax.random.fold_in(stream_key, 6), axis_at), (shards_of,), jnp.float32, low / len(cuts), top_value / len(cuts))
        return jnp.repeat(jnp.exp(draws), dims[axis_at] // shards_of).reshape((-1,) + (1,) * (len(dims) - axis_at - 1))

    level = one(*cuts[0])
    for cut in cuts[1:]:
        level = level * one(*cut)
    return level


def length_profile(amount, total, most, lean):
    portions = [(1 << 20) // math.isqrt(standing ** lean) + 1 for standing in range(2, amount + 1)]
    spare, given = total - most - (amount - 1), [1] * (amount - 1)
    while spare > 0:
        movable = [i for i in range(amount - 1) if given[i] < most]
        whole, remaining = sum([portions[i] for i in movable]), spare
        for i in movable:
            more = min(most - given[i], max(1, remaining * portions[i] // whole), spare)
            given[i] = given[i] + more
            spare = spare - more
    return np.array([most] + given)


def ragged_sizes(rng, count, total, reach, lean):
    if count == 2:
        one = jax.random.randint(rng, (), max(1, total - reach), min(reach, total - 1) + 1)
        return jnp.stack([one, total - one])
    sizes = jnp.asarray(length_profile(count, total, reach, lean), jnp.int32)
    pairs = (count - 1) // 2
    donor, taker = sizes[1:1 + 2 * pairs:2], sizes[2:2 + 2 * pairs:2]
    slack = jnp.minimum(donor - 1, reach - taker)
    shifted = jax.random.randint(jax.random.fold_in(rng, 1), (pairs,), 0, 1 << 20) % (slack + 1)
    sizes = sizes.at[1:1 + 2 * pairs:2].set(donor - shifted).at[2:2 + 2 * pairs:2].set(taker + shifted)
    return sizes[jax.random.permutation(jax.random.fold_in(rng, 2), count)]


def noise(key, extent, scale, most, pieces=(), kind=jnp.bfloat16):
    factor_of = level_of(key, extent, pieces, -0.22, 0.18) if pieces else 1.0
    values = jax.random.normal(key, extent, jnp.float32) * scale * factor_of
    return jnp.minimum(jnp.maximum(values, -most), most).astype(kind)


def setup_inputs(seed: int = 0) -> dict:
    streams_of = jax.random.split(jax.random.key(seed), 8)
    hidden = draw_hidden(jax.random.fold_in(streams_of[7], 71), 0)
    gain = draw_gain(jax.random.fold_in(streams_of[7], 71), 0)
    weights = draw_weights(jax.random.fold_in(streams_of[7], 71), 0)
    momentum = noise(streams_of[3], (GROUPS, D, QKVO), 1.0, 6.0, ((0, 8), (1, 32)), jnp.float32)
    cotangent = noise(streams_of[4], (GROUPS, GROUP_LENGTH, D), (3.0 / GROUP_LENGTH ** 0.5), 0.75, ((0, 8), (1, 32)))
    segment = jax.vmap(lambda own: jnp.searchsorted(jnp.cumsum(ragged_sizes(own, DOCS, GROUP_LENGTH, GROUP_LENGTH * 3 // 4, 0)), jnp.arange(GROUP_LENGTH), side="right"))(jax.random.split(streams_of[5], GROUPS)).reshape((GROUPS, GROUP_LENGTH)).astype(jnp.int32)
    distance = jax.random.randint(streams_of[6], (1,), 0, 1024).astype(jnp.int32)
    return {"hidden": hidden, "gain": gain, "weights": weights, "momentum": momentum, "cotangent": cotangent, "segment": segment, "distance": distance}


EPS = 1e-05
BETA = 0.9
RATE = 0.01
THETA = 500000.0
MASK_FILL = -1e+30

def widen_float(value_block):
    return lax.optimization_barrier(value_block.astype(jnp.bfloat16)).astype(jnp.float32)

def apply_rotary(value_block, token_positions, heads, sign):
    rows = value_block.shape[0]
    half = HEAD_SIZE // 2
    freq = jnp.power(THETA, -jnp.arange(half, dtype=jnp.float32) * 2.0 / HEAD_SIZE)
    angle = token_positions.astype(jnp.float32)[:, None] * freq[None, :]
    cosine = jnp.concatenate([jnp.cos(angle), jnp.cos(angle)], axis=1)[:, None, :]
    sine = sign * jnp.concatenate([jnp.sin(angle), jnp.sin(angle)], axis=1)[:, None, :]
    shaped = value_block.reshape(rows, heads, HEAD_SIZE)
    turned = jnp.concatenate([-shaped[..., half:], shaped[..., :half]], axis=2)
    return (shaped * cosine + turned * sine).reshape(rows, heads * HEAD_SIZE)

def one_group(hidden, gain, weights, momentum, cotangent, segment):
    query_width = QUERY_HEADS * HEAD_SIZE
    key_value_width = KEY_VALUE_HEADS * HEAD_SIZE
    proj_cols = query_width + 2 * key_value_width
    head_repeat = QUERY_HEADS // KEY_VALUE_HEADS
    score_scale = 1.0 / math.sqrt(HEAD_SIZE)
    master = weights.astype(jnp.bfloat16)
    local = hidden.astype(jnp.float32)
    normed = (local * lax.rsqrt(lax.optimization_barrier(jnp.mean(local * local, axis=1, keepdims=True)) + EPS) * gain[None, :]).astype(jnp.bfloat16)
    output_projection = jnp.dot(normed, master[:, :proj_cols], preferred_element_type=jnp.float32)
    out_full = master[:, proj_cols:]
    token_positions = jnp.arange(GROUP_LENGTH, dtype=jnp.int32)
    query_rows = apply_rotary(output_projection[:, :query_width], token_positions, QUERY_HEADS, 1.0).astype(jnp.bfloat16)
    key = apply_rotary(output_projection[:, query_width:query_width + key_value_width], token_positions, KEY_VALUE_HEADS, 1.0).astype(jnp.bfloat16)
    value_rows = output_projection[:, query_width + key_value_width:].astype(jnp.bfloat16)
    key_block3 = key.astype(jnp.float32).reshape(GROUP_LENGTH, KEY_VALUE_HEADS, HEAD_SIZE)
    value_block3 = value_rows.astype(jnp.float32).reshape(GROUP_LENGTH, KEY_VALUE_HEADS, HEAD_SIZE)
    mixed_gradient = jnp.dot(cotangent, out_full, preferred_element_type=jnp.float32).astype(jnp.bfloat16)

    def block_step(carry, index):
        dk_acc, dv_acc = carry
        block_start = (index * DEVICE_TOKENS).astype(jnp.int32)
        query_block = lax.dynamic_slice_in_dim(query_rows, block_start, DEVICE_TOKENS, 0).astype(jnp.float32).reshape(DEVICE_TOKENS, KEY_VALUE_HEADS, head_repeat, HEAD_SIZE)
        qpos = block_start + jnp.arange(DEVICE_TOKENS, dtype=jnp.int32)
        qseg = lax.dynamic_slice_in_dim(segment, block_start, DEVICE_TOKENS, 0)
        allowed = (token_positions[None, :] <= qpos[:, None]) & (segment[None, :] == qseg[:, None])
        unscaled_scores = jnp.einsum('imbp,emp->mbie', query_block, key_block3) * score_scale
        unscaled_scores = jnp.where(allowed[None, None], unscaled_scores, MASK_FILL)
        top = lax.optimization_barrier(jnp.max(unscaled_scores, axis=3, keepdims=True))
        expo = jnp.where(allowed[None, None], jnp.exp(unscaled_scores - top), 0.0)
        probability = widen_float(expo / lax.optimization_barrier(jnp.sum(expo, axis=3, keepdims=True)))
        mixed_output = jnp.einsum('lcia,alq->ilcq', probability, value_block3).reshape(DEVICE_TOKENS, query_width).astype(jnp.bfloat16)
        momentum_gradient = lax.dynamic_slice_in_dim(mixed_gradient, block_start, DEVICE_TOKENS, 0).astype(jnp.float32).reshape(DEVICE_TOKENS, KEY_VALUE_HEADS, head_repeat, HEAD_SIZE)
        softmax_delta = lax.optimization_barrier(jnp.sum(momentum_gradient * mixed_output.astype(jnp.float32).reshape(DEVICE_TOKENS, KEY_VALUE_HEADS, head_repeat, HEAD_SIZE), axis=3)).transpose(1, 2, 0)
        probability_gradient = jnp.einsum('imbp,emp->mbie', momentum_gradient, value_block3)
        score_gradient = widen_float(probability * (probability_gradient - softmax_delta[..., None]))
        query_gradient = jnp.einsum('lcia,alq->ilcq', score_gradient, key_block3).reshape(DEVICE_TOKENS, query_width) * score_scale
        key_gradient_block = widen_float((jnp.einsum('zfcx,czfm->xzm', score_gradient, query_block) * score_scale).reshape(GROUP_LENGTH, key_value_width))
        value_gradient_block = widen_float(jnp.einsum('zfcx,czfm->xzm', probability, momentum_gradient).reshape(GROUP_LENGTH, key_value_width))
        return ((dk_acc + key_gradient_block, dv_acc + value_gradient_block), (mixed_output, query_gradient))
    zeros_kv = jnp.zeros((GROUP_LENGTH, key_value_width), jnp.float32)
    blocks = jnp.arange(GROUP_LENGTH // DEVICE_TOKENS, dtype=jnp.int32)
    (key_gradient_sum, dv_sum), (mixed_blocks, dq_blocks) = lax.scan(block_step, (zeros_kv, zeros_kv), blocks)
    mixed_all = mixed_blocks.reshape(GROUP_LENGTH, query_width)
    dq_all = dq_blocks.reshape(GROUP_LENGTH, query_width)
    attn = jnp.dot(mixed_all, out_full.T, preferred_element_type=jnp.float32).astype(jnp.bfloat16)
    d_query = apply_rotary(dq_all, token_positions, QUERY_HEADS, -1.0).astype(jnp.bfloat16)
    key_gradient = apply_rotary(key_gradient_sum, token_positions, KEY_VALUE_HEADS, -1.0).astype(jnp.bfloat16)
    d_value = dv_sum.astype(jnp.bfloat16)
    d_proj = jnp.concatenate([d_query, key_gradient, d_value], axis=1)

    def grad_step(total, index):
        block_start = (index * DEVICE_TOKENS).astype(jnp.int32)
        rows_n = lax.dynamic_slice_in_dim(normed, block_start, DEVICE_TOKENS, 0)
        rows_d = lax.dynamic_slice_in_dim(d_proj, block_start, DEVICE_TOKENS, 0)
        rows_c = lax.dynamic_slice_in_dim(cotangent, block_start, DEVICE_TOKENS, 0)
        rows_m = lax.dynamic_slice_in_dim(mixed_all, block_start, DEVICE_TOKENS, 0)
        term = jnp.concatenate([jnp.dot(rows_n.T, rows_d, preferred_element_type=jnp.float32), jnp.dot(rows_c.T, rows_m, preferred_element_type=jnp.float32)], axis=1)
        return (total + widen_float(term), None)
    grad, unused = lax.scan(grad_step, jnp.zeros((D, QKVO), jnp.float32), blocks)
    new_m = BETA * momentum + grad
    new_w = weights - RATE * new_m
    return (attn, new_w, new_m)

def reference(hidden, gain, weights, momentum, cotangent, segment, distance):
    attn, stepped_w, stepped_m = lax.map(lambda items: one_group(*items), (hidden, gain, weights, momentum, cotangent, segment))
    bit_count = GROUPS.bit_length() - 1
    pair_bit = jnp.remainder(distance[0], bit_count).astype(jnp.int32)
    partner = jnp.bitwise_xor(jnp.arange(GROUPS, dtype=jnp.int32), jnp.left_shift(jnp.int32(1), pair_bit))
    new_weights = 0.5 * (stepped_w + stepped_w[partner])
    new_momentum = 0.5 * (stepped_m + stepped_m[partner])
    return (attn, new_weights, new_momentum)
```

```python
import functools
import math

import jax
import jax.numpy as jnp
from jax import lax
from jax.experimental import pallas as pl
from jax.experimental.pallas import tpu as pltpu
from jax.sharding import PartitionSpec as P

QUERY_HEADS = 16
KEY_VALUE_HEADS = 4
HEAD_SIZE = 64
REPEAT = QUERY_HEADS // KEY_VALUE_HEADS

EPS = 1e-05
BETA = 0.9
RATE = 0.01
THETA = 500000.0
MASK_FILL = -1e30
TOP_START = -1e20

PLANES = 8
SIDE = 4
TOKENS = 512
ROWS = 256
QKV = 384
WO = 256
VMEM = pltpu.CompilerParams(vmem_limit_bytes=56 * 1024 * 1024)
NT = (((1,), (1,)), ((), ()))
NN = (((1,), (0,)), ((), ()))

f32 = jnp.float32
bf16 = jnp.bfloat16


def dot(a, b, dims=NN):
    return lax.dot_general(a, b, dims, preferred_element_type=f32)


def along(x, step):
    n = PLANES * SIDE
    return lax.ppermute(x, "fsdp", [(i, (i + SIDE * step) % n) for i in range(n)])


def beside(x, mask):
    return lax.ppermute(x, "fsdp", [(i, i ^ mask) for i in range(PLANES * SIDE)])


def ring_gather(x):
    got = [None] * PLANES
    got[0] = x
    down = up = x
    for s in range(1, PLANES // 2 + 1):
        down = along(down, 1)
        got[-s % PLANES] = down
        if s < PLANES // 2:
            up = along(up, -1)
            got[s] = up
    return got


def ring_scatter(terms):
    add = lambda a, b: a.astype(f32) + b.astype(f32)
    up = down = None
    for s in range(PLANES // 2, 0, -1):
        t = terms[-s % PLANES]
        down = along(t if down is None else add(down, t).astype(bf16), -1)
        if s < PLANES // 2:
            t = terms[s]
            up = along(t if up is None else add(up, t).astype(bf16), 1)
    return add(add(down, up), terms[0])


def call(kernel, out_shape, n_smem, n_in, cost, alias=None):
    flops, bytes_, exps = cost
    return pl.pallas_call(
        kernel,
        out_shape=out_shape,
        in_specs=[pl.BlockSpec(memory_space=pltpu.SMEM)] * n_smem
        + [pl.BlockSpec(memory_space=pltpu.VMEM)] * n_in,
        out_specs=jax.tree.map(lambda _: pl.BlockSpec(memory_space=pltpu.VMEM), out_shape),
        input_output_aliases=alias or {},
        compiler_params=VMEM,
        cost_estimate=pl.CostEstimate(flops=flops, bytes_accessed=bytes_, transcendentals=exps),
    )


def plane_at(info, offset):
    return lax.rem(info[0] + (offset % PLANES), PLANES)


def lanes(shape):
    return lax.broadcasted_iota(jnp.int32, shape, len(shape) - 1)


def proj_kernel(info, normed, cos, sin, out_rows, *refs):
    blocks, (q_out, kv_out) = refs[:PLANES], refs[PLANES:]
    total = jnp.zeros((TOKENS, QKV), f32)
    for o in range(PLANES):
        at = pl.multiple_of(plane_at(info, o) * ROWS, ROWS)
        total = total + dot(normed[:, pl.ds(at, ROWS)], blocks[o][:ROWS])
    lane = lanes((TOKENS, 128))
    first = lax.rem(lane, HEAD_SIZE) < HEAD_SIZE // 2
    low = lane < HEAD_SIZE
    c, s = cos[...], sin[...]

    def turned(u):
        return jnp.where(first, pltpu.roll(u, 96, 1), pltpu.roll(u, 32, 1))

    for pair in range(2):
        u = total[:, 128 * pair : 128 * pair + 128]
        u = (u * c + turned(u) * s) * (1.0 / math.sqrt(HEAD_SIZE))
        q_out[2 * pair] = jnp.where(low, u, 0.0).astype(bf16)
        q_out[2 * pair + 1] = jnp.where(low, pltpu.roll(u, 64, 1), 0.0).astype(bf16)
    u = total[:, 256:]
    kv_out[:TOKENS] = jnp.where(low, u * c + turned(u) * s, u).astype(bf16)
    kv_out[TOKENS : TOKENS + ROWS] = out_rows[:, :128]
    kv_out[TOKENS + ROWS :] = out_rows[:, 128:]


def out_block(ref):
    return jnp.concatenate([ref[TOKENS : TOKENS + ROWS], ref[TOKENS + ROWS :]], axis=1)


def masked(s, src, qpos, start):
    kpos = src * TOKENS + lax.broadcasted_iota(jnp.int32, (TOKENS, TOKENS), 0)
    return jnp.where((kpos <= qpos) & (kpos >= start), s, MASK_FILL)


def on_block(info, src, body):
    base = src * TOKENS
    seen = (src <= info[0]) & (base + TOKENS > info[1])
    edge = (src == info[0]) | (base < info[2])

    @pl.when(seen & edge)
    def _():
        body(True)

    @pl.when(seen & jnp.logical_not(edge))
    def _():
        body(False)


def positions(info):
    return info[0] * TOKENS + lax.broadcasted_iota(jnp.int32, (1, TOKENS), 1)


def fwd_block(info, offset, q, kv, start, rows, acc):
    src = plane_at(info, offset)

    def body(mask):
        block = kv[:TOKENS]
        value_t = block.T[HEAD_SIZE:]
        for h in range(REPEAT):
            s = dot(block, q[h], NT)
            if mask:
                s = masked(s, src, positions(info), start[...])
            old = rows[h : h + 1]
            top = jnp.maximum(old, jnp.max(s, axis=0, keepdims=True))
            p = jnp.exp(s - top)
            fade = jnp.exp(old - top)
            rows[h : h + 1] = top
            rows[4 + h : 5 + h] = rows[4 + h : 5 + h] * fade + jnp.sum(p, axis=0, keepdims=True)
            at = slice(64 * h, 64 * h + 64)
            acc[at] = acc[at] * fade + dot(value_t, p.astype(bf16))

    on_block(info, src, body)


def fwd_kernel(offsets, info, q, start, *refs):
    n = len(offsets)
    kvs, refs = refs[:n], refs[n:]
    if offsets[0] == 0:
        rows, acc = refs
        rows[0:4] = jnp.full((4, TOKENS), TOP_START, f32)
        rows[4:8] = jnp.zeros((4, TOKENS), f32)
        acc[...] = jnp.zeros(acc.shape, f32)
    else:
        rows_in, acc_in, rows, acc = refs
        rows[...] = rows_in[...]
        acc[...] = acc_in[...]
    for o, kv in zip(offsets, kvs):
        fwd_block(info, o, q, kv, start, rows, acc)


def mid_kernel(info, rows, acc, cot, *refs):
    blocks, (mixed_t, d_out, back_rows, attn, grads) = refs[:PLANES], refs[PLANES:]
    d_mixed = jnp.zeros((TOKENS, WO), f32)
    for o in range(PLANES):
        at = pl.multiple_of(plane_at(info, o) * ROWS, ROWS)
        d_mixed = d_mixed + dot(cot[:, pl.ds(at, ROWS)], out_block(blocks[o]))
    d_mixed = d_mixed.astype(bf16).astype(f32)
    inverse = 1.0 / rows[4:8]
    back_rows[0:4] = rows[0:4]
    for h in range(REPEAT):
        at = slice(64 * h, 64 * h + 64)
        mixed_t[at] = (acc[at] * inverse[h : h + 1]).astype(bf16)
    mt = mixed_t[...]
    prod = d_mixed.T * mt.astype(f32)
    for h in range(REPEAT):
        back_rows[4 + h : 5 + h] = inverse[h : h + 1] * jnp.sum(
            prod[64 * h : 64 * h + 64], axis=0, keepdims=True
        )
    by_row = jnp.concatenate([inverse, inverse], axis=0).T
    high = lanes((TOKENS, 128)) >= HEAD_SIZE
    for pair in range(2):
        u = d_mixed[:, 128 * pair : 128 * pair + 128]
        scale = [by_row[:, 2 * pair + i : 2 * pair + i + 1] for i in range(2)]
        u = u * jnp.where(high, scale[1], scale[0])
        d_out[2 * pair] = jnp.where(high, pltpu.roll(u, 64, 1), 0.0).astype(bf16)
        d_out[2 * pair + 1] = jnp.where(high, u, 0.0).astype(bf16)
    mixed = mt.astype(f32).T.astype(bf16)
    for o in range(PLANES):
        at = pl.multiple_of(plane_at(info, o) * ROWS, ROWS)
        attn[:, pl.ds(at, ROWS)] = dot(mixed, out_block(blocks[o]), NT).astype(bf16)
        term = dot(mt, cot[:, pl.ds(at, ROWS)]).astype(bf16)
        grads[o, :ROWS] = term[:, :128]
        grads[o, ROWS:] = term[:, 128:]


def bwd_block(info, offset, q, d_out, rows, kv, start, acc, out):
    src = plane_at(info, offset)

    def body(mask):
        block = kv[:TOKENS]
        key_t = block.T[:HEAD_SIZE]
        total = out[...]
        for h in range(REPEAT):
            s = dot(block, q[h], NT)
            if mask:
                s = masked(s, src, positions(info), start[...])
            p = jnp.exp(s - rows[h : h + 1])
            dp = dot(block, d_out[h], NT)
            ds = (p * (dp - rows[4 + h : 5 + h])).astype(bf16)
            total = total + dot(p.astype(bf16), d_out[h]) + dot(ds, q[h])
            at = slice(64 * h, 64 * h + 64)
            acc[at] = acc[at] + dot(key_t, ds)
        out[...] = total

    on_block(info, src, body)


def bwd_kernel(offsets, n_got, info, q, d_out, rows, start, grads, *refs):
    n = len(offsets)
    kvs, refs = refs[:n], refs[n:]
    gots, refs = refs[:n_got], refs[n_got:]
    first = n_got == 0
    if first:
        acc, outs, sums = refs[0], refs[1 : 1 + n], refs[1 + n :]
        acc[...] = jnp.zeros(acc.shape, f32)
    else:
        acc, outs, sums = refs[1], refs[2 : 2 + n], refs[2 + n :]
        acc[...] = refs[0][...]
    for i, o in enumerate(offsets):
        term = grads[o % PLANES]
        if i < n_got:
            sums[i][...] = gots[i][:TOKENS].astype(f32)
            outs[i][TOKENS:] = (gots[i][TOKENS:].astype(f32) + term.astype(f32)).astype(bf16)
        else:
            sums[i][...] = jnp.zeros((TOKENS, 128), f32)
            outs[i][TOKENS:] = term
        bwd_block(info, o, q, d_out, rows, kvs[i], start, acc, sums[i])
        outs[i][:TOKENS] = sums[i][...].astype(bf16)


def last_kernel(
    info, q, d_out, rows, start, wo_grads, kv, got_a, got_b, acc_in, cos_t, sin_t, normed,
    grads, wo_sum, acc, out, d_t,
):
    acc[...] = acc_in[...]
    out[...] = got_a[:TOKENS].astype(f32) + got_b[:TOKENS].astype(f32)
    wo_sum[...] = (
        got_a[TOKENS:].astype(f32) + got_b[TOKENS:].astype(f32) + wo_grads[0].astype(f32)
    )
    bwd_block(info, 0, q, d_out, rows, kv, start, acc, out)
    c, s = cos_t[...], sin_t[...]
    kv_t = out[...].T

    def back(u, at, scale):
        one, two = u[:32], u[32:]
        d_t[at : at + 32] = ((one * c + two * s) * scale).astype(bf16)
        d_t[at + 32 : at + 64] = ((two * c - one * s) * scale).astype(bf16)

    for h in range(REPEAT):
        back(acc[64 * h : 64 * h + 64], 64 * h, 1.0 / math.sqrt(HEAD_SIZE))
    back(kv_t[:64], 256, 1.0)
    d_t[320:384] = kv_t[64:].astype(bf16)
    for o in range(PLANES):
        at = pl.multiple_of(plane_at(info, o) * ROWS, ROWS)
        grads[o] = dot(d_t[...], normed[:, pl.ds(at, ROWS)]).astype(bf16)


def shape(*dims, dtype=bf16):
    return jax.ShapeDtypeStruct(dims, dtype)


def to_side(blocks, own):
    pick = lambda arr, i: lax.dynamic_index_in_dim(arr, i, 0, keepdims=False)
    got = jnp.stack(
        [pick(blocks, own)] + [beside(pick(blocks, own ^ k), k) for k in range(1, SIDE)]
    )
    return [pick(got, own ^ i) for i in range(SIDE)]


def from_side(x, own):
    across = beside(x, 2)
    parts = [x, beside(x, 1), across, beside(across, 1)]
    full = jnp.zeros((SIDE,) + x.shape, x.dtype)
    for k, part in enumerate(parts):
        full = lax.dynamic_update_index_in_dim(full, part, own ^ k, 0)
    return full.reshape((SIDE * x.shape[0],) + x.shape[1:])


def on_device(hidden, gain, weights, momentum, cotangent, segment, distance):
    rank = lax.axis_index("fsdp")
    plane, own = rank // SIDE, rank % SIDE
    old_w, old_m = weights[0], momentum[0]

    wb = old_w.astype(bf16)
    cuts = [wb[:, :1024], wb[:, 1024:1280], wb[:, 1280:1536], wb[:, 1536:]]
    by_head = jnp.concatenate([c.reshape(c.shape[0], SIDE, -1) for c in cuts], axis=2)
    by_head = by_head.transpose(1, 0, 2)
    seg = segment[0]
    lane = lax.broadcasted_iota(jnp.int32, (SIDE, 16, QKV + WO), 2)
    counts = jnp.where(lane == 0, jnp.sum(seg == 0), jnp.where(lane == 1, jnp.sum(seg == 1), 0))
    sent = jnp.concatenate([by_head, counts.astype(bf16)], axis=1)
    got = to_side(sent, own)
    wo_rows = jnp.concatenate([b[:64, QKV:] for b in got], axis=0)
    tail = jnp.concatenate([b[64:65, :QKV] for b in got] + [got[0][68:80, :QKV]], axis=0)
    w_qkv = ring_gather(jnp.concatenate([b[:64, :QKV] for b in got] + [tail], axis=0))

    local = hidden[0].astype(f32)
    normed = (
        local * lax.rsqrt(jnp.mean(local * local, axis=1, keepdims=True) + EPS) * gain[0][None, :]
    ).astype(bf16)
    normed, _ = lax.optimization_barrier((normed, wo_rows))
    normed = from_side(normed, own)
    cot, _ = lax.optimization_barrier((cotangent[0], normed))
    cot = from_side(cot, own)

    groups = lax.axis_size("group")
    bits = groups.bit_length() - 1
    bit = jnp.remainder(distance[0], bits)

    def swap(b, x):
        return lax.ppermute(x, "group", [(i, i ^ 1 << b) for i in range(groups)])

    both, _ = lax.optimization_barrier((jnp.stack([old_w, old_m]).astype(bf16), cot))
    others = [swap(b, both) for b in range(bits)]
    other = others[0]
    for b in range(1, bits):
        other = jnp.where(bit == b, others[b], other)
    other = other.astype(f32)

    tokens = plane * TOKENS + jnp.arange(TOKENS, dtype=jnp.int32)
    counts = jnp.concatenate([b[ROWS : ROWS + SIDE, :2] for b in w_qkv], axis=0).astype(f32)
    counts = jnp.sum(counts, axis=0).astype(jnp.int32)
    second, third = counts[0], counts[0] + counts[1]
    start = jnp.where(tokens >= third, third, jnp.where(tokens >= second, second, 0))
    info = jnp.stack([plane.astype(jnp.int32), start[0], start[-1]])
    start = start[None, :]

    half = HEAD_SIZE // 2
    freq = jnp.power(THETA, -jnp.arange(half, dtype=f32) * 2.0 / HEAD_SIZE)
    angle = tokens.astype(f32)[:, None] * freq[None, :]
    cosine, sine = jnp.cos(angle), jnp.sin(angle)
    cos_rows = jnp.concatenate([cosine] * 4, axis=1)
    sin_rows = jnp.concatenate([-sine, sine] * 2, axis=1)
    cos_t, sin_t = cosine.T, sine.T

    q, kv = call(
        proj_kernel,
        (shape(REPEAT, TOKENS, 128), shape(2 * TOKENS, 128)),
        1,
        4 + PLANES,
        (2 * TOKENS * 2048 * QKV, 5 << 20, 0),
    )(plane.astype(jnp.int32)[None], normed, cos_rows, sin_rows, wo_rows, *w_qkv)

    kvs = ring_gather(kv)

    score = 2 * REPEAT * TOKENS * TOKENS * 128
    state_shape = (shape(8, TOKENS, dtype=f32), shape(256, TOKENS, dtype=f32))
    state = call(
        functools.partial(fwd_kernel, (0,)),
        state_shape,
        1,
        3,
        (2 * score, 2 << 20, 1 << 20),
    )(info, q, start, kvs[0])
    for offsets in ((-1, 1), (-2, 2), (-3, 3), (-4,)):
        n = len(offsets)
        state = call(
            functools.partial(fwd_kernel, offsets),
            state_shape,
            1,
            4 + n,
            (2 * n * score, 2 << 20, n << 20),
            {3 + n: 0, 4 + n: 1},
        )(info, q, start, *[kvs[o % PLANES] for o in offsets], *state)

    mixed_t, d_out, back_rows, attn_part, wo_grads = call(
        mid_kernel,
        (
            shape(256, TOKENS),
            shape(REPEAT, TOKENS, 128),
            shape(8, TOKENS, dtype=f32),
            shape(TOKENS, 2048),
            shape(PLANES, TOKENS, 128),
        ),
        1,
        3 + PLANES,
        (6 * TOKENS * 2048 * WO, 8 << 20, 0),
    )(info, *state, cot, *kvs)

    parts = attn_part.reshape(SIDE, TOKENS // SIDE, 2048)
    pick = lambda i: lax.dynamic_index_in_dim(parts, i, 0, keepdims=False)
    attn = pick(own).astype(f32)
    for k in range(1, SIDE):
        attn = attn + beside(pick(own ^ k), k).astype(f32)
    attn = attn.astype(bf16)

    acc_shape = shape(256, TOKENS, dtype=f32)
    common = (info, q, d_out, back_rows, start, wo_grads)
    acc, gots = None, ()
    for offsets in ((-4, 3), (-3, 2), (-2, 1), (-1,)):
        n, n_got = len(offsets), min(len(gots), len(offsets))
        gots_in = gots[:n_got]
        outs = pl.pallas_call(
            functools.partial(bwd_kernel, offsets, n_got),
            out_shape=(acc_shape,) + (shape(2 * TOKENS, 128),) * n,
            in_specs=[pl.BlockSpec(memory_space=pltpu.SMEM)]
            + [pl.BlockSpec(memory_space=pltpu.VMEM)] * (5 + n + n_got + (acc is not None)),
            out_specs=(pl.BlockSpec(memory_space=pltpu.VMEM),) * (1 + n),
            scratch_shapes=[pltpu.VMEM((TOKENS, 128), f32)] * n,
            input_output_aliases={} if acc is None else {6 + n + n_got: 0},
            compiler_params=VMEM,
            cost_estimate=pl.CostEstimate(
                flops=5 * n * score, bytes_accessed=4 << 20, transcendentals=n << 20
            ),
        )(*common, *[kvs[o % PLANES] for o in offsets], *gots_in, *([] if acc is None else [acc]))
        acc = outs[0]
        if n == 2:
            gots = (along(outs[1], -1), along(outs[2], 1))
        else:
            gots = (along(outs[1], -1), gots[1])

    grads, wo_sum = pl.pallas_call(
        last_kernel,
        out_shape=(shape(PLANES, QKV, ROWS), shape(TOKENS, 128, dtype=f32)),
        in_specs=[pl.BlockSpec(memory_space=pltpu.SMEM)]
        + [pl.BlockSpec(memory_space=pltpu.VMEM)] * 12,
        out_specs=(pl.BlockSpec(memory_space=pltpu.VMEM),) * 2,
        scratch_shapes=[
            pltpu.VMEM((256, TOKENS), f32),
            pltpu.VMEM((TOKENS, 128), f32),
            pltpu.VMEM((QKV, TOKENS), bf16),
        ],
        compiler_params=VMEM,
        cost_estimate=pl.CostEstimate(
            flops=5 * score, bytes_accessed=8 << 20, transcendentals=1 << 20
        ),
    )(*common, kvs[0], *gots, acc, cos_t, sin_t, normed)
    qkv_sum = ring_scatter([grads[o] for o in range(PLANES)])

    wo_sum = jnp.concatenate([wo_sum[:ROWS], wo_sum[ROWS:]], axis=1)
    sums = jnp.concatenate([qkv_sum, wo_sum], axis=0).T.astype(bf16)
    by_head = to_side(sums.reshape(SIDE, ROWS // SIDE, QKV + WO), own)
    grad = jnp.concatenate(
        [b[:, lo:hi] for lo, hi in ((0, 256), (256, 320), (320, 384), (384, 640)) for b in by_head],
        axis=1,
    )
    grad_pair = grad.astype(f32) + lax.switch(
        bit, [functools.partial(swap, b) for b in range(bits)], grad
    ).astype(f32)
    out_m = 0.5 * (BETA * (old_m + other[1]) + grad_pair)
    out_w = 0.5 * (old_w + other[0]) - RATE * out_m
    return (attn[None], out_w[None], out_m[None])


def solution(mesh):
    return jax.shard_map(
        on_device,
        mesh=mesh,
        in_specs=(
            P("group", "fsdp", None),
            P("group", None),
            P("group", "fsdp", None),
            P("group", "fsdp", None),
            P("group", "fsdp", None),
            P("group", "fsdp"),
            P(),
        ),
        out_specs=(P("group", "fsdp", None), P("group", "fsdp", None), P("group", "fsdp", None)),
        check_vma=False,
    )
```

```python
import functools
import math

import jax
import jax.numpy as jnp
from jax import lax
from jax.experimental import pallas as pl
from jax.experimental.pallas import tpu as pltpu
from jax.sharding import PartitionSpec as P

QUERY_HEADS = 16
KEY_VALUE_HEADS = 4
HEAD_SIZE = 64
REPEAT = QUERY_HEADS // KEY_VALUE_HEADS

EPS = 1e-05
BETA = 0.9
RATE = 0.01
THETA = 500000.0
MASK_FILL = -1e30
TOP_START = -1e20

PLANES = 8
SIDE = 4
TOKENS = 512
ROWS = 256
QKV = 384
WO = 256
PLANE_GROUPS = [[SIDE * p + i for i in range(SIDE)] for p in range(PLANES)]
RING_GROUPS = [[SIDE * p + i for p in range(PLANES)] for i in range(SIDE)]
NT = (((1,), (1,)), ((), ()))
NN = (((1,), (0,)), ((), ()))

f32 = jnp.float32
bf16 = jnp.bfloat16


def dot(a, b, dims=NN):
    return lax.dot_general(a, b, dims, preferred_element_type=f32)


def along(x, step):
    n = PLANES * SIDE
    return lax.ppermute(x, "fsdp", [(i, (i + SIDE * step) % n) for i in range(n)])


def beside(x, mask):
    return lax.ppermute(x, "fsdp", [(i, i ^ mask) for i in range(PLANES * SIDE)])


def ring_gather(x):
    got = [None] * PLANES
    got[0] = x
    down = up = x
    for s in range(1, PLANES // 2 + 1):
        down = along(down, 1)
        got[-s % PLANES] = down
        if s < PLANES // 2:
            up = along(up, -1)
            got[s] = up
    return got


def ring_scatter(terms):
    add = lambda a, b: a.astype(f32) + b.astype(f32)
    up = down = None
    for s in range(PLANES // 2, 0, -1):
        t = terms[-s % PLANES]
        down = along(t if down is None else add(down, t).astype(bf16), -1)
        if s < PLANES // 2:
            t = terms[s]
            up = along(t if up is None else add(up, t).astype(bf16), 1)
    return down, up


def call(kernel, outs, args, cost, scalars=1, scratch=(), alias=None, mib=24):
    flops, bytes_, exps = cost
    vmem, smem = (pl.BlockSpec(memory_space=m) for m in (pltpu.VMEM, pltpu.SMEM))
    out_specs = tuple(smem if o.shape == INFO.shape else vmem for o in outs)
    return pl.pallas_call(
        kernel,
        out_shape=tuple(outs),
        in_specs=[smem] * scalars + [vmem] * (len(args) - scalars),
        out_specs=out_specs,
        scratch_shapes=scratch,
        input_output_aliases=alias or {},
        compiler_params=pltpu.CompilerParams(vmem_limit_bytes=mib * 1024 * 1024),
        cost_estimate=pl.CostEstimate(flops=flops, bytes_accessed=bytes_, transcendentals=exps),
    )(*args)


def shape(*dims, dtype=bf16):
    return jax.ShapeDtypeStruct(dims, dtype)


INFO = shape(3, dtype=jnp.int32)


def plane_at(info, offset):
    return lax.rem(info[0] + (offset % PLANES), PLANES)


def lanes(shape):
    return lax.broadcasted_iota(jnp.int32, shape, len(shape) - 1)


def proj_kernel(place, cos, sin, *refs):
    parts, blocks = refs[:SIDE], refs[SIDE : SIDE + PLANES]
    normed, q_out, kv_out, start, info = refs[SIDE + PLANES :]
    for k in range(SIDE):
        at = pl.multiple_of((place[1] ^ k) * 128, 128)
        normed[pl.ds(at, 128)] = parts[k][...]
    total = jnp.zeros((TOKENS, QKV), f32)
    for o in range(PLANES):
        at = pl.multiple_of(plane_at(place, o) * ROWS, ROWS)
        total = total + dot(normed[:, pl.ds(at, ROWS)], blocks[o][:ROWS])

    tails = sum(b[ROWS : ROWS + 16].astype(f32)[:SIDE, :128] for b in blocks)
    lane = lanes(tails.shape)
    second = jnp.sum(jnp.where(lane == 0, tails, 0.0)).astype(jnp.int32)
    third = second + jnp.sum(jnp.where(lane == 1, tails, 0.0)).astype(jnp.int32)

    def start_of(t):
        return jnp.where(t >= third, third, jnp.where(t >= second, second, 0))

    start[...] = start_of(positions(place))
    info[0] = place[0]
    info[1] = start_of(place[0] * TOKENS)
    info[2] = start_of(place[0] * TOKENS + TOKENS - 1)

    lane = lanes((TOKENS, 128))
    first = lax.rem(lane, HEAD_SIZE) < HEAD_SIZE // 2
    low = lane < HEAD_SIZE
    c, s = cos[...], sin[...]

    def turned(u):
        return jnp.where(first, pltpu.roll(u, 96, 1), pltpu.roll(u, 32, 1))

    for pair in range(2):
        u = total[:, 128 * pair : 128 * pair + 128]
        u = (u * c + turned(u) * s) * (1.0 / math.sqrt(HEAD_SIZE))
        q_out[2 * pair] = jnp.where(low, u, 0.0).astype(bf16)
        q_out[2 * pair + 1] = jnp.where(low, pltpu.roll(u, 64, 1), 0.0).astype(bf16)
    u = total[:, 256:]
    kv_out[...] = jnp.where(low, u * c + turned(u) * s, u).astype(bf16)


def masked(s, src, qpos, start):
    kpos = src * TOKENS + lax.broadcasted_iota(jnp.int32, (TOKENS, TOKENS), 0)
    return jnp.where((kpos <= qpos) & (kpos >= start), s, MASK_FILL)


def on_block(info, src, body):
    base = src * TOKENS
    seen = (src <= info[0]) & (base + TOKENS > info[1])
    edge = (src == info[0]) | (base < info[2])

    @pl.when(seen & edge)
    def _():
        body(True)

    @pl.when(seen & jnp.logical_not(edge))
    def _():
        body(False)


def positions(info):
    return info[0] * TOKENS + lax.broadcasted_iota(jnp.int32, (1, TOKENS), 1)


def fwd_block(info, offset, q, kv, start, rows, acc):
    src = plane_at(info, offset)

    def body(mask):
        block = kv[...]
        value_t = block.T[HEAD_SIZE:]
        for h in range(REPEAT):
            s = dot(block, q[h], NT)
            if mask:
                s = masked(s, src, positions(info), start[...])
            old = rows[h : h + 1]
            top = jnp.maximum(old, jnp.max(s, axis=0, keepdims=True))
            p = jnp.exp(s - top)
            fade = jnp.exp(old - top)
            rows[h : h + 1] = top
            rows[4 + h : 5 + h] = rows[4 + h : 5 + h] * fade + jnp.sum(p, axis=0, keepdims=True)
            at = slice(64 * h, 64 * h + 64)
            acc[at] = acc[at] * fade + dot(value_t, p.astype(bf16))

    on_block(info, src, body)


def fwd_kernel(offsets, info, q, start, *refs):
    n = len(offsets)
    kvs, refs = refs[:n], refs[n:]
    if offsets[0] == 0:
        rows, acc = refs
        rows[0:4] = jnp.full((4, TOKENS), TOP_START, f32)
        rows[4:8] = jnp.zeros((4, TOKENS), f32)
        acc[...] = jnp.zeros(acc.shape, f32)
    else:
        rows_in, acc_in, rows, acc = refs
        rows[...] = rows_in[...]
        acc[...] = acc_in[...]
    for o, kv in zip(offsets, kvs):
        fwd_block(info, o, q, kv, start, rows, acc)


def mid_kernel(
    info, q, start, kv, rows_in, acc_in, cot, w_out,
    mixed_t, d_out, back_rows, grads, rows, acc,
):
    rows[...] = rows_in[...]
    acc[...] = acc_in[...]
    fwd_block(info, -4, q, kv, start, rows, acc)
    d_mixed = dot(cot[...], w_out[...]).astype(bf16).astype(f32)
    inverse = 1.0 / rows[4:8]
    back_rows[0:4] = rows[0:4]
    for h in range(REPEAT):
        at = slice(64 * h, 64 * h + 64)
        mixed_t[at] = (acc[at] * inverse[h : h + 1]).astype(bf16)
    mt = mixed_t[...]
    prod = d_mixed.T * mt.astype(f32)
    for h in range(REPEAT):
        back_rows[4 + h : 5 + h] = inverse[h : h + 1] * jnp.sum(
            prod[64 * h : 64 * h + 64], axis=0, keepdims=True
        )
    by_row = jnp.concatenate([inverse, inverse], axis=0).T
    high = lanes((TOKENS, 128)) >= HEAD_SIZE
    for pair in range(2):
        u = d_mixed[:, 128 * pair : 128 * pair + 128]
        scale = [by_row[:, 2 * pair + i : 2 * pair + i + 1] for i in range(2)]
        u = u * jnp.where(high, scale[1], scale[0])
        d_out[2 * pair] = jnp.where(high, pltpu.roll(u, 64, 1), 0.0).astype(bf16)
        d_out[2 * pair + 1] = jnp.where(high, u, 0.0).astype(bf16)
    for p in range(PLANES):
        grads[p] = dot(mt, cot[:, ROWS * p : ROWS * p + ROWS]).astype(bf16)


def attn_kernel(mixed_t, w_out, attn):
    mixed = mixed_t[...].astype(f32).T.astype(bf16)
    attn[...] = dot(mixed, w_out[...], NT).astype(bf16)


def bwd_block(info, offset, q, d_out, rows, kv, start, acc, out):
    src = plane_at(info, offset)

    def body(mask):
        block = kv[...]
        key_t = block.T[:HEAD_SIZE]
        total = out[...]
        for h in range(REPEAT):
            s = dot(block, q[h], NT)
            if mask:
                s = masked(s, src, positions(info), start[...])
            p = jnp.exp(s - rows[h : h + 1])
            dp = dot(block, d_out[h], NT)
            ds = (p * (dp - rows[4 + h : 5 + h])).astype(bf16)
            total = total + dot(p.astype(bf16), d_out[h]) + dot(ds, q[h])
            at = slice(64 * h, 64 * h + 64)
            acc[at] = acc[at] + dot(key_t, ds)
        out[...] = total

    on_block(info, src, body)


def bwd_kernel(offsets, info, q, d_out, rows, start, *refs):
    n = len(offsets)
    kvs, refs = refs[:n], refs[n:]
    acc, outs, sums = refs[-2 * n - 1], refs[-2 * n : -n], refs[-n:]
    acc[...] = refs[0][...] if len(refs) > 2 * n + 1 else jnp.zeros(acc.shape, f32)
    for i, o in enumerate(offsets):
        sums[i][...] = jnp.zeros((TOKENS, 128), f32)
        bwd_block(info, o, q, d_out, rows, kvs[i], start, acc, sums[i])
        outs[i][...] = sums[i][...].astype(bf16)


def turn_back(u, c, s, out, at, scale):
    one, two = u[:32], u[32:]
    out[at : at + 32] = ((one * c + two * s) * scale).astype(bf16)
    out[at + 32 : at + 64] = ((two * c - one * s) * scale).astype(bf16)


def own_kernel(
    info, q, d_out, rows, start, kv, acc_in, cos_t, sin_t, normed,
    out, grads, acc, d_t,
):
    acc[...] = acc_in[...]
    out[...] = jnp.zeros((TOKENS, 128), f32)
    bwd_block(info, 0, q, d_out, rows, kv, start, acc, out)
    c, s = cos_t[...], sin_t[...]
    for h in range(REPEAT):
        turn_back(acc[64 * h : 64 * h + 64], c, s, d_t, 64 * h, 1.0 / math.sqrt(HEAD_SIZE))
    for o in range(PLANES):
        at = pl.multiple_of(plane_at(info, o) * ROWS, ROWS)
        grads[o] = dot(d_t[...], normed[:, pl.ds(at, ROWS)]).astype(bf16)


def last_kernel(info, own, got_a, got_b, cos_t, sin_t, normed, q_grads, *refs):
    grads, d_t = refs[:PLANES], refs[PLANES]
    kv_t = (got_a[...].astype(f32) + got_b[...].astype(f32) + own[...]).T
    turn_back(kv_t[:64], cos_t[...], sin_t[...], d_t, 0, 1.0)
    d_t[64:128] = kv_t[64:].astype(bf16)
    for o in range(PLANES):
        at = pl.multiple_of(plane_at(info, o) * ROWS, ROWS)
        grads[o][:WO] = q_grads[o]
        grads[o][WO:] = dot(d_t[...], normed[:, pl.ds(at, ROWS)]).astype(bf16)


def to_side(blocks, own):
    pick = lambda arr, i: lax.dynamic_index_in_dim(arr, i, 0, keepdims=False)
    got = jnp.stack(
        [pick(blocks, own)] + [beside(pick(blocks, own ^ k), k) for k in range(1, SIDE)]
    )
    return [pick(got, own ^ i) for i in range(SIDE)]


def on_device(hidden, gain, weights, momentum, cotangent, segment, distance):
    rank = lax.axis_index("fsdp")
    plane, own = rank // SIDE, rank % SIDE
    old_w, old_m = weights[0], momentum[0]
    place = jnp.stack([plane, own]).astype(jnp.int32)

    wb = old_w.astype(bf16)
    cuts = [wb[:, :1024], wb[:, 1024:1280], wb[:, 1280:1536], wb[:, 1536:]]
    by_head = jnp.concatenate([c.reshape(c.shape[0], SIDE, -1) for c in cuts], axis=2)
    by_head = by_head.transpose(1, 0, 2)
    seg = segment[0]
    lane = lax.broadcasted_iota(jnp.int32, (SIDE, 16, QKV + WO), 2)
    counts = jnp.where(lane == 0, jnp.sum(seg == 0), jnp.where(lane == 1, jnp.sum(seg == 1), 0))
    sent = jnp.concatenate([by_head, counts.astype(bf16)], axis=1)
    got = to_side(sent, own)
    wo_rows = jnp.concatenate([b[:64, QKV:] for b in got], axis=0)
    tail = jnp.concatenate([b[64:65, :QKV] for b in got] + [got[0][68:80, :QKV]], axis=0)
    w_qkv = ring_gather(jnp.concatenate([b[:64, :QKV] for b in got] + [tail], axis=0))
    w_out = lax.all_gather(wo_rows, "fsdp", axis_index_groups=RING_GROUPS, axis=0, tiled=True)
    cot = lax.all_gather(
        cotangent[0], "fsdp", axis_index_groups=PLANE_GROUPS, axis=0, tiled=True
    )

    local = hidden[0].astype(f32)
    normed = (
        local * lax.rsqrt(jnp.mean(local * local, axis=1, keepdims=True) + EPS) * gain[0][None, :]
    ).astype(bf16)
    normed, _ = lax.optimization_barrier((normed, wo_rows))
    across = beside(normed, 2)
    parts = [normed, beside(normed, 1), across, beside(across, 1)]

    half = HEAD_SIZE // 2
    tokens = plane * TOKENS + jnp.arange(TOKENS, dtype=jnp.int32)
    freq = jnp.power(THETA, -jnp.arange(half, dtype=f32) * 2.0 / HEAD_SIZE)
    angle = tokens.astype(f32)[:, None] * freq[None, :]
    cosine, sine = jnp.cos(angle), jnp.sin(angle)
    cos_rows = jnp.concatenate([cosine] * 4, axis=1)
    sin_rows = jnp.concatenate([-sine, sine] * 2, axis=1)
    cos_t, sin_t = cosine.T, sine.T

    state_shape = (shape(8, TOKENS, dtype=f32), shape(256, TOKENS, dtype=f32))
    head_shape = shape(REPEAT, TOKENS, 128)
    kv_shape = shape(TOKENS, 128)
    score = 2 * REPEAT * TOKENS * TOKENS * 128

    normed, q, kv, start, info = call(
        proj_kernel,
        (shape(TOKENS, 2048), head_shape, kv_shape, shape(1, TOKENS, dtype=jnp.int32), INFO),
        (place, cos_rows, sin_rows, *parts, *w_qkv),
        (2 * TOKENS * 2048 * QKV, 8 << 20, 0),
    )

    kvs = ring_gather(kv)
    state = call(
        functools.partial(fwd_kernel, (0,)),
        state_shape,
        (info, q, start, kvs[0]),
        (2 * score, 2 << 20, 1 << 20),
    )
    for offsets in ((-1, 1), (-2, 2), (-3, 3)):
        state = call(
            functools.partial(fwd_kernel, offsets),
            state_shape,
            (info, q, start, *[kvs[o % PLANES] for o in offsets], *state),
            (4 * score, 2 << 20, 2 << 20),
            alias={5: 0, 6: 1},
        )

    mixed_t, d_out, back_rows, wo_grads = call(
        mid_kernel,
        (shape(256, TOKENS), head_shape, state_shape[0], shape(PLANES, WO, ROWS)),
        (info, q, start, kvs[4], *state, cot, w_out),
        (2 * score + 4 * TOKENS * 2048 * WO, 8 << 20, 1 << 20),
        scratch=[pltpu.VMEM((8, TOKENS), f32), pltpu.VMEM((256, TOKENS), f32)],
    )
    wo_sum = lax.psum_scatter(
        wo_grads, "fsdp", axis_index_groups=RING_GROUPS, scatter_dimension=0, tiled=True
    )[0]

    common = (info, q, d_out, back_rows, start)
    acc, terms = None, {}
    scratch = [pltpu.VMEM((TOKENS, 128), f32)]
    for offsets in ((-4, 3), (-3, 2), (-2, 1), (-1,)):
        n = len(offsets)
        args = common + tuple(kvs[o % PLANES] for o in offsets)
        acc, *outs = call(
            functools.partial(bwd_kernel, offsets),
            (state_shape[1],) + (kv_shape,) * n,
            args if acc is None else args + (acc,),
            (5 * n * score, 3 << 20, n << 20),
            scratch=scratch * n,
            alias=None if acc is None else {len(args): 0},
        )
        terms.update({o % PLANES: t for o, t in zip(offsets, outs)})
        if len(terms) == 2:
            (attn,) = call(
                attn_kernel,
                (shape(TOKENS, 2048),),
                (mixed_t, w_out),
                (2 * TOKENS * 2048 * WO, 4 << 20, 0),
                scalars=0,
            )
            attn = lax.psum_scatter(
                attn, "fsdp", axis_index_groups=PLANE_GROUPS, scatter_dimension=0, tiled=True
            )
    own_kv, q_grads = call(
        own_kernel,
        (shape(TOKENS, 128, dtype=f32), shape(PLANES, WO, ROWS)),
        (*common, kvs[0], acc, cos_t, sin_t, normed),
        (5 * score + 2 * TOKENS * 2048 * WO, 5 << 20, 1 << 20),
        scratch=[pltpu.VMEM((256, TOKENS), f32), pltpu.VMEM((WO, TOKENS), bf16)],
    )
    grads = call(
        last_kernel,
        (shape(QKV, ROWS),) * PLANES,
        (info, own_kv, *ring_scatter(terms), cos_t, sin_t, normed, q_grads),
        (2 * TOKENS * 2048 * 128, 6 << 20, 0),
        scratch=[pltpu.VMEM((128, TOKENS), bf16)],
    )
    qkv_sum = sum(x.astype(f32) for x in (*ring_scatter(grads), grads[0]))

    sums = jnp.concatenate([qkv_sum, wo_sum.astype(f32)], axis=0).T.astype(bf16)
    by_head = to_side(sums.reshape(SIDE, ROWS // SIDE, QKV + WO), own)
    grad = jnp.concatenate(
        [b[:, lo:hi] for lo, hi in ((0, 256), (256, 320), (320, 384), (384, 640)) for b in by_head],
        axis=1,
    ).astype(f32)

    new_m = BETA * old_m + grad
    new_w = old_w - RATE * new_m
    groups = lax.axis_size("group")
    bits = groups.bit_length() - 1

    def swap(b, x):
        return lax.ppermute(x, "group", [(i, i ^ 1 << b) for i in range(groups)])

    other = lax.switch(
        jnp.remainder(distance[0], bits),
        [functools.partial(swap, b) for b in range(bits)],
        jnp.stack([new_w, new_m]).astype(bf16),
    ).astype(f32)
    out_w = 0.5 * (new_w + other[0])
    out_m = 0.5 * (new_m + other[1])
    return (attn[None], out_w[None], out_m[None])


def solution(mesh):
    return jax.shard_map(
        on_device,
        mesh=mesh,
        in_specs=(
            P("group", "fsdp", None),
            P("group", None),
            P("group", "fsdp", None),
            P("group", "fsdp", None),
            P("group", "fsdp", None),
            P("group", "fsdp"),
            P(),
        ),
        out_specs=(P("group", "fsdp", None), P("group", "fsdp", None), P("group", "fsdp", None)),
        check_vma=False,
    )
```

```python
import functools
import math

import jax
import jax.numpy as jnp
from jax import lax
from jax.experimental import pallas as pl
from jax.experimental.pallas import tpu as pltpu
from jax.sharding import PartitionSpec as P

QUERY_HEADS = 16
KEY_VALUE_HEADS = 4
HEAD_SIZE = 64
REPEAT = QUERY_HEADS // KEY_VALUE_HEADS

EPS = 1e-05
BETA = 0.9
RATE = 0.01
THETA = 500000.0
MASK_FILL = -1e30
TOP_START = -1e20

PLANES = 8
SIDE = 4
TOKENS = 512
ROWS = 256
QKV = 384
WO = 256
PLANE_GROUPS = [[SIDE * p + i for i in range(SIDE)] for p in range(PLANES)]
RING_GROUPS = [[SIDE * p + i for p in range(PLANES)] for i in range(SIDE)]
NT = (((1,), (1,)), ((), ()))
NN = (((1,), (0,)), ((), ()))

f32 = jnp.float32
bf16 = jnp.bfloat16


def dot(a, b, dims=NN):
    return lax.dot_general(a, b, dims, preferred_element_type=f32)


def along(x, step):
    n = PLANES * SIDE
    return lax.ppermute(x, "fsdp", [(i, (i + SIDE * step) % n) for i in range(n)])


def beside(x, mask):
    return lax.ppermute(x, "fsdp", [(i, i ^ mask) for i in range(PLANES * SIDE)])


def ring_gather(x, beside_it=None):
    got = [None] * PLANES
    got[0] = x
    down = up = x
    for s in range(1, PLANES // 2 + 1):
        down = along(down, 1)
        if s < PLANES // 2:
            up = along(up, -1)
            if beside_it is not None:
                down, up = lax.optimization_barrier((down, up))
            if s == 2 and beside_it is not None:
                down, up, beside_it = lax.optimization_barrier((down, up, beside_it))
            got[s] = up
        got[-s % PLANES] = down
    return got, beside_it


def ring_scatter(terms):
    add = lambda a, b: a.astype(f32) + b.astype(f32)
    up = down = None
    for s in range(PLANES // 2, 0, -1):
        t = terms[-s % PLANES]
        down = along(t if down is None else add(down, t).astype(bf16), -1)
        if s < PLANES // 2:
            t = terms[s]
            up = along(t if up is None else add(up, t).astype(bf16), 1)
    return down, up


def call(kernel, outs, args, cost, scalars=1, scratch=(), alias=None, mib=12):
    flops, bytes_, exps = cost
    vmem, smem = (pl.BlockSpec(memory_space=m) for m in (pltpu.VMEM, pltpu.SMEM))
    out_specs = tuple(smem if o.shape == INFO.shape else vmem for o in outs)
    return pl.pallas_call(
        kernel,
        out_shape=tuple(outs),
        in_specs=[smem] * scalars + [vmem] * (len(args) - scalars),
        out_specs=out_specs,
        scratch_shapes=scratch,
        input_output_aliases=alias or {},
        compiler_params=pltpu.CompilerParams(vmem_limit_bytes=mib * 1024 * 1024),
        cost_estimate=pl.CostEstimate(flops=flops, bytes_accessed=bytes_, transcendentals=exps),
    )(*args)


def shape(*dims, dtype=bf16):
    return jax.ShapeDtypeStruct(dims, dtype)


INFO = shape(3, dtype=jnp.int32)


def plane_at(info, offset):
    return lax.rem(info[0] + (offset % PLANES), PLANES)


def lanes(shape):
    return lax.broadcasted_iota(jnp.int32, shape, len(shape) - 1)


def proj_kernel(place, cos, sin, *refs):
    parts, blocks = refs[:SIDE], refs[SIDE : SIDE + PLANES]
    normed, q_out, kv_out, start, info = refs[SIDE + PLANES :]
    for k in range(SIDE):
        at = pl.multiple_of((place[1] ^ k) * 128, 128)
        normed[pl.ds(at, 128)] = parts[k][...]
    total = jnp.zeros((TOKENS, QKV), f32)
    for o in range(PLANES):
        at = pl.multiple_of(plane_at(place, o) * ROWS, ROWS)
        total = total + dot(normed[:, pl.ds(at, ROWS)], blocks[o][:ROWS])

    tails = sum(b[ROWS : ROWS + 16].astype(f32)[:SIDE, :128] for b in blocks)
    lane = lanes(tails.shape)
    second = jnp.sum(jnp.where(lane == 0, tails, 0.0)).astype(jnp.int32)
    third = second + jnp.sum(jnp.where(lane == 1, tails, 0.0)).astype(jnp.int32)

    def start_of(t):
        return jnp.where(t >= third, third, jnp.where(t >= second, second, 0))

    start[...] = start_of(positions(place))
    info[0] = place[0]
    info[1] = start_of(place[0] * TOKENS)
    info[2] = start_of(place[0] * TOKENS + TOKENS - 1)

    lane = lanes((TOKENS, 128))
    first = lax.rem(lane, HEAD_SIZE) < HEAD_SIZE // 2
    low = lane < HEAD_SIZE
    c, s = cos[...], sin[...]

    def turned(u):
        return jnp.where(first, pltpu.roll(u, 96, 1), pltpu.roll(u, 32, 1))

    for pair in range(2):
        u = total[:, 128 * pair : 128 * pair + 128]
        u = (u * c + turned(u) * s) * (1.0 / math.sqrt(HEAD_SIZE))
        q_out[2 * pair] = jnp.where(low, u, 0.0).astype(bf16)
        q_out[2 * pair + 1] = jnp.where(low, pltpu.roll(u, 64, 1), 0.0).astype(bf16)
    u = total[:, 256:]
    kv_out[...] = jnp.where(low, u * c + turned(u) * s, u).astype(bf16)


def masked(s, src, qpos, start):
    kpos = src * TOKENS + lax.broadcasted_iota(jnp.int32, (TOKENS, TOKENS), 0)
    return jnp.where((kpos <= qpos) & (kpos >= start), s, MASK_FILL)


def on_blocks(info, offsets, body):
    def step(i, carry):
        src = plane_at(info, offsets[0])
        for n, o in enumerate(offsets[1:], 1):
            src = jnp.where(i == n, plane_at(info, o), src)
        base = src * TOKENS
        seen = (src <= info[0]) & (base + TOKENS > info[1])
        edge = (src == info[0]) | (base < info[2])

        @pl.when(seen & edge)
        def _():
            body(i, src, True)

        if offsets != (0,):

            @pl.when(seen & jnp.logical_not(edge))
            def _():
                body(i, src, False)

        return carry

    lax.fori_loop(0, len(offsets), step, 0)


def for_heads(body):
    def step(h, carry):
        body(h, pl.ds(pl.multiple_of(h * HEAD_SIZE, HEAD_SIZE), HEAD_SIZE))
        return carry

    lax.fori_loop(0, REPEAT, step, 0)


def positions(info):
    return info[0] * TOKENS + lax.broadcasted_iota(jnp.int32, (1, TOKENS), 1)


def fwd_blocks(info, offsets, q, kvs, start, rows, acc, kv, value_t):
    for i, ref in enumerate(kvs):
        kv[i] = ref[...]

    def block(i, src, mask):
        value_t[...] = kv[i].T[HEAD_SIZE:]

        def head(h, at):
            s = dot(kv[i], q[h], NT)
            if mask:
                s = masked(s, src, positions(info), start[...])
            old = rows[h]
            top = jnp.maximum(old, jnp.max(s, axis=0, keepdims=True))
            p = jnp.exp(s - top)
            fade = jnp.exp(old - top)
            rows[h] = top
            rows[4 + h] = rows[4 + h] * fade + jnp.sum(p, axis=0, keepdims=True)
            acc[at] = acc[at] * fade + dot(value_t[...], p.astype(bf16))

        for_heads(head)

    on_blocks(info, offsets, block)


def fwd_scratch(n):
    return [pltpu.VMEM((n, TOKENS, 128), bf16), pltpu.VMEM((HEAD_SIZE, TOKENS), bf16)]


def fwd_kernel(offsets, info, q, start, *refs):
    n = len(offsets)
    kvs, refs = refs[:n], refs[n:]
    if offsets[0] == 0:
        rows, acc, *scratch = refs
        rows[0:4] = jnp.full((4, 1, TOKENS), TOP_START, f32)
        rows[4:8] = jnp.zeros((4, 1, TOKENS), f32)
        acc[...] = jnp.zeros(acc.shape, f32)
    else:
        rows_in, acc_in, rows, acc, *scratch = refs
        rows[...] = rows_in[...]
        acc[...] = acc_in[...]
    fwd_blocks(info, offsets, q, kvs, start, rows, acc, *scratch)


def mid_kernel(
    info, q, start, kv, rows_in, acc_in, cot, w_out,
    mixed_t, d_out, back_rows, grads, rows, acc, *scratch,
):
    rows[...] = rows_in[...]
    acc[...] = acc_in[...]
    fwd_blocks(info, (-4,), q, (kv,), start, rows, acc, *scratch)
    d_mixed = dot(cot[...], w_out[...]).astype(bf16).astype(f32)
    inverse = jnp.concatenate([1.0 / rows[4 + h] for h in range(REPEAT)], axis=0)
    back_rows[0:4] = rows[0:4]
    for h in range(REPEAT):
        at = slice(64 * h, 64 * h + 64)
        mixed_t[at] = (acc[at] * inverse[h : h + 1]).astype(bf16)
    mt = mixed_t[...]
    prod = d_mixed.T * mt.astype(f32)
    for h in range(REPEAT):
        back_rows[4 + h] = inverse[h : h + 1] * jnp.sum(
            prod[64 * h : 64 * h + 64], axis=0, keepdims=True
        )
    by_row = jnp.concatenate([inverse, inverse], axis=0).T
    high = lanes((TOKENS, 128)) >= HEAD_SIZE
    for pair in range(2):
        u = d_mixed[:, 128 * pair : 128 * pair + 128]
        scale = [by_row[:, 2 * pair + i : 2 * pair + i + 1] for i in range(2)]
        u = u * jnp.where(high, scale[1], scale[0])
        d_out[2 * pair] = jnp.where(high, pltpu.roll(u, 64, 1), 0.0).astype(bf16)
        d_out[2 * pair + 1] = jnp.where(high, u, 0.0).astype(bf16)
    for p in range(PLANES):
        grads[p] = dot(mt, cot[:, ROWS * p : ROWS * p + ROWS]).astype(bf16)


def attn_kernel(mixed_t, w_out, attn):
    mixed = mixed_t[...].astype(f32).T.astype(bf16)
    attn[...] = dot(mixed, w_out[...], NT).astype(bf16)


def bwd_blocks(info, offsets, q, d_out, rows, kvs, start, acc, sums, kv, key_t):
    for i, ref in enumerate(kvs):
        kv[i] = ref[...]
        sums[i] = jnp.zeros((TOKENS, 128), f32)

    def block(i, src, mask):
        key_t[...] = kv[i].T[:HEAD_SIZE]

        def head(h, at):
            s = dot(kv[i], q[h], NT)
            if mask:
                s = masked(s, src, positions(info), start[...])
            p = jnp.exp(s - rows[h])
            dp = dot(kv[i], d_out[h], NT)
            ds = (p * (dp - rows[4 + h])).astype(bf16)
            sums[i] = sums[i] + (dot(p.astype(bf16), d_out[h]) + dot(ds, q[h]))
            acc[at] = acc[at] + dot(key_t[...], ds)

        for_heads(head)

    on_blocks(info, offsets, block)


def bwd_scratch(n):
    return [pltpu.VMEM((n, TOKENS, 128), f32)] + fwd_scratch(n)


def bwd_kernel(offsets, info, q, d_out, rows, start, *refs):
    n = len(offsets)
    kvs, refs, scratch = refs[:n], refs[n:-3], refs[-3:]
    acc, outs = refs[-n - 1], refs[-n:]
    acc[...] = refs[0][...] if len(refs) > n + 1 else jnp.zeros(acc.shape, f32)
    bwd_blocks(info, offsets, q, d_out, rows, kvs, start, acc, *scratch)
    for i in range(n):
        outs[i][...] = scratch[0][i].astype(bf16)


def turn_back(u, c, s, out, at, scale):
    one, two = u[:32], u[32:]
    out[at : at + 32] = ((one * c + two * s) * scale).astype(bf16)
    out[at + 32 : at + 64] = ((two * c - one * s) * scale).astype(bf16)


def own_kernel(
    info, q, d_out, rows, start, kv, acc_in, cos_t, sin_t, normed,
    out, grads, acc, d_t, *scratch,
):
    acc[...] = acc_in[...]
    bwd_blocks(info, (0,), q, d_out, rows, (kv,), start, acc, *scratch)
    out[...] = scratch[0][0]
    c, s = cos_t[...], sin_t[...]
    for h in range(REPEAT):
        turn_back(acc[64 * h : 64 * h + 64], c, s, d_t, 64 * h, 1.0 / math.sqrt(HEAD_SIZE))
    for o in range(PLANES):
        at = pl.multiple_of(plane_at(info, o) * ROWS, ROWS)
        grads[o] = dot(d_t[...], normed[:, pl.ds(at, ROWS)]).astype(bf16)


def last_kernel(info, own, got_a, got_b, cos_t, sin_t, normed, q_grads, *refs):
    grads, d_t = refs[:PLANES], refs[PLANES]
    kv_t = (got_a[...].astype(f32) + got_b[...].astype(f32) + own[...]).T
    turn_back(kv_t[:64], cos_t[...], sin_t[...], d_t, 0, 1.0)
    d_t[64:128] = kv_t[64:].astype(bf16)
    for o in range(PLANES):
        at = pl.multiple_of(plane_at(info, o) * ROWS, ROWS)
        grads[o][:WO] = q_grads[o]
        grads[o][WO:] = dot(d_t[...], normed[:, pl.ds(at, ROWS)]).astype(bf16)


def to_side(blocks, own):
    pick = lambda arr, i: lax.dynamic_index_in_dim(arr, i, 0, keepdims=False)
    got = jnp.stack(
        [pick(blocks, own)] + [beside(pick(blocks, own ^ k), k) for k in range(1, SIDE)]
    )
    return [pick(got, own ^ i) for i in range(SIDE)]


def on_device(hidden, gain, weights, momentum, cotangent, segment, distance):
    rank = lax.axis_index("fsdp")
    plane, own = rank // SIDE, rank % SIDE
    old_w, old_m = weights[0], momentum[0]
    place = jnp.stack([plane, own]).astype(jnp.int32)

    wb = old_w.astype(bf16)
    cuts = [wb[:, :1024], wb[:, 1024:1280], wb[:, 1280:1536], wb[:, 1536:]]
    by_head = jnp.concatenate([c.reshape(c.shape[0], SIDE, -1) for c in cuts], axis=2)
    by_head = by_head.transpose(1, 0, 2)
    seg = segment[0]
    lane = lax.broadcasted_iota(jnp.int32, (SIDE, 16, QKV + WO), 2)
    counts = jnp.where(lane == 0, jnp.sum(seg == 0), jnp.where(lane == 1, jnp.sum(seg == 1), 0))
    sent = jnp.concatenate([by_head, counts.astype(bf16)], axis=1)
    got = to_side(sent, own)
    wo_rows = jnp.concatenate([b[:64, QKV:] for b in got], axis=0)
    tail = jnp.concatenate([b[64:65, :QKV] for b in got] + [got[0][68:80, :QKV]], axis=0)
    w_rows = jnp.concatenate([b[:64, :QKV] for b in got] + [tail], axis=0)
    cot = lax.all_gather(
        cotangent[0], "fsdp", axis_index_groups=PLANE_GROUPS, axis=0, tiled=True
    )

    local = hidden[0].astype(f32)
    normed = (
        local * lax.rsqrt(jnp.mean(local * local, axis=1, keepdims=True) + EPS) * gain[0][None, :]
    ).astype(bf16)
    normed, w_rows = lax.optimization_barrier((normed, w_rows))
    w_qkv, across = ring_gather(w_rows, beside(normed, 2))
    parts = [normed, beside(normed, 1), across, beside(across, 1)]
    parts[0], cot = lax.optimization_barrier((parts[0], cot))
    wo_rows, _ = lax.optimization_barrier((wo_rows, across))
    w_out = lax.all_gather(wo_rows, "fsdp", axis_index_groups=RING_GROUPS, axis=0, tiled=True)

    half = HEAD_SIZE // 2
    tokens = plane * TOKENS + jnp.arange(TOKENS, dtype=jnp.int32)
    freq = jnp.power(THETA, -jnp.arange(half, dtype=f32) * 2.0 / HEAD_SIZE)
    angle = tokens.astype(f32)[:, None] * freq[None, :]
    cosine, sine = jnp.cos(angle), jnp.sin(angle)
    cos_rows = jnp.concatenate([cosine] * 4, axis=1)
    sin_rows = jnp.concatenate([-sine, sine] * 2, axis=1)
    cos_t, sin_t = cosine.T, sine.T

    state_shape = (shape(8, 1, TOKENS, dtype=f32), shape(256, TOKENS, dtype=f32))
    head_shape = shape(REPEAT, TOKENS, 128)
    kv_shape = shape(TOKENS, 128)
    score = 2 * REPEAT * TOKENS * TOKENS * 128

    normed, q, kv, start, info = call(
        proj_kernel,
        (shape(TOKENS, 2048), head_shape, kv_shape, shape(1, TOKENS, dtype=jnp.int32), INFO),
        (place, cos_rows, sin_rows, *parts, *w_qkv),
        (2 * TOKENS * 2048 * QKV, 8 << 20, 0),
    )

    kvs, _ = ring_gather(kv)
    state = call(
        functools.partial(fwd_kernel, (0,)),
        state_shape,
        (info, q, start, kvs[0]),
        (2 * score, 2 << 20, 1 << 20),
        scratch=fwd_scratch(1),
    )
    for offsets in ((-1, 1), (-2, 2), (-3, 3)):
        state = call(
            functools.partial(fwd_kernel, offsets),
            state_shape,
            (info, q, start, *[kvs[o % PLANES] for o in offsets], *state),
            (4 * score, 2 << 20, 2 << 20),
            scratch=fwd_scratch(2),
            alias={5: 0, 6: 1},
        )

    mixed_t, d_out, back_rows, wo_grads = call(
        mid_kernel,
        (shape(256, TOKENS), head_shape, state_shape[0], shape(PLANES, WO, ROWS)),
        (info, q, start, kvs[4], *state, cot, w_out),
        (2 * score + 4 * TOKENS * 2048 * WO, 8 << 20, 1 << 20),
        scratch=[pltpu.VMEM((8, 1, TOKENS), f32), pltpu.VMEM((256, TOKENS), f32)] + fwd_scratch(1),
    )
    wo_sum = lax.psum_scatter(
        wo_grads, "fsdp", axis_index_groups=RING_GROUPS, scatter_dimension=0, tiled=True
    )[0]

    common = (info, q, d_out, back_rows, start)
    tie = lax.optimization_barrier
    add = lambda a, b: (a.astype(f32) + b.astype(f32)).astype(bf16)

    def back_step(offsets, acc):
        n = len(offsets)
        args = common + tuple(kvs[o % PLANES] for o in offsets)
        return call(
            functools.partial(bwd_kernel, offsets),
            (state_shape[1],) + (kv_shape,) * n,
            args if acc is None else args + (acc,),
            (5 * n * score, 3 << 20, n << 20),
            scratch=bwd_scratch(n),
            alias=None if acc is None else {len(args): 0},
        )

    acc, down, up = back_step((-4, 3), None)
    (attn,) = call(
        attn_kernel,
        (shape(TOKENS, 2048),),
        (mixed_t, w_out),
        (2 * TOKENS * 2048 * WO, 4 << 20, 0),
        scalars=0,
    )
    acc, attn = tie((acc, attn))
    attn = lax.psum_scatter(
        attn, "fsdp", axis_index_groups=PLANE_GROUPS, scatter_dimension=0, tiled=True
    )
    down, up = along(down, -1), along(up, 1)
    for offsets in ((-3, 2), (-2, 1)):
        acc, *terms = back_step(offsets, acc)
        acc, down, up = tie((acc, add(down, terms[0]), add(up, terms[1])))
        down, up = along(down, -1), along(up, 1)
    acc, term = back_step((-1,), acc)
    acc, down = tie((acc, add(down, term)))
    down = along(down, -1)
    own_kv, q_grads = call(
        own_kernel,
        (shape(TOKENS, 128, dtype=f32), shape(PLANES, WO, ROWS)),
        (*common, kvs[0], acc, cos_t, sin_t, normed),
        (5 * score + 2 * TOKENS * 2048 * WO, 5 << 20, 1 << 20),
        scratch=[pltpu.VMEM((256, TOKENS), f32), pltpu.VMEM((WO, TOKENS), bf16)] + bwd_scratch(1),
    )
    own_kv, wo_sum = tie((own_kv, wo_sum))
    grads = call(
        last_kernel,
        (shape(QKV, ROWS),) * PLANES,
        (info, own_kv, down, up, cos_t, sin_t, normed, q_grads),
        (2 * TOKENS * 2048 * 128, 6 << 20, 0),
        scratch=[pltpu.VMEM((128, TOKENS), bf16)],
    )
    qkv_sum = sum(x.astype(f32) for x in (*ring_scatter(grads), grads[0]))

    qkv_sum, attn = tie((qkv_sum, attn))
    sums = jnp.concatenate([qkv_sum, wo_sum.astype(f32)], axis=0).T.astype(bf16)
    by_head = to_side(sums.reshape(SIDE, ROWS // SIDE, QKV + WO), own)
    grad = jnp.concatenate(
        [b[:, lo:hi] for lo, hi in ((0, 256), (256, 320), (320, 384), (384, 640)) for b in by_head],
        axis=1,
    ).astype(f32)

    new_m = BETA * old_m + grad
    new_w = old_w - RATE * new_m
    groups = lax.axis_size("group")
    bits = groups.bit_length() - 1

    def swap(b, x):
        return lax.ppermute(x, "group", [(i, i ^ 1 << b) for i in range(groups)])

    other = lax.switch(
        jnp.remainder(distance[0], bits),
        [functools.partial(swap, b) for b in range(bits)],
        jnp.stack([new_w, new_m]).astype(bf16),
    ).astype(f32)
    out_w = 0.5 * (new_w + other[0])
    out_m = 0.5 * (new_m + other[1])
    return (attn[None], out_w[None], out_m[None])


def solution(mesh):
    return jax.shard_map(
        on_device,
        mesh=mesh,
        in_specs=(
            P("group", "fsdp", None),
            P("group", None),
            P("group", "fsdp", None),
            P("group", "fsdp", None),
            P("group", "fsdp", None),
            P("group", "fsdp"),
            P(),
        ),
        out_specs=(P("group", "fsdp", None), P("group", "fsdp", None), P("group", "fsdp", None)),
        check_vma=False,
    )
```

```python
import functools
import math

import jax
import jax.numpy as jnp
from jax import lax
from jax.experimental import pallas as pl
from jax.experimental.pallas import tpu as pltpu
from jax.sharding import PartitionSpec as P

QUERY_HEADS = 16
KEY_VALUE_HEADS = 4
HEAD_SIZE = 64
REPEAT = QUERY_HEADS // KEY_VALUE_HEADS

EPS = 1e-05
BETA = 0.9
RATE = 0.01
THETA = 500000.0
MASK_FILL = -1e30
TOP_START = -1e20

PLANES = 8
SIDE = 4
TOKENS = 512
ROWS = 256
QKV = 384
WO = 256
NT = (((1,), (1,)), ((), ()))
NN = (((1,), (0,)), ((), ()))

f32 = jnp.float32
bf16 = jnp.bfloat16


def dot(a, b, dims=NN):
    return lax.dot_general(a, b, dims, preferred_element_type=f32)


def along(x, step):
    n = PLANES * SIDE
    return lax.ppermute(x, "fsdp", [(i, (i + SIDE * step) % n) for i in range(n)])


def beside(x, mask):
    return lax.ppermute(x, "fsdp", [(i, i ^ mask) for i in range(PLANES * SIDE)])


def ring_gather(x, beside_it=None):
    got = [None] * PLANES
    got[0] = x
    down = up = x
    for s in range(1, PLANES // 2 + 1):
        down = along(down, 1)
        if s < PLANES // 2:
            up = along(up, -1)
            if beside_it is not None:
                down, up = lax.optimization_barrier((down, up))
            if s == 2 and beside_it is not None:
                down, up, beside_it = lax.optimization_barrier((down, up, beside_it))
            got[s] = up
        got[-s % PLANES] = down
    return got, beside_it


def ring_scatter(terms):
    add = lambda a, b: a.astype(f32) + b.astype(f32)
    up = down = None
    for s in range(PLANES // 2, 0, -1):
        t = terms[-s % PLANES]
        down = along(t if down is None else add(down, t).astype(bf16), -1)
        if s < PLANES // 2:
            t = terms[s]
            up = along(t if up is None else add(up, t).astype(bf16), 1)
    return down, up


def call(kernel, outs, args, cost, scalars=1, scratch=(), rows=None, mib=60):
    rows = rows or {}
    bufs_of = lambda i: (rows[i][1], *args[i].shape[1:]) if i in rows else args[i].shape
    flops, bytes_, exps = cost
    vmem, smem, hbm = (
        pl.BlockSpec(memory_space=m) for m in (pltpu.VMEM, pltpu.SMEM, pltpu.HBM)
    )
    large = [i for i, a in enumerate(args) if a.size * a.dtype.itemsize >= 1 << 15]
    in_specs = [smem] * scalars + [vmem] * (len(args) - scalars)
    for i in large:
        in_specs[i] = hbm

    def fetching(*refs):
        ins, rest = list(refs[: len(args)]), refs[len(args) : -len(large) - 1]
        bufs, sems = refs[-len(large) - 1 : -1], refs[-1]
        copies = [
            pltpu.make_async_copy(
                ins[i].at[pl.ds(*rows[i])] if i in rows else ins[i], buf, sems.at[k]
            )
            for k, (i, buf) in enumerate(zip(large, bufs))
        ]
        for c in copies:
            c.start()
        for c in copies:
            c.wait()
        for i, buf in zip(large, bufs):
            ins[i] = buf
        kernel(*ins, *rest)

    return pl.pallas_call(
        fetching,
        out_shape=tuple(outs),
        in_specs=in_specs,
        out_specs=tuple(smem if o.shape == INFO.shape else vmem for o in outs),
        scratch_shapes=[
            *scratch,
            *[pltpu.VMEM(bufs_of(i), args[i].dtype) for i in large],
            pltpu.SemaphoreType.DMA((len(large),)),
        ],
        compiler_params=pltpu.CompilerParams(vmem_limit_bytes=mib * 1024 * 1024),
        cost_estimate=pl.CostEstimate(flops=flops, bytes_accessed=bytes_, transcendentals=exps),
    )(*args)


def shape(*dims, dtype=bf16):
    return jax.ShapeDtypeStruct(dims, dtype)


INFO = shape(3, dtype=jnp.int32)


def plane_at(info, offset):
    return lax.rem(info[0] + (offset % PLANES), PLANES)


def lanes(shape):
    return lax.broadcasted_iota(jnp.int32, shape, len(shape) - 1)


def proj_kernel(place, cos, sin, wo_rows, *refs):
    parts, blocks = refs[:SIDE], refs[SIDE : SIDE + PLANES]
    normed, q_out, kv_out, start, info = refs[SIDE + PLANES :]
    for k in range(SIDE):
        at = pl.multiple_of((place[1] ^ k) * 128, 128)
        normed[pl.ds(at, 128)] = parts[k][...]
    total = jnp.zeros((TOKENS, QKV), f32)
    for o in range(PLANES):
        at = pl.multiple_of(plane_at(place, o) * ROWS, ROWS)
        total = total + dot(normed[:, pl.ds(at, ROWS)], blocks[o][:ROWS])

    tails = sum(b[ROWS : ROWS + 16].astype(f32)[:SIDE, :128] for b in blocks)
    lane = lanes(tails.shape)
    second = jnp.sum(jnp.where(lane == 0, tails, 0.0)).astype(jnp.int32)
    third = second + jnp.sum(jnp.where(lane == 1, tails, 0.0)).astype(jnp.int32)

    def start_of(t):
        return jnp.where(t >= third, third, jnp.where(t >= second, second, 0))

    start[...] = start_of(positions(place))
    info[0] = place[0]
    info[1] = start_of(place[0] * TOKENS)
    info[2] = start_of(place[0] * TOKENS + TOKENS - 1)

    lane = lanes((TOKENS, 128))
    first = lax.rem(lane, HEAD_SIZE) < HEAD_SIZE // 2
    low = lane < HEAD_SIZE
    c, s = cos[...], sin[...]

    def turned(u):
        return jnp.where(first, pltpu.roll(u, 96, 1), pltpu.roll(u, 32, 1))

    for pair in range(2):
        u = total[:, 128 * pair : 128 * pair + 128]
        u = (u * c + turned(u) * s) * (1.0 / math.sqrt(HEAD_SIZE))
        q_out[2 * pair] = jnp.where(low, u, 0.0).astype(bf16)
        q_out[2 * pair + 1] = jnp.where(low, pltpu.roll(u, 64, 1), 0.0).astype(bf16)
    u = total[:, 256:]
    kv_out[:TOKENS] = jnp.where(low, u * c + turned(u) * s, u).astype(bf16)
    kv_out[TOKENS : TOKENS + ROWS] = wo_rows[:, :128]
    kv_out[TOKENS + ROWS :] = wo_rows[:, 128:]


def masked(s, src, qpos, start):
    kpos = src * TOKENS + lax.broadcasted_iota(jnp.int32, (TOKENS, TOKENS), 0)
    return jnp.where((kpos <= qpos) & (kpos >= start), s, MASK_FILL)


def on_blocks(info, offsets, body):
    def step(i, carry):
        src = plane_at(info, offsets[0])
        for n, o in enumerate(offsets[1:], 1):
            src = jnp.where(i == n, plane_at(info, o), src)
        base = src * TOKENS
        seen = (src <= info[0]) & (base + TOKENS > info[1])
        edge = (src == info[0]) | (base < info[2])

        @pl.when(seen & edge)
        def _():
            body(i, src, True)

        if offsets != (0,):

            @pl.when(seen & jnp.logical_not(edge))
            def _():
                body(i, src, False)

        return carry

    lax.fori_loop(0, len(offsets), step, 0)


def for_heads(body):
    def step(h, carry):
        body(h, pl.ds(pl.multiple_of(h * HEAD_SIZE, HEAD_SIZE), HEAD_SIZE))
        return carry

    lax.fori_loop(0, REPEAT, step, 0, unroll=2)


def positions(info):
    return info[0] * TOKENS + lax.broadcasted_iota(jnp.int32, (1, TOKENS), 1)


def fwd_blocks(info, offsets, q, kvs, start, rows, acc, kv, value_t):
    for i, ref in enumerate(kvs):
        kv[i] = ref[...]

    def block(i, src, mask):
        value_t[...] = kv[i].T[HEAD_SIZE:]

        def head(h, at):
            s = dot(kv[i], q[h], NT)
            if mask:
                s = masked(s, src, positions(info), start[...])
            old = rows[h]
            top = jnp.maximum(old, jnp.max(s, axis=0, keepdims=True))
            p = jnp.exp(s - top)
            fade = jnp.exp(old - top)
            rows[h] = top
            rows[4 + h] = rows[4 + h] * fade + jnp.sum(p, axis=0, keepdims=True)
            acc[at] = acc[at] * fade + dot(value_t[...], p.astype(bf16))

        for_heads(head)

    on_blocks(info, offsets, block)


def fwd_scratch(n):
    return [pltpu.VMEM((n, TOKENS, 128), bf16), pltpu.VMEM((HEAD_SIZE, TOKENS), bf16)]


def fwd_kernel(offsets, info, q, start, *refs):
    n = len(offsets)
    kvs, refs = refs[:n], refs[n:]
    if offsets[0] == 0:
        rows, acc, *scratch = refs
        rows[0:4] = jnp.full((4, 1, TOKENS), TOP_START, f32)
        rows[4:8] = jnp.zeros((4, 1, TOKENS), f32)
        acc[...] = jnp.zeros(acc.shape, f32)
    else:
        rows_in, acc_in, rows, acc, *scratch = refs
        rows[...] = rows_in[...]
        acc[...] = acc_in[...]
    fwd_blocks(info, offsets, q, kvs, start, rows, acc, *scratch)


def out_block(ref):
    return jnp.concatenate([ref[:ROWS], ref[ROWS:]], axis=1)


def mid_kernel(info, place, q, start, kv, rows_in, acc_in, *refs):
    parts, blocks, refs = refs[:SIDE], refs[SIDE : SIDE + PLANES], refs[SIDE + PLANES :]
    mixed_t, d_out, back_rows, w_out = refs[:4]
    grads, (rows, acc, cot, *scratch) = refs[4 : 4 + PLANES], refs[4 + PLANES :]
    rows[...] = rows_in[...]
    acc[...] = acc_in[...]
    fwd_blocks(info, (-4,), q, (kv,), start, rows, acc, *scratch)
    for k in range(SIDE):
        at = pl.multiple_of((place[1] ^ k) * 128, 128)
        cot[pl.ds(at, 128)] = parts[k][...]
    for o in range(PLANES):
        at = pl.multiple_of(plane_at(info, o) * ROWS, ROWS)
        w_out[pl.ds(at, ROWS)] = out_block(blocks[o])
    d_mixed = dot(cot[...], w_out[...]).astype(bf16).astype(f32)
    inverse = jnp.concatenate([1.0 / rows[4 + h] for h in range(REPEAT)], axis=0)
    back_rows[0:4] = rows[0:4]
    for h in range(REPEAT):
        at = slice(64 * h, 64 * h + 64)
        mixed_t[at] = (acc[at] * inverse[h : h + 1]).astype(bf16)
    mt = mixed_t[...]
    prod = d_mixed.T * mt.astype(f32)
    for h in range(REPEAT):
        back_rows[4 + h] = inverse[h : h + 1] * jnp.sum(
            prod[64 * h : 64 * h + 64], axis=0, keepdims=True
        )
    by_row = jnp.concatenate([inverse, inverse], axis=0).T
    high = lanes((TOKENS, 128)) >= HEAD_SIZE
    for pair in range(2):
        u = d_mixed[:, 128 * pair : 128 * pair + 128]
        scale = [by_row[:, 2 * pair + i : 2 * pair + i + 1] for i in range(2)]
        u = u * jnp.where(high, scale[1], scale[0])
        d_out[2 * pair] = jnp.where(high, pltpu.roll(u, 64, 1), 0.0).astype(bf16)
        d_out[2 * pair + 1] = jnp.where(high, u, 0.0).astype(bf16)
    for o in range(PLANES):
        at = pl.multiple_of(plane_at(info, o) * ROWS, ROWS)
        term = dot(mt, cot[:, pl.ds(at, ROWS)]).astype(bf16)
        grads[o][:ROWS] = term[:, :128]
        grads[o][ROWS:] = term[:, 128:]


def attn_kernel(mixed_t, w_out, attn):
    mixed = mixed_t[...].astype(f32).T.astype(bf16)
    attn[...] = dot(mixed, w_out[...], NT).astype(bf16)


def bwd_blocks(info, offsets, q, d_out, rows, kvs, start, acc, sums, kv, key_t):
    for i, ref in enumerate(kvs):
        kv[i] = ref[...]
        sums[i] = jnp.zeros((TOKENS, 128), f32)

    def block(i, src, mask):
        key_t[...] = kv[i].T[:HEAD_SIZE]

        def head(h, at):
            s = dot(kv[i], q[h], NT)
            if mask:
                s = masked(s, src, positions(info), start[...])
            p = jnp.exp(s - rows[h])
            dp = dot(kv[i], d_out[h], NT)
            ds = (p * (dp - rows[4 + h])).astype(bf16)
            sums[i] = sums[i] + (dot(p.astype(bf16), d_out[h]) + dot(ds, q[h]))
            acc[at] = acc[at] + dot(key_t[...], ds)

        for_heads(head)

    on_blocks(info, offsets, block)


def bwd_scratch(n):
    return [pltpu.VMEM((n, TOKENS, 128), f32)] + fwd_scratch(n)


def bwd_kernel(offsets, info, q, d_out, rows, start, *refs):
    n = len(offsets)
    kvs, wo_terms, refs, scratch = refs[:n], refs[n : 2 * n], refs[2 * n : -3], refs[-3:]
    acc, outs = refs[-n - 1], refs[-n:]
    acc[...] = refs[0][...] if len(refs) > n + 1 else jnp.zeros(acc.shape, f32)
    bwd_blocks(info, offsets, q, d_out, rows, kvs, start, acc, *scratch)
    for i in range(n):
        outs[i][:TOKENS] = scratch[0][i].astype(bf16)
        outs[i][TOKENS:] = wo_terms[i][...]


def turn_back(u, c, s, out, at, scale):
    one, two = u[:32], u[32:]
    out[at : at + 32] = ((one * c + two * s) * scale).astype(bf16)
    out[at + 32 : at + 64] = ((two * c - one * s) * scale).astype(bf16)


def own_kernel(
    info, q, d_out, rows, start, kv, acc_in, cos_t, sin_t, normed,
    out, grads, acc, d_t, *scratch,
):
    acc[...] = acc_in[...]
    bwd_blocks(info, (0,), q, d_out, rows, (kv,), start, acc, *scratch)
    out[...] = scratch[0][0]
    c, s = cos_t[...], sin_t[...]
    for h in range(REPEAT):
        turn_back(acc[64 * h : 64 * h + 64], c, s, d_t, 64 * h, 1.0 / math.sqrt(HEAD_SIZE))
    for o in range(PLANES):
        at = pl.multiple_of(plane_at(info, o) * ROWS, ROWS)
        grads[o] = dot(d_t[...], normed[:, pl.ds(at, ROWS)]).astype(bf16)


def last_kernel(info, own, wo_own, got_a, got_b, cos_t, sin_t, normed, q_grads, *refs):
    wo_sum, grads, d_t = refs[0], refs[1 : 1 + PLANES], refs[1 + PLANES]
    got = got_a[...].astype(f32) + got_b[...].astype(f32)
    kv_t = (got[:TOKENS] + own[...]).T
    wo_sum[...] = got[TOKENS:] + wo_own[...].astype(f32)
    turn_back(kv_t[:64], cos_t[...], sin_t[...], d_t, 0, 1.0)
    d_t[64:128] = kv_t[64:].astype(bf16)
    for o in range(PLANES):
        at = pl.multiple_of(plane_at(info, o) * ROWS, ROWS)
        grads[o][:WO] = q_grads[o]
        grads[o][WO:] = dot(d_t[...], normed[:, pl.ds(at, ROWS)]).astype(bf16)


def to_side(blocks, own):
    pick = lambda arr, i: lax.dynamic_index_in_dim(arr, i, 0, keepdims=False)
    got = jnp.stack(
        [pick(blocks, own)] + [beside(pick(blocks, own ^ k), k) for k in range(1, SIDE)]
    )
    return [pick(got, own ^ i) for i in range(SIDE)]


def on_device(hidden, gain, weights, momentum, cotangent, segment, distance):
    rank = lax.axis_index("fsdp")
    plane, own = rank // SIDE, rank % SIDE
    old_w, old_m = weights[0], momentum[0]
    place = jnp.stack([plane, own]).astype(jnp.int32)

    local = hidden[0].astype(f32)
    normed = (
        local * lax.rsqrt(jnp.mean(local * local, axis=1, keepdims=True) + EPS) * gain[0][None, :]
    ).astype(bf16)
    normed, old_w = lax.optimization_barrier((normed, old_w))
    wb = old_w.astype(bf16)
    cuts = [wb[:, :1024], wb[:, 1024:1280], wb[:, 1280:1536], wb[:, 1536:]]
    by_head = jnp.concatenate([c.reshape(c.shape[0], SIDE, -1) for c in cuts], axis=2)
    by_head = by_head.transpose(1, 0, 2)
    seg = segment[0]
    lane = lax.broadcasted_iota(jnp.int32, (SIDE, 16, QKV + WO), 2)
    counts = jnp.where(lane == 0, jnp.sum(seg == 0), jnp.where(lane == 1, jnp.sum(seg == 1), 0))
    sent = jnp.concatenate([by_head, counts.astype(bf16)], axis=1)
    got = to_side(sent, own)
    wo_rows = jnp.concatenate([b[:64, QKV:] for b in got], axis=0)
    tail = jnp.concatenate([b[64:65, :QKV] for b in got] + [got[0][68:80, :QKV]], axis=0)
    w_rows = jnp.concatenate([b[:64, :QKV] for b in got] + [tail], axis=0)
    w_qkv, across = ring_gather(w_rows, beside(normed, 2))
    parts = [normed, beside(normed, 1), across, beside(across, 1)]

    half = HEAD_SIZE // 2
    tokens = plane * TOKENS + jnp.arange(TOKENS, dtype=jnp.int32)
    freq = jnp.power(THETA, -jnp.arange(half, dtype=f32) * 2.0 / HEAD_SIZE)
    angle = tokens.astype(f32)[:, None] * freq[None, :]
    cosine, sine = jnp.cos(angle), jnp.sin(angle)
    cos_rows = jnp.concatenate([cosine] * 4, axis=1)
    sin_rows = jnp.concatenate([-sine, sine] * 2, axis=1)
    cos_t, sin_t = cosine.T, sine.T

    state_shape = (shape(8, 1, TOKENS, dtype=f32), shape(256, TOKENS, dtype=f32))
    head_shape = shape(REPEAT, TOKENS, 128)
    sent_shape = shape(2 * TOKENS, 128)
    keys = (0, TOKENS)
    score = 2 * REPEAT * TOKENS * TOKENS * 128

    normed, q, kv, start, info = call(
        proj_kernel,
        (shape(TOKENS, 2048), head_shape, sent_shape, shape(1, TOKENS, dtype=jnp.int32), INFO),
        (place, cos_rows, sin_rows, wo_rows, *parts, *w_qkv),
        (2 * TOKENS * 2048 * QKV, 8 << 20, 0),
    )

    kvs, _ = ring_gather(kv)
    cot, _ = lax.optimization_barrier((cotangent[0], q))
    across = beside(cot, 2)
    cots = [cot, beside(cot, 1), across, beside(across, 1)]
    state = call(
        functools.partial(fwd_kernel, (0,)),
        state_shape,
        (info, q, start, kvs[0]),
        (2 * score, 2 << 20, 1 << 20),
        scratch=fwd_scratch(1),
        rows={3: keys},
    )
    for offsets in ((-1, 1), (-2, 2), (-3, 3)):
        state = call(
            functools.partial(fwd_kernel, offsets),
            state_shape,
            (info, q, start, *[kvs[o % PLANES] for o in offsets], *state),
            (4 * score, 2 << 20, 2 << 20),
            scratch=fwd_scratch(2),
            rows={3: keys, 4: keys},
        )

    mixed_t, d_out, back_rows, w_out, *wo_grads = call(
        mid_kernel,
        (shape(256, TOKENS), head_shape, state_shape[0], shape(2048, WO))
        + (shape(TOKENS, 128),) * PLANES,
        (info, place, q, start, kvs[4], *state, *cots, *kvs),
        (2 * score + 4 * TOKENS * 2048 * WO, 8 << 20, 1 << 20),
        scalars=2,
        scratch=[pltpu.VMEM((8, 1, TOKENS), f32), pltpu.VMEM((256, TOKENS), f32)]
        + [pltpu.VMEM((TOKENS, 2048), bf16)]
        + fwd_scratch(1),
        rows={4: keys} | {7 + SIDE + o: (TOKENS, TOKENS) for o in range(PLANES)},
    )

    common = (info, q, d_out, back_rows, start)
    tie = lax.optimization_barrier
    add = lambda a, b: (a.astype(f32) + b.astype(f32)).astype(bf16)

    def back_step(offsets, acc):
        n = len(offsets)
        args = common + tuple(x[o % PLANES] for x in (kvs, wo_grads) for o in offsets)
        return call(
            functools.partial(bwd_kernel, offsets),
            (state_shape[1],) + (sent_shape,) * n,
            args if acc is None else args + (acc,),
            (5 * n * score, 3 << 20, n << 20),
            scratch=bwd_scratch(n),
            rows={5 + i: keys for i in range(n)},
        )

    acc, down, up = back_step((-4, 3), None)
    (attn_part,) = call(
        attn_kernel,
        (shape(TOKENS, 2048),),
        (mixed_t, w_out),
        (2 * TOKENS * 2048 * WO, 4 << 20, 0),
        scalars=0,
    )
    acc, attn_parts = tie((acc, attn_part))
    down, up = along(down, -1), along(up, 1)
    for offsets in ((-3, 2), (-2, 1)):
        acc, *terms = back_step(offsets, acc)
        acc, down, up = tie((acc, add(down, terms[0]), add(up, terms[1])))
        down, up = along(down, -1), along(up, 1)
    parts = attn_parts.reshape(SIDE, TOKENS // SIDE, 2048)
    pick = lambda i: lax.dynamic_index_in_dim(parts, i, 0, keepdims=False)
    attn = [beside(pick(own ^ k), k) for k in range(1, SIDE)] + [pick(own)]
    attn = sum(x.astype(f32) for x in attn).astype(bf16)
    acc, term = back_step((-1,), acc)
    acc, down, attn = tie((acc, add(down, term), attn))
    down = along(down, -1)
    own_kv, q_grads = call(
        own_kernel,
        (shape(TOKENS, 128, dtype=f32), shape(PLANES, WO, ROWS)),
        (*common, kvs[0], acc, cos_t, sin_t, normed),
        (5 * score + 2 * TOKENS * 2048 * WO, 5 << 20, 1 << 20),
        scratch=[pltpu.VMEM((256, TOKENS), f32), pltpu.VMEM((WO, TOKENS), bf16)] + bwd_scratch(1),
        rows={5: keys},
    )
    wo_sum, *grads = call(
        last_kernel,
        (shape(TOKENS, 128, dtype=f32),) + (shape(QKV, ROWS),) * PLANES,
        (info, own_kv, wo_grads[0], down, up, cos_t, sin_t, normed, q_grads),
        (2 * TOKENS * 2048 * 128, 6 << 20, 0),
        scratch=[pltpu.VMEM((128, TOKENS), bf16)],
    )
    qkv_sum = sum(x.astype(f32) for x in (*ring_scatter(grads), grads[0]))

    wo_sum = jnp.concatenate([wo_sum[:ROWS], wo_sum[ROWS:]], axis=1)
    sums = jnp.concatenate([qkv_sum, wo_sum], axis=0).T.astype(bf16)
    by_head = to_side(sums.reshape(SIDE, ROWS // SIDE, QKV + WO), own)
    grad = jnp.concatenate(
        [b[:, lo:hi] for lo, hi in ((0, 256), (256, 320), (320, 384), (384, 640)) for b in by_head],
        axis=1,
    ).astype(f32)

    new_m = BETA * old_m + grad
    new_w = old_w - RATE * new_m
    groups = lax.axis_size("group")
    bits = groups.bit_length() - 1

    def swap(b, x):
        return lax.ppermute(x, "group", [(i, i ^ 1 << b) for i in range(groups)])

    other = lax.switch(
        jnp.remainder(distance[0], bits),
        [functools.partial(swap, b) for b in range(bits)],
        jnp.stack([new_w, new_m]).astype(bf16),
    ).astype(f32)
    out_w = 0.5 * (new_w + other[0])
    out_m = 0.5 * (new_m + other[1])
    return (attn[None], out_w[None], out_m[None])


def solution(mesh):
    return jax.shard_map(
        on_device,
        mesh=mesh,
        in_specs=(
            P("group", "fsdp", None),
            P("group", None),
            P("group", "fsdp", None),
            P("group", "fsdp", None),
            P("group", "fsdp", None),
            P("group", "fsdp"),
            P(),
        ),
        out_specs=(P("group", "fsdp", None), P("group", "fsdp", None), P("group", "fsdp", None)),
        check_vma=False,
    )
```

```python
import functools
import math

import jax
import jax.numpy as jnp
from jax import lax
from jax.experimental import pallas as pl
from jax.experimental.pallas import tpu as pltpu
from jax.sharding import PartitionSpec as P

QUERY_HEADS = 16
KEY_VALUE_HEADS = 4
HEAD_SIZE = 64
REPEAT = QUERY_HEADS // KEY_VALUE_HEADS

EPS = 1e-05
BETA = 0.9
RATE = 0.01
THETA = 500000.0
MASK_FILL = -1e30
TOP_START = -1e20

PLANES = 8
SIDE = 4
TOKENS = 512
ROWS = 256
QKV = 384
WO = 256
NT = (((1,), (1,)), ((), ()))
NN = (((1,), (0,)), ((), ()))

f32 = jnp.float32
bf16 = jnp.bfloat16


def dot(a, b, dims=NN):
    return lax.dot_general(a, b, dims, preferred_element_type=f32)


def along(x, step):
    n = PLANES * SIDE
    return lax.ppermute(x, "fsdp", [(i, (i + SIDE * step) % n) for i in range(n)])


def beside(x, mask):
    return lax.ppermute(x, "fsdp", [(i, i ^ mask) for i in range(PLANES * SIDE)])


def ring_gather(x, beside_it=None):
    got = [None] * PLANES
    got[0] = x
    down = up = x
    for s in range(1, PLANES // 2 + 1):
        down = along(down, 1)
        if s < PLANES // 2:
            up = along(up, -1)
            if beside_it is not None:
                down, up = lax.optimization_barrier((down, up))
            if s == 2 and beside_it is not None:
                down, up, beside_it = lax.optimization_barrier((down, up, beside_it))
            got[s] = up
        got[-s % PLANES] = down
    return got, beside_it


def call(kernel, outs, args, cost=(1 << 20, 1 << 20, 0), scalars=1, scratch=(), alias=None, mib=8):
    flops, bytes_, exps = cost
    vmem, smem = (pl.BlockSpec(memory_space=m) for m in (pltpu.VMEM, pltpu.SMEM))
    return pl.pallas_call(
        kernel,
        out_shape=tuple(outs),
        in_specs=[smem] * scalars + [vmem] * (len(args) - scalars),
        out_specs=tuple(smem if o.shape == INFO.shape else vmem for o in outs),
        scratch_shapes=scratch,
        input_output_aliases=alias or {},
        compiler_params=pltpu.CompilerParams(vmem_limit_bytes=mib * 1024 * 1024),
        cost_estimate=pl.CostEstimate(flops=flops, bytes_accessed=bytes_, transcendentals=exps),
    )(*args)


def shape(*dims, dtype=bf16):
    return jax.ShapeDtypeStruct(dims, dtype)


INFO = shape(3, dtype=jnp.int32)


def add_kernel(*refs):
    n = len(refs) // 3
    for a, b, out in zip(refs[:n], refs[n : 2 * n], refs[2 * n :]):
        out[...] = (a[...].astype(f32) + b[...].astype(f32)).astype(bf16)


def add(got, terms):
    like = [shape(*t.shape) for t in terms]
    return call(add_kernel, like, (*got, *terms), scalars=0)


def ring_scatter(terms):
    down, up = along(terms[4], -1), along(terms[3], 1)
    for s in (2, 1):
        down, up = add((down, up), (terms[-s - 1], terms[s]))
        down, up = along(down, -1), along(up, 1)
    (down,) = add((down,), (terms[-1],))
    return along(down, -1), up


def prep_kernel(place, hidden, gain, weights, seg, normed, *refs):
    outs, sent = refs[:SIDE], refs[SIDE]
    x = hidden[...].astype(f32)
    scale = lax.rsqrt(jnp.mean(x * x, axis=1, keepdims=True) + EPS)
    normed[...] = (x * scale * gain[...]).astype(bf16)
    documents = seg[...]
    first, second = (jnp.sum((documents == d).astype(f32)) for d in range(2))
    lane = lanes((16, QKV + WO))
    counts = jnp.where(lane == 0, first, jnp.where(lane == 1, second, 0.0)).astype(bf16)
    for j in range(SIDE):
        cuts = [(256 * j, 256), (1024 + 64 * j, 64), (1280 + 64 * j, 64), (1536 + 256 * j, 256)]
        block = jnp.concatenate([weights[:, at : at + n] for at, n in cuts], axis=1)
        sent[j, :64] = block.astype(bf16)
        sent[j, 64:] = counts
    for k in range(SIDE):
        outs[k][...] = sent[place[1] ^ k]


def join_kernel(place, *refs):
    got, (w_rows, wo_rows) = refs[:SIDE], refs[SIDE:]
    row = lax.broadcasted_iota(jnp.int32, (16, QKV), 0)
    tail = jnp.zeros((16, QKV), f32)
    for k in range(SIDE):
        at = pl.multiple_of((place[1] ^ k) * 64, 64)
        w_rows[pl.ds(at, 64)] = got[k][:64, :QKV]
        wo_rows[pl.ds(at, 64)] = got[k][:64, QKV:]
        tail = jnp.where(row == k, got[k][64:, :QKV].astype(f32), tail)
    w_rows[ROWS:] = tail.astype(bf16)


def sum_kernel(*refs):
    refs[-1][...] = sum(r[...].astype(f32) for r in refs[:-1]).astype(bf16)


def split_kernel(place, down, up, own, wo_sum, *refs):
    outs, total = refs[:SIDE], refs[SIDE]
    qkv = down[...].astype(f32) + up[...].astype(f32) + own[...].astype(f32)
    total[:, :QKV] = qkv.T
    total[:, QKV:] = jnp.concatenate([wo_sum[:ROWS], wo_sum[ROWS:]], axis=1).T
    for k in range(SIDE):
        at = pl.multiple_of((place[1] ^ k) * 64, 64)
        outs[k][...] = total[pl.ds(at, 64)].astype(bf16)


def step_kernel(place, weights, momentum, *refs):
    got, (new_w, new_m, both, by_head) = refs[:SIDE], refs[SIDE:]
    for k in range(SIDE):
        by_head[place[1] ^ k] = got[k][...]
    for lo, n, to in ((0, 256, 0), (256, 64, 1024), (320, 64, 1280), (384, 256, 1536)):
        grad = jnp.concatenate([by_head[j, :, lo : lo + n] for j in range(SIDE)], axis=1)
        at = slice(to, to + SIDE * n)
        m = BETA * momentum[:, at] + grad.astype(f32)
        w = weights[:, at] - RATE * m
        new_m[:, at] = m
        new_w[:, at] = w
        both[0, :, at] = w.astype(bf16)
        both[1, :, at] = m.astype(bf16)


def mean_kernel(w, m, other, out_w, out_m):
    out_w[...] = 0.5 * (w[...] + other[0].astype(f32))
    out_m[...] = 0.5 * (m[...] + other[1].astype(f32))


def plane_at(info, offset):
    return lax.rem(info[0] + (offset % PLANES), PLANES)


def lanes(shape):
    return lax.broadcasted_iota(jnp.int32, shape, len(shape) - 1)


def proj_kernel(place, cos, sin, wo_rows, *refs):
    parts, blocks = refs[:SIDE], refs[SIDE : SIDE + PLANES]
    normed, q_out, kv_out, start, info = refs[SIDE + PLANES :]
    for k in range(SIDE):
        at = pl.multiple_of((place[1] ^ k) * 128, 128)
        normed[pl.ds(at, 128)] = parts[k][...]
    total = jnp.zeros((TOKENS, QKV), f32)
    for o in range(PLANES):
        at = pl.multiple_of(plane_at(place, o) * ROWS, ROWS)
        total = total + dot(normed[:, pl.ds(at, ROWS)], blocks[o][:ROWS])

    tails = sum(b[ROWS : ROWS + 16].astype(f32)[:SIDE, :128] for b in blocks)
    lane = lanes(tails.shape)
    second = jnp.sum(jnp.where(lane == 0, tails, 0.0)).astype(jnp.int32)
    third = second + jnp.sum(jnp.where(lane == 1, tails, 0.0)).astype(jnp.int32)

    def start_of(t):
        return jnp.where(t >= third, third, jnp.where(t >= second, second, 0))

    start[...] = start_of(positions(place))
    info[0] = place[0]
    info[1] = start_of(place[0] * TOKENS)
    info[2] = start_of(place[0] * TOKENS + TOKENS - 1)

    lane = lanes((TOKENS, 128))
    first = lax.rem(lane, HEAD_SIZE) < HEAD_SIZE // 2
    low = lane < HEAD_SIZE
    c, s = cos[...], sin[...]

    def turned(u):
        return jnp.where(first, pltpu.roll(u, 96, 1), pltpu.roll(u, 32, 1))

    for pair in range(2):
        u = total[:, 128 * pair : 128 * pair + 128]
        u = (u * c + turned(u) * s) * (1.0 / math.sqrt(HEAD_SIZE))
        q_out[2 * pair] = jnp.where(low, u, 0.0).astype(bf16)
        q_out[2 * pair + 1] = jnp.where(low, pltpu.roll(u, 64, 1), 0.0).astype(bf16)
    u = total[:, 256:]
    kv_out[:TOKENS] = jnp.where(low, u * c + turned(u) * s, u).astype(bf16)
    kv_out[TOKENS : TOKENS + ROWS] = wo_rows[:, :128]
    kv_out[TOKENS + ROWS :] = wo_rows[:, 128:]


def masked(s, src, qpos, start):
    kpos = src * TOKENS + lax.broadcasted_iota(jnp.int32, (TOKENS, TOKENS), 0)
    return jnp.where((kpos <= qpos) & (kpos >= start), s, MASK_FILL)


def on_blocks(info, offsets, body):
    def step(i, carry):
        src = plane_at(info, offsets[0])
        for n, o in enumerate(offsets[1:], 1):
            src = jnp.where(i == n, plane_at(info, o), src)
        base = src * TOKENS
        seen = (src <= info[0]) & (base + TOKENS > info[1])
        edge = (src == info[0]) | (base < info[2])

        @pl.when(seen & edge)
        def _():
            body(i, src, True)

        if offsets != (0,):

            @pl.when(seen & jnp.logical_not(edge))
            def _():
                body(i, src, False)

        return carry

    lax.fori_loop(0, len(offsets), step, 0)


def for_heads(body):
    def step(h, carry):
        body(h, pl.ds(pl.multiple_of(h * HEAD_SIZE, HEAD_SIZE), HEAD_SIZE))
        return carry

    lax.fori_loop(0, REPEAT, step, 0)


def positions(info):
    return info[0] * TOKENS + lax.broadcasted_iota(jnp.int32, (1, TOKENS), 1)


def fwd_blocks(info, offsets, q, kvs, start, rows, acc, kv, value_t):
    for i, ref in enumerate(kvs):
        kv[i] = ref[:TOKENS]

    def block(i, src, mask):
        value_t[...] = kv[i].T[HEAD_SIZE:]

        def head(h, at):
            s = dot(kv[i], q[h], NT)
            if mask:
                s = masked(s, src, positions(info), start[...])
            old = rows[h]
            top = jnp.maximum(old, jnp.max(s, axis=0, keepdims=True))
            p = jnp.exp(s - top)
            fade = jnp.exp(old - top)
            rows[h] = top
            rows[4 + h] = rows[4 + h] * fade + jnp.sum(p, axis=0, keepdims=True)
            acc[at] = acc[at] * fade + dot(value_t[...], p.astype(bf16))

        for_heads(head)

    on_blocks(info, offsets, block)


def fwd_scratch(n):
    return [pltpu.VMEM((n, TOKENS, 128), bf16), pltpu.VMEM((HEAD_SIZE, TOKENS), bf16)]


def fwd_kernel(offsets, info, q, start, *refs):
    n = len(offsets)
    kvs, refs = refs[:n], refs[n:]
    if offsets[0] == 0:
        rows, acc, *scratch = refs
        rows[0:4] = jnp.full((4, 1, TOKENS), TOP_START, f32)
        rows[4:8] = jnp.zeros((4, 1, TOKENS), f32)
        acc[...] = jnp.zeros(acc.shape, f32)
    else:
        rows_in, acc_in, rows, acc, *scratch = refs
        rows[...] = rows_in[...]
        acc[...] = acc_in[...]
    fwd_blocks(info, offsets, q, kvs, start, rows, acc, *scratch)


def out_block(ref):
    return jnp.concatenate([ref[TOKENS : TOKENS + ROWS], ref[TOKENS + ROWS :]], axis=1)


def mid_kernel(info, place, q, start, kv, rows_in, acc_in, *refs):
    parts, blocks, refs = refs[:SIDE], refs[SIDE : SIDE + PLANES], refs[SIDE + PLANES :]
    mixed_t, d_out, back_rows, w_out = refs[:4]
    grads, (rows, acc, cot, *scratch) = refs[4 : 4 + PLANES], refs[4 + PLANES :]
    rows[...] = rows_in[...]
    acc[...] = acc_in[...]
    fwd_blocks(info, (-4,), q, (kv,), start, rows, acc, *scratch)
    for k in range(SIDE):
        at = pl.multiple_of((place[1] ^ k) * 128, 128)
        cot[pl.ds(at, 128)] = parts[k][...]
    for o in range(PLANES):
        at = pl.multiple_of(plane_at(info, o) * ROWS, ROWS)
        w_out[pl.ds(at, ROWS)] = out_block(blocks[o])
    d_mixed = dot(cot[...], w_out[...]).astype(bf16).astype(f32)
    inverse = jnp.concatenate([1.0 / rows[4 + h] for h in range(REPEAT)], axis=0)
    back_rows[0:4] = rows[0:4]
    for h in range(REPEAT):
        at = slice(64 * h, 64 * h + 64)
        mixed_t[at] = (acc[at] * inverse[h : h + 1]).astype(bf16)
    mt = mixed_t[...]
    prod = d_mixed.T * mt.astype(f32)
    for h in range(REPEAT):
        back_rows[4 + h] = inverse[h : h + 1] * jnp.sum(
            prod[64 * h : 64 * h + 64], axis=0, keepdims=True
        )
    by_row = jnp.concatenate([inverse, inverse], axis=0).T
    high = lanes((TOKENS, 128)) >= HEAD_SIZE
    for pair in range(2):
        u = d_mixed[:, 128 * pair : 128 * pair + 128]
        scale = [by_row[:, 2 * pair + i : 2 * pair + i + 1] for i in range(2)]
        u = u * jnp.where(high, scale[1], scale[0])
        d_out[2 * pair] = jnp.where(high, pltpu.roll(u, 64, 1), 0.0).astype(bf16)
        d_out[2 * pair + 1] = jnp.where(high, u, 0.0).astype(bf16)
    for o in range(PLANES):
        at = pl.multiple_of(plane_at(info, o) * ROWS, ROWS)
        term = dot(mt, cot[:, pl.ds(at, ROWS)]).astype(bf16)
        grads[o][:ROWS] = term[:, :128]
        grads[o][ROWS:] = term[:, 128:]


def attn_kernel(place, mixed_t, w_out, *refs):
    outs, mixed = refs[:SIDE], refs[SIDE]
    mixed[...] = mixed_t[...].astype(f32).T
    for k in range(SIDE):
        at = pl.multiple_of((place[1] ^ k) * 128, 128)
        outs[k][...] = dot(mixed[pl.ds(at, 128)].astype(bf16), w_out[...], NT).astype(bf16)


def bwd_blocks(info, offsets, q, d_out, rows, kvs, start, acc, sums, kv, key_t):
    for i, ref in enumerate(kvs):
        kv[i] = ref[:TOKENS]
        sums[i] = jnp.zeros((TOKENS, 128), f32)

    def block(i, src, mask):
        key_t[...] = kv[i].T[:HEAD_SIZE]

        def head(h, at):
            s = dot(kv[i], q[h], NT)
            if mask:
                s = masked(s, src, positions(info), start[...])
            p = jnp.exp(s - rows[h])
            dp = dot(kv[i], d_out[h], NT)
            ds = (p * (dp - rows[4 + h])).astype(bf16)
            sums[i] = sums[i] + (dot(p.astype(bf16), d_out[h]) + dot(ds, q[h]))
            acc[at] = acc[at] + dot(key_t[...], ds)

        for_heads(head)

    on_blocks(info, offsets, block)


def bwd_scratch(n):
    return [pltpu.VMEM((n, TOKENS, 128), f32)] + fwd_scratch(n)


def bwd_kernel(offsets, info, q, d_out, rows, start, *refs):
    n = len(offsets)
    kvs, wo_terms, refs, scratch = refs[:n], refs[n : 2 * n], refs[2 * n : -3], refs[-3:]
    acc, outs = refs[-n - 1], refs[-n:]
    acc[...] = refs[0][...] if len(refs) > n + 1 else jnp.zeros(acc.shape, f32)
    bwd_blocks(info, offsets, q, d_out, rows, kvs, start, acc, *scratch)
    for i in range(n):
        outs[i][:TOKENS] = scratch[0][i].astype(bf16)
        outs[i][TOKENS:] = wo_terms[i][...]


def turn_back(u, c, s, out, at, scale):
    one, two = u[:32], u[32:]
    out[at : at + 32] = ((one * c + two * s) * scale).astype(bf16)
    out[at + 32 : at + 64] = ((two * c - one * s) * scale).astype(bf16)


def own_kernel(
    info, q, d_out, rows, start, kv, acc_in, cos_t, sin_t, normed,
    out, grads, acc, d_t, *scratch,
):
    acc[...] = acc_in[...]
    bwd_blocks(info, (0,), q, d_out, rows, (kv,), start, acc, *scratch)
    out[...] = scratch[0][0]
    c, s = cos_t[...], sin_t[...]
    for h in range(REPEAT):
        turn_back(acc[64 * h : 64 * h + 64], c, s, d_t, 64 * h, 1.0 / math.sqrt(HEAD_SIZE))
    for o in range(PLANES):
        at = pl.multiple_of(plane_at(info, o) * ROWS, ROWS)
        grads[o] = dot(d_t[...], normed[:, pl.ds(at, ROWS)]).astype(bf16)


def last_kernel(info, own, wo_own, got_a, got_b, cos_t, sin_t, normed, q_grads, *refs):
    wo_sum, grads, d_t = refs[0], refs[1 : 1 + PLANES], refs[1 + PLANES]
    got = got_a[...].astype(f32) + got_b[...].astype(f32)
    kv_t = (got[:TOKENS] + own[...]).T
    wo_sum[...] = got[TOKENS:] + wo_own[...].astype(f32)
    turn_back(kv_t[:64], cos_t[...], sin_t[...], d_t, 0, 1.0)
    d_t[64:128] = kv_t[64:].astype(bf16)
    for o in range(PLANES):
        at = pl.multiple_of(plane_at(info, o) * ROWS, ROWS)
        grads[o][:WO] = q_grads[o]
        grads[o][WO:] = dot(d_t[...], normed[:, pl.ds(at, ROWS)]).astype(bf16)


def on_device(hidden, gain, weights, momentum, cotangent, segment, distance):
    rank = lax.axis_index("fsdp")
    plane, own = rank // SIDE, rank % SIDE
    old_w, old_m = weights[0], momentum[0]
    place = jnp.stack([plane, own]).astype(jnp.int32)

    tie = lax.optimization_barrier

    half = HEAD_SIZE // 2
    tokens = plane * TOKENS + jnp.arange(TOKENS, dtype=jnp.int32)
    freq = jnp.power(THETA, -jnp.arange(half, dtype=f32) * 2.0 / HEAD_SIZE)
    angle = tokens.astype(f32)[:, None] * freq[None, :]
    cosine, sine = jnp.cos(angle), jnp.sin(angle)
    cos_rows = jnp.concatenate([cosine] * 4, axis=1)
    sin_rows = jnp.concatenate([-sine, sine] * 2, axis=1)
    cos_t, sin_t = cosine.T, sine.T

    normed, *sent = call(
        prep_kernel,
        (shape(128, 2048),) + (shape(80, QKV + WO),) * SIDE,
        (place, hidden[0], gain, old_w, segment),
        scratch=[pltpu.VMEM((SIDE, 80, QKV + WO), bf16)],
    )
    got = [sent[0]] + [beside(sent[k], k) for k in range(1, SIDE)]
    w_rows, wo_rows = call(join_kernel, (shape(ROWS + 16, QKV), shape(ROWS, WO)), (place, *got))
    w_rows, cos_rows, sin_rows, cos_t, sin_t = tie((w_rows, cos_rows, sin_rows, cos_t, sin_t))
    w_qkv, across = ring_gather(w_rows, beside(normed, 2))
    parts = [normed, beside(normed, 1), across, beside(across, 1)]

    state_shape = (shape(8, 1, TOKENS, dtype=f32), shape(256, TOKENS, dtype=f32))
    head_shape = shape(REPEAT, TOKENS, 128)
    sent_shape = shape(2 * TOKENS, 128)
    score = 2 * REPEAT * TOKENS * TOKENS * 128

    normed, q, kv, start, info = call(
        proj_kernel,
        (shape(TOKENS, 2048), head_shape, sent_shape, shape(1, TOKENS, dtype=jnp.int32), INFO),
        (place, cos_rows, sin_rows, wo_rows, *parts, *w_qkv),
        (2 * TOKENS * 2048 * QKV, 8 << 20, 0),
    )

    kvs, _ = ring_gather(kv)
    cot, _ = lax.optimization_barrier((cotangent[0], q))
    across = beside(cot, 2)
    cots = [cot, beside(cot, 1), across, beside(across, 1)]
    state = call(
        functools.partial(fwd_kernel, (0,)),
        state_shape,
        (info, q, start, kvs[0]),
        (2 * score, 2 << 20, 1 << 20),
        scratch=fwd_scratch(1),
    )
    for offsets in ((-1, 1), (-2, 2), (-3, 3)):
        state = call(
            functools.partial(fwd_kernel, offsets),
            state_shape,
            (info, q, start, *[kvs[o % PLANES] for o in offsets], *state),
            (4 * score, 2 << 20, 2 << 20),
            scratch=fwd_scratch(2),
            alias={5: 0, 6: 1},
        )

    mixed_t, d_out, back_rows, w_out, *wo_grads = call(
        mid_kernel,
        (shape(256, TOKENS), head_shape, state_shape[0], shape(2048, WO))
        + (shape(TOKENS, 128),) * PLANES,
        (info, place, q, start, kvs[4], *state, *cots, *kvs),
        (2 * score + 4 * TOKENS * 2048 * WO, 8 << 20, 1 << 20),
        scalars=2,
        scratch=[pltpu.VMEM((8, 1, TOKENS), f32), pltpu.VMEM((256, TOKENS), f32)]
        + [pltpu.VMEM((TOKENS, 2048), bf16)]
        + fwd_scratch(1),
        mib=16,
    )

    common = (info, q, d_out, back_rows, start)

    def back_step(offsets, acc):
        n = len(offsets)
        args = common + tuple(x[o % PLANES] for x in (kvs, wo_grads) for o in offsets)
        return call(
            functools.partial(bwd_kernel, offsets),
            (state_shape[1],) + (sent_shape,) * n,
            args if acc is None else args + (acc,),
            (5 * n * score, 3 << 20, n << 20),
            scratch=bwd_scratch(n),
            alias=None if acc is None else {len(args): 0},
        )

    acc, down, up = back_step((-4, 3), None)
    attn = call(
        attn_kernel,
        (shape(TOKENS // SIDE, 2048),) * SIDE,
        (place, mixed_t, w_out),
        (2 * TOKENS * 2048 * WO, 4 << 20, 0),
        scratch=[pltpu.VMEM((TOKENS, WO), f32)],
    )
    acc, *attn = tie((acc, *attn))
    attn[1:] = [beside(attn[k], k) for k in range(1, SIDE)]
    down, up = along(down, -1), along(up, 1)
    for offsets in ((-3, 2), (-2, 1)):
        acc, *terms = back_step(offsets, acc)
        acc, down, up = tie((acc, *add((down, up), terms)))
        down, up = along(down, -1), along(up, 1)
    acc, term = back_step((-1,), acc)
    acc, down = tie((acc, *add((down,), (term,))))
    down = along(down, -1)
    own_kv, q_grads = call(
        own_kernel,
        (shape(TOKENS, 128, dtype=f32), shape(PLANES, WO, ROWS)),
        (*common, kvs[0], acc, cos_t, sin_t, normed),
        (5 * score + 2 * TOKENS * 2048 * WO, 5 << 20, 1 << 20),
        scratch=[pltpu.VMEM((256, TOKENS), f32), pltpu.VMEM((WO, TOKENS), bf16)] + bwd_scratch(1),
    )
    (attn,) = call(sum_kernel, (shape(TOKENS // SIDE, 2048),), attn, scalars=0)
    own_kv, attn = tie((own_kv, attn))
    wo_sum, *grads = call(
        last_kernel,
        (shape(TOKENS, 128, dtype=f32),) + (shape(QKV, ROWS),) * PLANES,
        (info, own_kv, wo_grads[0], down, up, cos_t, sin_t, normed, q_grads),
        (2 * TOKENS * 2048 * 128, 6 << 20, 0),
        scratch=[pltpu.VMEM((128, TOKENS), bf16)],
    )
    sent = call(
        split_kernel,
        (shape(64, QKV + WO),) * SIDE,
        (place, *ring_scatter(grads), grads[0], wo_sum),
        scratch=[pltpu.VMEM((ROWS, QKV + WO), f32)],
    )
    got = [sent[0]] + [beside(sent[k], k) for k in range(1, SIDE)]
    whole = shape(*old_w.shape, dtype=f32)
    new_w, new_m, both = call(
        step_kernel,
        (whole, whole, shape(2, *old_w.shape)),
        (place, old_w, old_m, *got),
        scratch=[pltpu.VMEM((SIDE, 64, QKV + WO), bf16)],
    )
    groups = lax.axis_size("group")
    bits = groups.bit_length() - 1

    def swap(b, x):
        return lax.ppermute(x, "group", [(i, i ^ 1 << b) for i in range(groups)])

    other = lax.switch(
        jnp.remainder(distance[0], bits), [functools.partial(swap, b) for b in range(bits)], both
    )
    out_w, out_m = call(mean_kernel, (whole, whole), (new_w, new_m, other), scalars=0)
    return (attn[None], out_w[None], out_m[None])


def solution(mesh):
    return jax.shard_map(
        on_device,
        mesh=mesh,
        in_specs=(
            P("group", "fsdp", None),
            P("group", None),
            P("group", "fsdp", None),
            P("group", "fsdp", None),
            P("group", "fsdp", None),
            P("group", "fsdp"),
            P(),
        ),
        out_specs=(P("group", "fsdp", None), P("group", "fsdp", None), P("group", "fsdp", None)),
        check_vma=False,
    )
```

```python
import functools
import math

import jax
import jax.numpy as jnp
from jax import lax
from jax.experimental import pallas as pl
from jax.experimental.pallas import tpu as pltpu
from jax.sharding import PartitionSpec as P

QUERY_HEADS = 16
KEY_VALUE_HEADS = 4
HEAD_SIZE = 64
REPEAT = QUERY_HEADS // KEY_VALUE_HEADS

EPS = 1e-05
BETA = 0.9
RATE = 0.01
THETA = 500000.0
MASK_FILL = -1e30
TOP_START = -1e20

PLANES = 8
SIDE = 4
TOKENS = 512
ROWS = 256
QKV = 384
WO = 256
NT = (((1,), (1,)), ((), ()))
NN = (((1,), (0,)), ((), ()))

f32 = jnp.float32
bf16 = jnp.bfloat16


def dot(a, b, dims=NN):
    return lax.dot_general(a, b, dims, preferred_element_type=f32)


def along(x, step):
    n = PLANES * SIDE
    return lax.ppermute(x, "fsdp", [(i, (i + SIDE * step) % n) for i in range(n)])


def beside(x, mask):
    return lax.ppermute(x, "fsdp", [(i, i ^ mask) for i in range(PLANES * SIDE)])


def ring_gather(x, beside_it=None):
    got = [None] * PLANES
    got[0] = x
    down = up = x
    for s in range(1, PLANES // 2 + 1):
        down = along(down, 1)
        if s < PLANES // 2:
            up = along(up, -1)
            if s == 2 and beside_it is not None:
                up, beside_it = lax.optimization_barrier((up, beside_it))
            got[s] = up
        got[-s % PLANES] = down
    return got, beside_it


def call(kernel, outs, args, cost=(1 << 20, 1 << 20, 0), scalars=1, scratch=(), alias=None, mib=8, space=pltpu.VMEM):
    flops, bytes_, exps = cost
    vmem, smem = (pl.BlockSpec(memory_space=m) for m in (pltpu.VMEM, pltpu.SMEM))
    return pl.pallas_call(
        kernel,
        out_shape=tuple(outs),
        in_specs=[smem] * scalars + [pl.BlockSpec(memory_space=space)] * (len(args) - scalars),
        out_specs=tuple(smem if o.shape == INFO.shape else vmem for o in outs),
        scratch_shapes=scratch,
        input_output_aliases=alias or {},
        compiler_params=pltpu.CompilerParams(vmem_limit_bytes=mib * 1024 * 1024),
        cost_estimate=pl.CostEstimate(flops=flops, bytes_accessed=bytes_, transcendentals=exps),
    )(*args)


def shape(*dims, dtype=bf16):
    return jax.ShapeDtypeStruct(dims, dtype)


INFO = shape(3, dtype=jnp.int32)


def add(got, term):
    return call(sum_kernel, (shape(*term.shape),), (got, term), scalars=0, mib=4)[0]


def ring_scatter(terms):
    down, up = along(terms[4], -1), along(terms[3], 1)
    for s in (2, 1):
        down, up = along(add(down, terms[-s - 1]), -1), along(add(up, terms[s]), 1)
    return along(add(down, terms[-1]), -1), up


def prep_kernel(place, *refs):
    sources, normed, rounded, refs = refs[:4], refs[4], refs[5], refs[6:]
    outs, sent, sems = refs[:SIDE], refs[SIDE], refs[-1]
    hidden, gain, weights, seg = refs[SIDE + 1 : SIDE + 5]
    copies = [
        pltpu.make_async_copy(source, to, sems.at[i])
        for i, (source, to) in enumerate(zip(sources, (hidden, gain, weights, seg)))
    ]
    for c in copies:
        c.start()
    for c in copies:
        c.wait()
    rounded[...] = weights[...].astype(bf16)
    x = hidden[...].astype(f32)
    scale = lax.rsqrt(jnp.mean(x * x, axis=1, keepdims=True) + EPS)
    normed[...] = (x * scale * gain[...]).astype(bf16)
    documents = seg[...]
    first, second = (jnp.sum((documents == d).astype(f32)) for d in range(2))
    lane = lanes((16, QKV + WO))
    counts = jnp.where(lane == 0, first, jnp.where(lane == 1, second, 0.0)).astype(bf16)
    for j in range(SIDE):
        cuts = [(256 * j, 256), (1024 + 64 * j, 64), (1280 + 64 * j, 64), (1536 + 256 * j, 256)]
        block = jnp.concatenate([weights[:, at : at + n] for at, n in cuts], axis=1)
        sent[j, :64] = block.astype(bf16)
        sent[j, 64:] = counts
    for k in range(SIDE):
        outs[k][...] = sent[place[1] ^ k]


def join_kernel(place, *refs):
    got, (w_rows, wo_rows) = refs[:SIDE], refs[SIDE:]
    row = lax.broadcasted_iota(jnp.int32, (16, QKV), 0)
    tail = jnp.zeros((16, QKV), f32)
    for k in range(SIDE):
        at = pl.multiple_of((place[1] ^ k) * 64, 64)
        w_rows[pl.ds(at, 64)] = got[k][:64, :QKV]
        wo_rows[pl.ds(at, 64)] = got[k][:64, QKV:]
        tail = jnp.where(row == k, got[k][64:, :QKV].astype(f32), tail)
    w_rows[ROWS:] = tail.astype(bf16)


def sum_kernel(*refs):
    refs[-1][...] = sum(r[...].astype(f32) for r in refs[:-1]).astype(bf16)


def split_kernel(place, down, up, own, wo_sum, *refs):
    outs, total = refs[:SIDE], refs[SIDE]
    qkv = down[...].astype(f32) + up[...].astype(f32) + own[...].astype(f32)
    total[:, :QKV] = qkv.T
    total[:, QKV:] = jnp.concatenate([wo_sum[:ROWS], wo_sum[ROWS:]], axis=1).T
    for k in range(SIDE):
        at = pl.multiple_of((place[1] ^ k) * 64, 64)
        outs[k][...] = total[pl.ds(at, 64)].astype(bf16)


def step_kernel(place, momentum, *refs):
    got, (new_m, sent, by_head) = refs[:SIDE], refs[SIDE:]
    for k in range(SIDE):
        by_head[place[1] ^ k] = got[k][...]
    for lo, n, to in ((0, 256, 0), (256, 64, 1024), (320, 64, 1280), (384, 256, 1536)):
        grad = jnp.concatenate([by_head[j, :, lo : lo + n] for j in range(SIDE)], axis=1)
        at = slice(to, to + SIDE * n)
        m = BETA * momentum[:, at] + grad.astype(f32)
        new_m[:, at] = m
        sent[:, at] = m.astype(bf16)


def mean_kernel(bit, w, m, other, *refs):
    partners, (out_w, out_m) = refs[:-2], refs[-2:]
    mean_m = 0.5 * (m[...] + other[...].astype(f32))
    out_m[...] = mean_m
    for b, partner in enumerate(partners):

        @pl.when(bit[0] == b)
        def _():
            out_w[...] = 0.5 * (w[...] + partner[...].astype(f32)) - RATE * mean_m


def plane_at(info, offset):
    return lax.rem(info[0] + (offset % PLANES), PLANES)


def lanes(shape):
    return lax.broadcasted_iota(jnp.int32, shape, len(shape) - 1)


def proj_kernel(place, cos, sin, wo_rows, *refs):
    parts, blocks = refs[:SIDE], refs[SIDE : SIDE + PLANES]
    normed, q_out, kv_out, start, info = refs[SIDE + PLANES :]
    for k in range(SIDE):
        at = pl.multiple_of((place[1] ^ k) * 128, 128)
        normed[pl.ds(at, 128)] = parts[k][...]
    total = jnp.zeros((TOKENS, QKV), f32)
    for o in range(PLANES):
        at = pl.multiple_of(plane_at(place, o) * ROWS, ROWS)
        total = total + dot(normed[:, pl.ds(at, ROWS)], blocks[o][:ROWS])

    tails = sum(b[ROWS : ROWS + 16].astype(f32)[:SIDE, :128] for b in blocks)
    lane = lanes(tails.shape)
    second = jnp.sum(jnp.where(lane == 0, tails, 0.0)).astype(jnp.int32)
    third = second + jnp.sum(jnp.where(lane == 1, tails, 0.0)).astype(jnp.int32)

    def start_of(t):
        return jnp.where(t >= third, third, jnp.where(t >= second, second, 0))

    start[...] = start_of(positions(place))
    info[0] = place[0]
    info[1] = start_of(place[0] * TOKENS)
    info[2] = start_of(place[0] * TOKENS + TOKENS - 1)

    lane = lanes((TOKENS, 128))
    first = lax.rem(lane, HEAD_SIZE) < HEAD_SIZE // 2
    low = lane < HEAD_SIZE
    c, s = cos[...], sin[...]

    def turned(u):
        return jnp.where(first, pltpu.roll(u, 96, 1), pltpu.roll(u, 32, 1))

    for pair in range(2):
        u = total[:, 128 * pair : 128 * pair + 128]
        u = (u * c + turned(u) * s) * (1.0 / math.sqrt(HEAD_SIZE))
        q_out[2 * pair] = jnp.where(low, u, 0.0).astype(bf16)
        q_out[2 * pair + 1] = jnp.where(low, pltpu.roll(u, 64, 1), 0.0).astype(bf16)
    u = total[:, 256:]
    kv_out[:TOKENS] = jnp.where(low, u * c + turned(u) * s, u).astype(bf16)
    kv_out[TOKENS : TOKENS + ROWS] = wo_rows[:, :128]
    kv_out[TOKENS + ROWS :] = wo_rows[:, 128:]


def masked(s, src, qpos, start):
    kpos = src * TOKENS + lax.broadcasted_iota(jnp.int32, (TOKENS, TOKENS), 0)
    return jnp.where((kpos <= qpos) & (kpos >= start), s, MASK_FILL)


def on_blocks(info, offsets, body):
    def step(i, carry):
        src = plane_at(info, offsets[0])
        for n, o in enumerate(offsets[1:], 1):
            src = jnp.where(i == n, plane_at(info, o), src)
        base = src * TOKENS
        seen = (src <= info[0]) & (base + TOKENS > info[1])
        edge = (src == info[0]) | (base < info[2])

        @pl.when(seen & edge)
        def _():
            body(i, src, True)

        if offsets != (0,):

            @pl.when(seen & jnp.logical_not(edge))
            def _():
                body(i, src, False)

        return carry

    lax.fori_loop(0, len(offsets), step, 0)


def for_heads(body):
    def step(h, carry):
        body(h, pl.ds(pl.multiple_of(h * HEAD_SIZE, HEAD_SIZE), HEAD_SIZE))
        return carry

    lax.fori_loop(0, REPEAT, step, 0)


def positions(info):
    return info[0] * TOKENS + lax.broadcasted_iota(jnp.int32, (1, TOKENS), 1)


def fwd_blocks(info, offsets, q, kvs, start, rows, acc, kv, value_t):
    for i, ref in enumerate(kvs):
        kv[i] = ref[:TOKENS]

    def block(i, src, mask):
        value_t[...] = kv[i].T[HEAD_SIZE:]

        def head(h, at):
            s = dot(kv[i], q[h], NT)
            if mask:
                s = masked(s, src, positions(info), start[...])
            old = rows[h]
            top = jnp.maximum(old, jnp.max(s, axis=0, keepdims=True))
            p = jnp.exp(s - top)
            fade = jnp.exp(old - top)
            rows[h] = top
            rows[4 + h] = rows[4 + h] * fade + jnp.sum(p, axis=0, keepdims=True)
            acc[at] = acc[at] * fade + dot(value_t[...], p.astype(bf16))

        for_heads(head)

    on_blocks(info, offsets, block)


def fwd_scratch(n):
    return [pltpu.VMEM((n, TOKENS, 128), bf16), pltpu.VMEM((HEAD_SIZE, TOKENS), bf16)]


def fwd_kernel(offsets, info, q, start, *refs):
    n = len(offsets)
    kvs, refs = refs[:n], refs[n:]
    if offsets[0] == 0:
        rows, acc, *scratch = refs
        rows[0:4] = jnp.full((4, 1, TOKENS), TOP_START, f32)
        rows[4:8] = jnp.zeros((4, 1, TOKENS), f32)
        acc[...] = jnp.zeros(acc.shape, f32)
    else:
        rows_in, acc_in, rows, acc, *scratch = refs
        rows[...] = rows_in[...]
        acc[...] = acc_in[...]
    fwd_blocks(info, offsets, q, kvs, start, rows, acc, *scratch)


def out_block(ref):
    return jnp.concatenate([ref[TOKENS : TOKENS + ROWS], ref[TOKENS + ROWS :]], axis=1)


def mid_kernel(info, place, q, start, kv, rows_in, acc_in, *refs):
    parts, blocks, refs = refs[:SIDE], refs[SIDE : SIDE + PLANES], refs[SIDE + PLANES :]
    mixed_t, d_out, back_rows, w_out = refs[:4]
    grads, (rows, acc, cot, *scratch) = refs[4 : 4 + PLANES], refs[4 + PLANES :]
    rows[...] = rows_in[...]
    acc[...] = acc_in[...]
    fwd_blocks(info, (-4,), q, (kv,), start, rows, acc, *scratch)
    for k in range(SIDE):
        at = pl.multiple_of((place[1] ^ k) * 128, 128)
        cot[pl.ds(at, 128)] = parts[k][...]
    for o in range(PLANES):
        at = pl.multiple_of(plane_at(info, o) * ROWS, ROWS)
        w_out[pl.ds(at, ROWS)] = out_block(blocks[o])
    d_mixed = dot(cot[...], w_out[...]).astype(bf16).astype(f32)
    inverse = jnp.concatenate([1.0 / rows[4 + h] for h in range(REPEAT)], axis=0)
    back_rows[0:4] = rows[0:4]
    for h in range(REPEAT):
        at = slice(64 * h, 64 * h + 64)
        mixed_t[at] = (acc[at] * inverse[h : h + 1]).astype(bf16)
    mt = mixed_t[...]
    prod = d_mixed.T * mt.astype(f32)
    for h in range(REPEAT):
        back_rows[4 + h] = inverse[h : h + 1] * jnp.sum(
            prod[64 * h : 64 * h + 64], axis=0, keepdims=True
        )
    by_row = jnp.concatenate([inverse, inverse], axis=0).T
    high = lanes((TOKENS, 128)) >= HEAD_SIZE
    for pair in range(2):
        u = d_mixed[:, 128 * pair : 128 * pair + 128]
        scale = [by_row[:, 2 * pair + i : 2 * pair + i + 1] for i in range(2)]
        u = u * jnp.where(high, scale[1], scale[0])
        d_out[2 * pair] = jnp.where(high, pltpu.roll(u, 64, 1), 0.0).astype(bf16)
        d_out[2 * pair + 1] = jnp.where(high, u, 0.0).astype(bf16)
    for o in range(PLANES):
        at = pl.multiple_of(plane_at(info, o) * ROWS, ROWS)
        term = dot(mt, cot[:, pl.ds(at, ROWS)]).astype(bf16)
        grads[o][:ROWS] = term[:, :128]
        grads[o][ROWS:] = term[:, 128:]


def attn_kernel(place, mixed_t, w_out, kept, sent, mixed):
    mixed[...] = mixed_t[...].astype(f32).T
    for k in range(SIDE):
        at = pl.multiple_of((place[1] ^ k) * 128, 128)
        out = sent if k % 2 else kept
        out[k // 2] = dot(mixed[pl.ds(at, 128)].astype(bf16), w_out[...], NT).astype(bf16)


def cores_kernel(a, b, own, across):
    own[...] = (a[0].astype(f32) + b[0].astype(f32)).astype(bf16)
    across[...] = (a[1].astype(f32) + b[1].astype(f32)).astype(bf16)


def bwd_blocks(info, offsets, q, d_out, rows, kvs, start, acc, sums, kv, key_t):
    for i, ref in enumerate(kvs):
        kv[i] = ref[:TOKENS]
        sums[i] = jnp.zeros((TOKENS, 128), f32)

    def block(i, src, mask):
        key_t[...] = kv[i].T[:HEAD_SIZE]

        def head(h, at):
            s = dot(kv[i], q[h], NT)
            if mask:
                s = masked(s, src, positions(info), start[...])
            p = jnp.exp(s - rows[h])
            dp = dot(kv[i], d_out[h], NT)
            ds = (p * (dp - rows[4 + h])).astype(bf16)
            sums[i] = sums[i] + (dot(p.astype(bf16), d_out[h]) + dot(ds, q[h]))
            acc[at] = acc[at] + dot(key_t[...], ds)

        for_heads(head)

    on_blocks(info, offsets, block)


def bwd_scratch(n):
    return [pltpu.VMEM((n, TOKENS, 128), f32)] + fwd_scratch(n)


def bwd_kernel(offsets, info, q, d_out, rows, start, *refs):
    n = len(offsets)
    kvs, wo_terms, refs, scratch = refs[:n], refs[n : 2 * n], refs[2 * n : -3], refs[-3:]
    acc, outs = refs[-n - 1], refs[-n:]
    acc[...] = refs[0][...] if len(refs) > n + 1 else jnp.zeros(acc.shape, f32)
    bwd_blocks(info, offsets, q, d_out, rows, kvs, start, acc, *scratch)
    for i in range(n):
        outs[i][:TOKENS] = scratch[0][i].astype(bf16)
        outs[i][TOKENS:] = wo_terms[i][...]


def turn_back(u, c, s, out, at, scale):
    one, two = u[:32], u[32:]
    out[at : at + 32] = ((one * c + two * s) * scale).astype(bf16)
    out[at + 32 : at + 64] = ((two * c - one * s) * scale).astype(bf16)


def own_kernel(
    info, q, d_out, rows, start, kv, acc_in, cos_t, sin_t, normed,
    out, grads, acc, d_t, *scratch,
):
    acc[...] = acc_in[...]
    bwd_blocks(info, (0,), q, d_out, rows, (kv,), start, acc, *scratch)
    out[...] = scratch[0][0]
    c, s = cos_t[...], sin_t[...]
    for h in range(REPEAT):
        turn_back(acc[64 * h : 64 * h + 64], c, s, d_t, 64 * h, 1.0 / math.sqrt(HEAD_SIZE))
    for o in range(PLANES):
        at = pl.multiple_of(plane_at(info, o) * ROWS, ROWS)
        grads[o] = dot(d_t[...], normed[:, pl.ds(at, ROWS)]).astype(bf16)


def last_kernel(info, own, wo_own, got_a, got_b, cos_t, sin_t, normed, q_grads, *refs):
    wo_sum, grads, d_t = refs[0], refs[1 : 1 + PLANES], refs[1 + PLANES]
    got = got_a[...].astype(f32) + got_b[...].astype(f32)
    kv_t = (got[:TOKENS] + own[...]).T
    wo_sum[...] = got[TOKENS:] + wo_own[...].astype(f32)
    turn_back(kv_t[:64], cos_t[...], sin_t[...], d_t, 0, 1.0)
    d_t[64:128] = kv_t[64:].astype(bf16)
    for o in range(PLANES):
        at = pl.multiple_of(plane_at(info, o) * ROWS, ROWS)
        grads[o][:WO] = q_grads[o]
        grads[o][WO:] = dot(d_t[...], normed[:, pl.ds(at, ROWS)]).astype(bf16)


def on_device(hidden, gain, weights, momentum, cotangent, segment, distance):
    rank = lax.axis_index("fsdp")
    plane, own = rank // SIDE, rank % SIDE
    old_w, old_m = weights[0], momentum[0]
    place = jnp.stack([plane, own]).astype(jnp.int32)

    tie = lax.optimization_barrier

    half = HEAD_SIZE // 2
    tokens = plane * TOKENS + jnp.arange(TOKENS, dtype=jnp.int32)
    freq = jnp.power(THETA, -jnp.arange(half, dtype=f32) * 2.0 / HEAD_SIZE)
    angle = tokens.astype(f32)[:, None] * freq[None, :]
    cosine, sine = jnp.cos(angle), jnp.sin(angle)
    cos_rows = jnp.concatenate([cosine] * 4, axis=1)
    sin_rows = jnp.concatenate([-sine, sine] * 2, axis=1)
    cos_t, sin_t = cosine.T, sine.T

    normed, rounded, *sent = call(
        prep_kernel,
        (shape(128, 2048), shape(*old_w.shape)) + (shape(80, QKV + WO),) * SIDE,
        (place, hidden[0], gain, old_w, segment),
        scratch=[
            pltpu.VMEM((SIDE, 80, QKV + WO), bf16),
            pltpu.VMEM((128, 2048), bf16),
            pltpu.VMEM(gain.shape, f32),
            pltpu.VMEM(old_w.shape, f32),
            pltpu.VMEM(segment.shape, jnp.int32),
            pltpu.SemaphoreType.DMA((4,)),
        ],
        space=pl.ANY,
        mib=60,
    )
    got = [sent[0]] + [beside(sent[k], k) for k in range(1, SIDE)]
    w_rows, wo_rows = call(join_kernel, (shape(ROWS + 16, QKV), shape(ROWS, WO)), (place, *got))
    w_rows, cos_rows, sin_rows, cos_t, sin_t = tie((w_rows, cos_rows, sin_rows, cos_t, sin_t))
    w_qkv, across = ring_gather(w_rows, beside(normed, 2))
    parts = [normed, beside(normed, 1), across, beside(across, 1)]

    groups = lax.axis_size("group")
    bits = groups.bit_length() - 1
    bit = jnp.remainder(distance, bits).astype(jnp.int32)

    def swap(b, x):
        return lax.ppermute(x, "group", [(i, i ^ 1 << b) for i in range(groups)])


    state_shape = (shape(8, 1, TOKENS, dtype=f32), shape(256, TOKENS, dtype=f32))
    head_shape = shape(REPEAT, TOKENS, 128)
    sent_shape = shape(2 * TOKENS, 128)
    score = 2 * REPEAT * TOKENS * TOKENS * 128

    normed, q, kv, start, info = call(
        proj_kernel,
        (shape(TOKENS, 2048), head_shape, sent_shape, shape(1, TOKENS, dtype=jnp.int32), INFO),
        (place, cos_rows, sin_rows, wo_rows, *parts, *w_qkv),
        (2 * TOKENS * 2048 * QKV, 8 << 20, 0),
    )

    kvs, _ = ring_gather(kv)
    cot, _ = lax.optimization_barrier((cotangent[0], q))
    across = beside(cot, 2)
    cots = [cot, beside(cot, 1), across, beside(across, 1)]
    cots[0], *partners = tie((cots[0], *[swap(b, rounded) for b in range(bits)]))
    state = call(
        functools.partial(fwd_kernel, (0,)),
        state_shape,
        (info, q, start, kvs[0]),
        (2 * score, 2 << 20, 1 << 20),
        scratch=fwd_scratch(1),
    )
    for offsets in ((-1, 1), (-2, 2), (-3, 3)):
        state = call(
            functools.partial(fwd_kernel, offsets),
            state_shape,
            (info, q, start, *[kvs[o % PLANES] for o in offsets], *state),
            (4 * score, 2 << 20, 2 << 20),
            scratch=fwd_scratch(2),
            alias={5: 0, 6: 1},
        )

    mixed_t, d_out, back_rows, w_out, *wo_grads = call(
        mid_kernel,
        (shape(256, TOKENS), head_shape, state_shape[0], shape(2048, WO))
        + (shape(TOKENS, 128),) * PLANES,
        (info, place, q, start, kvs[4], *state, *cots, *kvs),
        (2 * score + 4 * TOKENS * 2048 * WO, 8 << 20, 1 << 20),
        scalars=2,
        scratch=[pltpu.VMEM((8, 1, TOKENS), f32), pltpu.VMEM((256, TOKENS), f32)]
        + [pltpu.VMEM((TOKENS, 2048), bf16)]
        + fwd_scratch(1),
        mib=16,
    )

    common = (info, q, d_out, back_rows, start)

    def back_step(offsets, acc):
        n = len(offsets)
        args = common + tuple(x[o % PLANES] for x in (kvs, wo_grads) for o in offsets)
        return call(
            functools.partial(bwd_kernel, offsets),
            (state_shape[1],) + (sent_shape,) * n,
            args if acc is None else args + (acc,),
            (5 * n * score, 3 << 20, n << 20),
            scratch=bwd_scratch(n),
            alias=None if acc is None else {len(args): 0},
        )

    acc, down, up = back_step((-4, 3), None)
    kept, sent = call(
        attn_kernel,
        (shape(2, TOKENS // SIDE, 2048),) * 2,
        (place, mixed_t, w_out),
        (2 * TOKENS * 2048 * WO, 4 << 20, 0),
        scratch=[pltpu.VMEM((TOKENS, WO), f32)],
    )
    acc, kept = tie((acc, kept))
    token_block = shape(TOKENS // SIDE, 2048)
    attn, across = call(cores_kernel, (token_block,) * 2, (kept, beside(sent, 1)), scalars=0)
    down, up = along(down, -1), along(up, 1)
    for offsets in ((-3, 2), (-2, 1)):
        acc, *terms = back_step(offsets, acc)
        down, up = add(down, terms[0]), add(up, terms[1])
        acc, _, _, across = tie((acc, down, up, across))
        down, up = along(down, -1), along(up, 1)
    across = beside(across, 2)
    acc, term = back_step((-1,), acc)
    down = add(down, term)
    acc, _ = tie((acc, down))
    down = along(down, -1)
    own_kv, q_grads = call(
        own_kernel,
        (shape(TOKENS, 128, dtype=f32), shape(PLANES, WO, ROWS)),
        (*common, kvs[0], acc, cos_t, sin_t, normed),
        (5 * score + 2 * TOKENS * 2048 * WO, 5 << 20, 1 << 20),
        scratch=[pltpu.VMEM((256, TOKENS), f32), pltpu.VMEM((WO, TOKENS), bf16)] + bwd_scratch(1),
    )
    attn = add(attn, across)
    own_kv, attn = tie((own_kv, attn))
    wo_sum, *grads = call(
        last_kernel,
        (shape(TOKENS, 128, dtype=f32),) + (shape(QKV, ROWS),) * PLANES,
        (info, own_kv, wo_grads[0], down, up, cos_t, sin_t, normed, q_grads),
        (2 * TOKENS * 2048 * 128, 6 << 20, 0),
        scratch=[pltpu.VMEM((128, TOKENS), bf16)],
    )
    down, up = ring_scatter(grads)
    sent = call(
        split_kernel,
        (shape(64, QKV + WO),) * SIDE,
        (place, down, up, grads[0], wo_sum),
        scratch=[pltpu.VMEM((ROWS, QKV + WO), f32)],
    )
    got = [sent[0]] + [beside(sent[k], k) for k in range(1, SIDE)]
    whole = shape(*old_w.shape, dtype=f32)
    new_m, sent = call(
        step_kernel,
        (whole, shape(*old_w.shape)),
        (place, old_m, *got),
        scratch=[pltpu.VMEM((SIDE, 64, QKV + WO), bf16)],
    )
    other = lax.switch(bit[0], [functools.partial(swap, b) for b in range(bits)], sent)
    out_w, out_m = call(mean_kernel, (whole, whole), (bit, old_w, new_m, other, *partners))
    return (attn[None], out_w[None], out_m[None])


def solution(mesh):
    return jax.shard_map(
        on_device,
        mesh=mesh,
        in_specs=(
            P("group", "fsdp", None),
            P("group", None),
            P("group", "fsdp", None),
            P("group", "fsdp", None),
            P("group", "fsdp", None),
            P("group", "fsdp"),
            P(),
        ),
        out_specs=(P("group", "fsdp", None), P("group", "fsdp", None), P("group", "fsdp", None)),
        check_vma=False,
    )
```

```python
import functools
import math

import jax
import jax.numpy as jnp
from jax import lax
from jax.experimental import pallas as pl
from jax.experimental.pallas import tpu as pltpu
from jax.sharding import PartitionSpec as P

QUERY_HEADS = 16
KEY_VALUE_HEADS = 4
HEAD_SIZE = 64
REPEAT = QUERY_HEADS // KEY_VALUE_HEADS

EPS = 1e-05
BETA = 0.9
RATE = 0.01
THETA = 500000.0
MASK_FILL = -1e30
TOP_START = -1e20

PLANES = 8
SIDE = 4
TOKENS = 512
ROWS = 256
QKV = 384
WO = 256
NT = (((1,), (1,)), ((), ()))
NN = (((1,), (0,)), ((), ()))

f32 = jnp.float32
bf16 = jnp.bfloat16


def dot(a, b, dims=NN):
    return lax.dot_general(a, b, dims, preferred_element_type=f32)


def along(x, step):
    n = PLANES * SIDE
    return lax.ppermute(x, "fsdp", [(i, (i + SIDE * step) % n) for i in range(n)])


def beside(x, mask):
    return lax.ppermute(x, "fsdp", [(i, i ^ mask) for i in range(PLANES * SIDE)])


def ring_gather(x, second=None, first=None):
    got = [None] * PLANES
    got[0] = x
    down = up = x
    for s in range(1, PLANES // 2 + 1):
        down = along(down, 1)
        if s < PLANES // 2:
            up = along(up, -1)
            if s == 2 and second is not None:
                up, second = lax.optimization_barrier((up, second))
            if s == 1 and first is not None:
                down, up, first = lax.optimization_barrier((down, up, first))
            got[s] = up
        got[-s % PLANES] = down
    return got, second, first


def call(kernel, outs, args, cost=(1 << 20, 1 << 20, 0), scalars=1, scratch=(), alias=None, mib=8, space=pltpu.VMEM):
    flops, bytes_, exps = cost
    vmem, smem = (pl.BlockSpec(memory_space=m) for m in (pltpu.VMEM, pltpu.SMEM))
    return pl.pallas_call(
        kernel,
        out_shape=tuple(outs),
        in_specs=[smem] * scalars + [pl.BlockSpec(memory_space=space)] * (len(args) - scalars),
        out_specs=tuple(smem if o.shape == INFO.shape else vmem for o in outs),
        scratch_shapes=scratch,
        input_output_aliases=alias or {},
        compiler_params=pltpu.CompilerParams(vmem_limit_bytes=mib * 1024 * 1024),
        cost_estimate=pl.CostEstimate(flops=flops, bytes_accessed=bytes_, transcendentals=exps),
    )(*args)


def shape(*dims, dtype=bf16):
    return jax.ShapeDtypeStruct(dims, dtype)


INFO = shape(3, dtype=jnp.int32)


def add(got, term):
    return call(sum_kernel, (shape(*term.shape),), (got, term), scalars=0, mib=4)[0]


def ring_scatter(terms):
    down, up = along(terms[4], -1), along(terms[3], 1)
    for s in (2, 1):
        down, up = along(add(down, terms[-s - 1]), -1), along(add(up, terms[s]), 1)
    return along(add(down, terms[-1]), -1), up


def prep_kernel(place, *refs):
    sources, normed, rounded, refs = refs[:4], refs[4], refs[5], refs[6:]
    outs, sent, sems = refs[:SIDE], refs[SIDE], refs[-1]
    hidden, gain, weights, seg = refs[SIDE + 1 : SIDE + 5]
    copies = [
        pltpu.make_async_copy(source, to, sems.at[i])
        for i, (source, to) in enumerate(zip(sources, (hidden, gain, weights, seg)))
    ]
    for c in copies:
        c.start()
    for c in copies:
        c.wait()
    rounded[...] = weights[...].astype(bf16)
    x = hidden[...].astype(f32)
    scale = lax.rsqrt(jnp.mean(x * x, axis=1, keepdims=True) + EPS)
    normed[...] = (x * scale * gain[...]).astype(bf16)
    documents = seg[...]
    first, second = (jnp.sum((documents == d).astype(f32)) for d in range(2))
    lane = lanes((16, QKV + WO))
    counts = jnp.where(lane == 0, first, jnp.where(lane == 1, second, 0.0)).astype(bf16)
    for j in range(SIDE):
        cuts = [(256 * j, 256), (1024 + 64 * j, 64), (1280 + 64 * j, 64), (1536 + 256 * j, 256)]
        block = jnp.concatenate([weights[:, at : at + n] for at, n in cuts], axis=1)
        sent[j, :64] = block.astype(bf16)
        sent[j, 64:] = counts
    for k in range(SIDE):
        outs[k][...] = sent[place[1] ^ k]


def join_kernel(place, *refs):
    got, (w_rows, wo_rows) = refs[:SIDE], refs[SIDE:]
    row = lax.broadcasted_iota(jnp.int32, (16, QKV), 0)
    tail = jnp.zeros((16, QKV), f32)
    for k in range(SIDE):
        at = pl.multiple_of((place[1] ^ k) * 64, 64)
        w_rows[pl.ds(at, 64)] = got[k][:64, :QKV]
        wo_rows[pl.ds(at, 64)] = got[k][:64, QKV:]
        tail = jnp.where(row == k, got[k][64:, :QKV].astype(f32), tail)
    w_rows[ROWS:] = tail.astype(bf16)


def sum_kernel(*refs):
    refs[-1][...] = sum(r[...].astype(f32) for r in refs[:-1]).astype(bf16)


def split_kernel(place, down, up, own, wo_sum, *refs):
    outs, total = refs[:SIDE], refs[SIDE]
    qkv = down[...].astype(f32) + up[...].astype(f32) + own[...].astype(f32)
    total[:, :QKV] = qkv.T
    total[:, QKV:] = jnp.concatenate([wo_sum[:ROWS], wo_sum[ROWS:]], axis=1).T
    for k in range(SIDE):
        at = pl.multiple_of((place[1] ^ k) * 64, 64)
        outs[k][...] = total[pl.ds(at, 64)].astype(bf16)


def step_kernel(place, momentum, *refs):
    got, (new_m, sent, by_head) = refs[:SIDE], refs[SIDE:]
    for k in range(SIDE):
        by_head[place[1] ^ k] = got[k][...]
    for lo, n, to in ((0, 256, 0), (256, 64, 1024), (320, 64, 1280), (384, 256, 1536)):
        grad = jnp.concatenate([by_head[j, :, lo : lo + n] for j in range(SIDE)], axis=1)
        at = slice(to, to + SIDE * n)
        m = BETA * momentum[:, at] + grad.astype(f32)
        new_m[:, at] = m
        sent[:, at] = m.astype(bf16)


def mean_kernel(w, m, other, partner, out_w, out_m):
    mean_m = 0.5 * (m[...] + other[...].astype(f32))
    out_m[...] = mean_m
    out_w[...] = 0.5 * (w[...] + partner[...].astype(f32)) - RATE * mean_m


def plane_at(info, offset):
    return lax.rem(info[0] + (offset % PLANES), PLANES)


def lanes(shape):
    return lax.broadcasted_iota(jnp.int32, shape, len(shape) - 1)


def proj_kernel(place, cos, sin, wo_rows, *refs):
    parts, blocks = refs[:SIDE], refs[SIDE : SIDE + PLANES]
    normed, q_out, kv_out, start, info = refs[SIDE + PLANES :]
    for k in range(SIDE):
        at = pl.multiple_of((place[1] ^ k) * 128, 128)
        normed[pl.ds(at, 128)] = parts[k][...]
    total = jnp.zeros((TOKENS, QKV), f32)
    for o in range(PLANES):
        at = pl.multiple_of(plane_at(place, o) * ROWS, ROWS)
        total = total + dot(normed[:, pl.ds(at, ROWS)], blocks[o][:ROWS])

    tails = sum(b[ROWS : ROWS + 16].astype(f32)[:SIDE, :128] for b in blocks)
    lane = lanes(tails.shape)
    second = jnp.sum(jnp.where(lane == 0, tails, 0.0)).astype(jnp.int32)
    third = second + jnp.sum(jnp.where(lane == 1, tails, 0.0)).astype(jnp.int32)

    def start_of(t):
        return jnp.where(t >= third, third, jnp.where(t >= second, second, 0))

    start[...] = start_of(positions(place))
    info[0] = place[0]
    info[1] = start_of(place[0] * TOKENS)
    info[2] = start_of(place[0] * TOKENS + TOKENS - 1)

    lane = lanes((TOKENS, 128))
    first = lax.rem(lane, HEAD_SIZE) < HEAD_SIZE // 2
    low = lane < HEAD_SIZE
    c, s = cos[...], sin[...]

    def turned(u):
        return jnp.where(first, pltpu.roll(u, 96, 1), pltpu.roll(u, 32, 1))

    for pair in range(2):
        u = total[:, 128 * pair : 128 * pair + 128]
        u = (u * c + turned(u) * s) * (1.0 / math.sqrt(HEAD_SIZE))
        q_out[2 * pair] = jnp.where(low, u, 0.0).astype(bf16)
        q_out[2 * pair + 1] = jnp.where(low, pltpu.roll(u, 64, 1), 0.0).astype(bf16)
    u = total[:, 256:]
    kv_out[:TOKENS] = jnp.where(low, u * c + turned(u) * s, u).astype(bf16)
    kv_out[TOKENS : TOKENS + ROWS] = wo_rows[:, :128]
    kv_out[TOKENS + ROWS :] = wo_rows[:, 128:]


def masked(s, src, qpos, start):
    kpos = src * TOKENS + lax.broadcasted_iota(jnp.int32, (TOKENS, TOKENS), 0)
    return jnp.where((kpos <= qpos) & (kpos >= start), s, MASK_FILL)


def on_blocks(info, offsets, body):
    def step(i, carry):
        src = plane_at(info, offsets[0])
        for n, o in enumerate(offsets[1:], 1):
            src = jnp.where(i == n, plane_at(info, o), src)
        base = src * TOKENS
        seen = (src <= info[0]) & (base + TOKENS > info[1])
        edge = (src == info[0]) | (base < info[2])

        @pl.when(seen & edge)
        def _():
            body(i, src, True)

        if offsets != (0,):

            @pl.when(seen & jnp.logical_not(edge))
            def _():
                body(i, src, False)

        return carry

    lax.fori_loop(0, len(offsets), step, 0)


def for_heads(body):
    def step(h, carry):
        body(h, pl.ds(pl.multiple_of(h * HEAD_SIZE, HEAD_SIZE), HEAD_SIZE))
        return carry

    lax.fori_loop(0, REPEAT, step, 0)


def positions(info):
    return info[0] * TOKENS + lax.broadcasted_iota(jnp.int32, (1, TOKENS), 1)


def fwd_blocks(info, offsets, q, kvs, start, rows, acc, kv, value_t):
    for i, ref in enumerate(kvs):
        kv[i] = ref[:TOKENS]

    def block(i, src, mask):
        value_t[...] = kv[i].T[HEAD_SIZE:]

        def head(h, at):
            s = dot(kv[i], q[h], NT)
            if mask:
                s = masked(s, src, positions(info), start[...])
            old = rows[h]
            top = jnp.maximum(old, jnp.max(s, axis=0, keepdims=True))
            p = jnp.exp(s - top)
            fade = jnp.exp(old - top)
            rows[h] = top
            rows[4 + h] = rows[4 + h] * fade + jnp.sum(p, axis=0, keepdims=True)
            acc[at] = acc[at] * fade + dot(value_t[...], p.astype(bf16))

        for_heads(head)

    on_blocks(info, offsets, block)


def fwd_scratch(n):
    return [pltpu.VMEM((n, TOKENS, 128), bf16), pltpu.VMEM((HEAD_SIZE, TOKENS), bf16)]


def fwd_kernel(offsets, info, q, start, *refs):
    n = len(offsets)
    kvs, refs = refs[:n], refs[n:]
    if offsets[0] == 0:
        rows, acc, *scratch = refs
        rows[0:4] = jnp.full((4, 1, TOKENS), TOP_START, f32)
        rows[4:8] = jnp.zeros((4, 1, TOKENS), f32)
        acc[...] = jnp.zeros(acc.shape, f32)
    else:
        rows_in, acc_in, rows, acc, *scratch = refs
        rows[...] = rows_in[...]
        acc[...] = acc_in[...]
    fwd_blocks(info, offsets, q, kvs, start, rows, acc, *scratch)


def out_block(ref):
    return jnp.concatenate([ref[TOKENS : TOKENS + ROWS], ref[TOKENS + ROWS :]], axis=1)


def mid_kernel(info, place, q, start, kv, rows_in, acc_in, *refs):
    parts, blocks, refs = refs[:SIDE], refs[SIDE : SIDE + PLANES], refs[SIDE + PLANES :]
    mixed_t, d_out, back_rows, w_out = refs[:4]
    grads, (rows, acc, cot, *scratch) = refs[4 : 4 + PLANES], refs[4 + PLANES :]
    rows[...] = rows_in[...]
    acc[...] = acc_in[...]
    fwd_blocks(info, (-4,), q, (kv,), start, rows, acc, *scratch)
    for k in range(SIDE):
        at = pl.multiple_of((place[1] ^ k) * 128, 128)
        cot[pl.ds(at, 128)] = parts[k][...]
    for o in range(PLANES):
        at = pl.multiple_of(plane_at(info, o) * ROWS, ROWS)
        w_out[pl.ds(at, ROWS)] = out_block(blocks[o])
    d_mixed = dot(cot[...], w_out[...]).astype(bf16).astype(f32)
    inverse = jnp.concatenate([1.0 / rows[4 + h] for h in range(REPEAT)], axis=0)
    back_rows[0:4] = rows[0:4]
    for h in range(REPEAT):
        at = slice(64 * h, 64 * h + 64)
        mixed_t[at] = (acc[at] * inverse[h : h + 1]).astype(bf16)
    mt = mixed_t[...]
    prod = d_mixed.T * mt.astype(f32)
    for h in range(REPEAT):
        back_rows[4 + h] = inverse[h : h + 1] * jnp.sum(
            prod[64 * h : 64 * h + 64], axis=0, keepdims=True
        )
    by_row = jnp.concatenate([inverse, inverse], axis=0).T
    high = lanes((TOKENS, 128)) >= HEAD_SIZE
    for pair in range(2):
        u = d_mixed[:, 128 * pair : 128 * pair + 128]
        scale = [by_row[:, 2 * pair + i : 2 * pair + i + 1] for i in range(2)]
        u = u * jnp.where(high, scale[1], scale[0])
        d_out[2 * pair] = jnp.where(high, pltpu.roll(u, 64, 1), 0.0).astype(bf16)
        d_out[2 * pair + 1] = jnp.where(high, u, 0.0).astype(bf16)
    for o in range(PLANES):
        at = pl.multiple_of(plane_at(info, o) * ROWS, ROWS)
        term = dot(mt, cot[:, pl.ds(at, ROWS)]).astype(bf16)
        grads[o][:ROWS] = term[:, :128]
        grads[o][ROWS:] = term[:, 128:]


def attn_kernel(place, mixed_t, w_out, kept, sent, mixed):
    mixed[...] = mixed_t[...].astype(f32).T
    for k in range(SIDE):
        at = pl.multiple_of((place[1] ^ k) * 128, 128)
        out = sent if k % 2 else kept
        out[k // 2] = dot(mixed[pl.ds(at, 128)].astype(bf16), w_out[...], NT).astype(bf16)


def cores_kernel(a, b, own, across):
    own[...] = (a[0].astype(f32) + b[0].astype(f32)).astype(bf16)
    across[...] = (a[1].astype(f32) + b[1].astype(f32)).astype(bf16)


def bwd_blocks(info, offsets, q, d_out, rows, kvs, start, acc, sums, kv, key_t):
    for i, ref in enumerate(kvs):
        kv[i] = ref[:TOKENS]
        sums[i] = jnp.zeros((TOKENS, 128), f32)

    def block(i, src, mask):
        key_t[...] = kv[i].T[:HEAD_SIZE]

        def head(h, at):
            s = dot(kv[i], q[h], NT)
            if mask:
                s = masked(s, src, positions(info), start[...])
            p = jnp.exp(s - rows[h])
            dp = dot(kv[i], d_out[h], NT)
            ds = (p * (dp - rows[4 + h])).astype(bf16)
            sums[i] = sums[i] + (dot(p.astype(bf16), d_out[h]) + dot(ds, q[h]))
            acc[at] = acc[at] + dot(key_t[...], ds)

        for_heads(head)

    on_blocks(info, offsets, block)


def bwd_scratch(n):
    return [pltpu.VMEM((n, TOKENS, 128), f32)] + fwd_scratch(n)


def bwd_kernel(offsets, info, q, d_out, rows, start, *refs):
    n = len(offsets)
    kvs, wo_terms, refs, scratch = refs[:n], refs[n : 2 * n], refs[2 * n : -3], refs[-3:]
    acc, outs = refs[-n - 1], refs[-n:]
    acc[...] = refs[0][...] if len(refs) > n + 1 else jnp.zeros(acc.shape, f32)
    bwd_blocks(info, offsets, q, d_out, rows, kvs, start, acc, *scratch)
    for i in range(n):
        outs[i][:TOKENS] = scratch[0][i].astype(bf16)
        outs[i][TOKENS:] = wo_terms[i][...]


def turn_back(u, c, s, out, at, scale):
    one, two = u[:32], u[32:]
    out[at : at + 32] = ((one * c + two * s) * scale).astype(bf16)
    out[at + 32 : at + 64] = ((two * c - one * s) * scale).astype(bf16)


def own_kernel(
    info, q, d_out, rows, start, kv, acc_in, cos_t, sin_t, normed,
    out, grads, acc, d_t, *scratch,
):
    acc[...] = acc_in[...]
    bwd_blocks(info, (0,), q, d_out, rows, (kv,), start, acc, *scratch)
    out[...] = scratch[0][0]
    c, s = cos_t[...], sin_t[...]
    for h in range(REPEAT):
        turn_back(acc[64 * h : 64 * h + 64], c, s, d_t, 64 * h, 1.0 / math.sqrt(HEAD_SIZE))
    for o in range(PLANES):
        at = pl.multiple_of(plane_at(info, o) * ROWS, ROWS)
        grads[o] = dot(d_t[...], normed[:, pl.ds(at, ROWS)]).astype(bf16)


def last_kernel(info, own, wo_own, got_a, got_b, cos_t, sin_t, normed, q_grads, *refs):
    wo_sum, grads, d_t = refs[0], refs[1 : 1 + PLANES], refs[1 + PLANES]
    got = got_a[...].astype(f32) + got_b[...].astype(f32)
    kv_t = (got[:TOKENS] + own[...]).T
    wo_sum[...] = got[TOKENS:] + wo_own[...].astype(f32)
    turn_back(kv_t[:64], cos_t[...], sin_t[...], d_t, 0, 1.0)
    d_t[64:128] = kv_t[64:].astype(bf16)
    for o in range(PLANES):
        at = pl.multiple_of(plane_at(info, o) * ROWS, ROWS)
        grads[o][:WO] = q_grads[o]
        grads[o][WO:] = dot(d_t[...], normed[:, pl.ds(at, ROWS)]).astype(bf16)


def on_device(hidden, gain, weights, momentum, cotangent, segment, distance):
    rank = lax.axis_index("fsdp")
    plane, own = rank // SIDE, rank % SIDE
    old_w, old_m = weights[0], momentum[0]
    place = jnp.stack([plane, own]).astype(jnp.int32)

    tie = lax.optimization_barrier

    half = HEAD_SIZE // 2
    tokens = plane * TOKENS + jnp.arange(TOKENS, dtype=jnp.int32)
    freq = jnp.power(THETA, -jnp.arange(half, dtype=f32) * 2.0 / HEAD_SIZE)
    angle = tokens.astype(f32)[:, None] * freq[None, :]
    cosine, sine = jnp.cos(angle), jnp.sin(angle)
    cos_rows = jnp.concatenate([cosine] * 4, axis=1)
    sin_rows = jnp.concatenate([-sine, sine] * 2, axis=1)
    cos_t, sin_t = cosine.T, sine.T

    normed, rounded, *sent = call(
        prep_kernel,
        (shape(128, 2048), shape(*old_w.shape)) + (shape(80, QKV + WO),) * SIDE,
        (place, hidden[0], gain, old_w, segment),
        scratch=[
            pltpu.VMEM((SIDE, 80, QKV + WO), bf16),
            pltpu.VMEM((128, 2048), bf16),
            pltpu.VMEM(gain.shape, f32),
            pltpu.VMEM(old_w.shape, f32),
            pltpu.VMEM(segment.shape, jnp.int32),
            pltpu.SemaphoreType.DMA((4,)),
        ],
        space=pl.ANY,
        mib=60,
    )
    got = [sent[0]] + [beside(sent[k], k) for k in range(1, SIDE)]
    w_rows, wo_rows = call(join_kernel, (shape(ROWS + 16, QKV), shape(ROWS, WO)), (place, *got))
    w_rows, cos_rows, sin_rows, cos_t, sin_t = tie((w_rows, cos_rows, sin_rows, cos_t, sin_t))

    groups = lax.axis_size("group")
    bits = groups.bit_length() - 1
    bit = jnp.remainder(distance[0], bits)

    def swap(x):
        def by(b):
            return lambda x: lax.ppermute(x, "group", [(i, i ^ 1 << b) for i in range(groups)])

        return lax.switch(bit, [by(b) for b in range(bits)], x)

    rounded, _ = tie((rounded, w_rows))
    w_qkv, across, partner = ring_gather(w_rows, beside(normed, 2), swap(rounded))
    parts = [normed, beside(normed, 1), across, beside(across, 1)]

    state_shape = (shape(8, 1, TOKENS, dtype=f32), shape(256, TOKENS, dtype=f32))
    head_shape = shape(REPEAT, TOKENS, 128)
    sent_shape = shape(2 * TOKENS, 128)
    score = 2 * REPEAT * TOKENS * TOKENS * 128

    normed, q, kv, start, info = call(
        proj_kernel,
        (shape(TOKENS, 2048), head_shape, sent_shape, shape(1, TOKENS, dtype=jnp.int32), INFO),
        (place, cos_rows, sin_rows, wo_rows, *parts, *w_qkv),
        (2 * TOKENS * 2048 * QKV, 8 << 20, 0),
    )

    kvs, *_ = ring_gather(kv)
    cot, _ = lax.optimization_barrier((cotangent[0], q))
    across = beside(cot, 2)
    cots = [cot, beside(cot, 1), across, beside(across, 1)]
    state = call(
        functools.partial(fwd_kernel, (0,)),
        state_shape,
        (info, q, start, kvs[0]),
        (2 * score, 2 << 20, 1 << 20),
        scratch=fwd_scratch(1),
    )
    for offsets in ((-1, 1), (-2, 2), (-3, 3)):
        state = call(
            functools.partial(fwd_kernel, offsets),
            state_shape,
            (info, q, start, *[kvs[o % PLANES] for o in offsets], *state),
            (4 * score, 2 << 20, 2 << 20),
            scratch=fwd_scratch(2),
            alias={5: 0, 6: 1},
        )

    mixed_t, d_out, back_rows, w_out, *wo_grads = call(
        mid_kernel,
        (shape(256, TOKENS), head_shape, state_shape[0], shape(2048, WO))
        + (shape(TOKENS, 128),) * PLANES,
        (info, place, q, start, kvs[4], *state, *cots, *kvs),
        (2 * score + 4 * TOKENS * 2048 * WO, 8 << 20, 1 << 20),
        scalars=2,
        scratch=[pltpu.VMEM((8, 1, TOKENS), f32), pltpu.VMEM((256, TOKENS), f32)]
        + [pltpu.VMEM((TOKENS, 2048), bf16)]
        + fwd_scratch(1),
        mib=16,
    )

    common = (info, q, d_out, back_rows, start)

    def back_step(offsets, acc):
        n = len(offsets)
        args = common + tuple(x[o % PLANES] for x in (kvs, wo_grads) for o in offsets)
        return call(
            functools.partial(bwd_kernel, offsets),
            (state_shape[1],) + (sent_shape,) * n,
            args if acc is None else args + (acc,),
            (5 * n * score, 3 << 20, n << 20),
            scratch=bwd_scratch(n),
            alias=None if acc is None else {len(args): 0},
        )

    acc, down, up = back_step((-4, 3), None)
    kept, sent = call(
        attn_kernel,
        (shape(2, TOKENS // SIDE, 2048),) * 2,
        (place, mixed_t, w_out),
        (2 * TOKENS * 2048 * WO, 4 << 20, 0),
        scratch=[pltpu.VMEM((TOKENS, WO), f32)],
    )
    acc, kept = tie((acc, kept))
    token_block = shape(TOKENS // SIDE, 2048)
    attn, across = call(cores_kernel, (token_block,) * 2, (kept, beside(sent, 1)), scalars=0)
    down, up = along(down, -1), along(up, 1)
    for offsets in ((-3, 2), (-2, 1)):
        acc, *terms = back_step(offsets, acc)
        down, up = add(down, terms[0]), add(up, terms[1])
        acc, _, _, across = tie((acc, down, up, across))
        down, up = along(down, -1), along(up, 1)
    across = beside(across, 2)
    acc, term = back_step((-1,), acc)
    down = add(down, term)
    acc, _ = tie((acc, down))
    down = along(down, -1)
    own_kv, q_grads = call(
        own_kernel,
        (shape(TOKENS, 128, dtype=f32), shape(PLANES, WO, ROWS)),
        (*common, kvs[0], acc, cos_t, sin_t, normed),
        (5 * score + 2 * TOKENS * 2048 * WO, 5 << 20, 1 << 20),
        scratch=[pltpu.VMEM((256, TOKENS), f32), pltpu.VMEM((WO, TOKENS), bf16)] + bwd_scratch(1),
    )
    attn = add(attn, across)
    own_kv, attn = tie((own_kv, attn))
    wo_sum, *grads = call(
        last_kernel,
        (shape(TOKENS, 128, dtype=f32),) + (shape(QKV, ROWS),) * PLANES,
        (info, own_kv, wo_grads[0], down, up, cos_t, sin_t, normed, q_grads),
        (2 * TOKENS * 2048 * 128, 6 << 20, 0),
        scratch=[pltpu.VMEM((128, TOKENS), bf16)],
    )
    down, up = ring_scatter(grads)
    sent = call(
        split_kernel,
        (shape(64, QKV + WO),) * SIDE,
        (place, down, up, grads[0], wo_sum),
        scratch=[pltpu.VMEM((ROWS, QKV + WO), f32)],
    )
    got = [sent[0]] + [beside(sent[k], k) for k in range(1, SIDE)]
    whole = shape(*old_w.shape, dtype=f32)
    new_m, sent = call(
        step_kernel,
        (whole, shape(*old_w.shape)),
        (place, old_m, *got),
        scratch=[pltpu.VMEM((SIDE, 64, QKV + WO), bf16)],
    )
    out_w, out_m = call(
        mean_kernel, (whole, whole), (old_w, new_m, swap(sent), partner), scalars=0
    )
    return (attn[None], out_w[None], out_m[None])


def solution(mesh):
    return jax.shard_map(
        on_device,
        mesh=mesh,
        in_specs=(
            P("group", "fsdp", None),
            P("group", None),
            P("group", "fsdp", None),
            P("group", "fsdp", None),
            P("group", "fsdp", None),
            P("group", "fsdp"),
            P(),
        ),
        out_specs=(P("group", "fsdp", None), P("group", "fsdp", None), P("group", "fsdp", None)),
        check_vma=False,
    )
```

```python
import functools
import math

import jax
import jax.numpy as jnp
from jax import lax
from jax.experimental import pallas as pl
from jax.experimental.pallas import tpu as pltpu
from jax.sharding import PartitionSpec as P

QUERY_HEADS = 16
KEY_VALUE_HEADS = 4
HEAD_SIZE = 64
REPEAT = QUERY_HEADS // KEY_VALUE_HEADS

EPS = 1e-05
BETA = 0.9
RATE = 0.01
THETA = 500000.0
MASK_FILL = -1e30
TOP_START = -1e20

PLANES = 8
SIDE = 4
TOKENS = 512
ROWS = 256
QKV = 384
WO = 256
NT = (((1,), (1,)), ((), ()))
NN = (((1,), (0,)), ((), ()))

f32 = jnp.float32
bf16 = jnp.bfloat16


def dot(a, b, dims=NN):
    return lax.dot_general(a, b, dims, preferred_element_type=f32)


def along(x, step):
    n = PLANES * SIDE
    return lax.ppermute(x, "fsdp", [(i, (i + SIDE * step) % n) for i in range(n)])


def beside(x, mask):
    return lax.ppermute(x, "fsdp", [(i, i ^ mask) for i in range(PLANES * SIDE)])


def ring_gather(x, second=None, first=None):
    got = [None] * PLANES
    got[0] = x
    down = up = x
    for s in range(1, PLANES // 2 + 1):
        down = along(down, 1)
        if s < PLANES // 2:
            up = along(up, -1)
            if s == 2 and second is not None:
                up, second = lax.optimization_barrier((up, second))
            if s == 1 and first is not None:
                down, up, first = lax.optimization_barrier((down, up, first))
            got[s] = up
        got[-s % PLANES] = down
    return got, second, first


def call(kernel, outs, args, cost=(1 << 20, 1 << 20, 0), scalars=1, scratch=(), alias=None, mib=8, space=pltpu.VMEM):
    flops, bytes_, exps = cost
    vmem, smem = (pl.BlockSpec(memory_space=m) for m in (pltpu.VMEM, pltpu.SMEM))
    return pl.pallas_call(
        kernel,
        out_shape=tuple(outs),
        in_specs=[smem] * scalars + [pl.BlockSpec(memory_space=space)] * (len(args) - scalars),
        out_specs=tuple(smem if o.shape == INFO.shape else vmem for o in outs),
        scratch_shapes=scratch,
        input_output_aliases=alias or {},
        compiler_params=pltpu.CompilerParams(vmem_limit_bytes=mib * 1024 * 1024),
        cost_estimate=pl.CostEstimate(flops=flops, bytes_accessed=bytes_, transcendentals=exps),
    )(*args)


def shape(*dims, dtype=bf16):
    return jax.ShapeDtypeStruct(dims, dtype)


INFO = shape(3, dtype=jnp.int32)


def add(got, term):
    return call(sum_kernel, (shape(*term.shape),), (got, term), scalars=0, mib=4)[0]


def ring_scatter(terms):
    down, up = along(terms[4], -1), along(terms[3], 1)
    for s in (2, 1):
        down, up = along(add(down, terms[-s - 1]), -1), along(add(up, terms[s]), 1)
    return along(add(down, terms[-1]), -1), up


def prep_kernel(place, *refs):
    sources, normed, rounded, refs = refs[:4], refs[4], refs[5], refs[6:]
    outs, sent, sems = refs[:SIDE], refs[SIDE], refs[-1]
    hidden, gain, weights, seg = refs[SIDE + 1 : SIDE + 5]
    copies = [
        pltpu.make_async_copy(source, to, sems.at[i])
        for i, (source, to) in enumerate(zip(sources, (hidden, gain, weights, seg)))
    ]
    for c in copies:
        c.start()
    for c in copies:
        c.wait()
    rounded[...] = weights[...].astype(bf16)
    x = hidden[...].astype(f32)
    scale = lax.rsqrt(jnp.mean(x * x, axis=1, keepdims=True) + EPS)
    normed[...] = (x * scale * gain[...]).astype(bf16)
    documents = seg[...]
    first, second = (jnp.sum((documents == d).astype(f32)) for d in range(2))
    lane = lanes((16, QKV + WO))
    counts = jnp.where(lane == 0, first, jnp.where(lane == 1, second, 0.0)).astype(bf16)
    for j in range(SIDE):
        cuts = [(256 * j, 256), (1024 + 64 * j, 64), (1280 + 64 * j, 64), (1536 + 256 * j, 256)]
        block = jnp.concatenate([weights[:, at : at + n] for at, n in cuts], axis=1)
        sent[j, :64] = block.astype(bf16)
        sent[j, 64:] = counts
    for k in range(SIDE):
        outs[k][...] = sent[place[1] ^ k]


def join_kernel(place, *refs):
    got, (w_rows, wo_rows) = refs[:SIDE], refs[SIDE:]
    row = lax.broadcasted_iota(jnp.int32, (16, QKV), 0)
    tail = jnp.zeros((16, QKV), f32)
    for k in range(SIDE):
        at = pl.multiple_of((place[1] ^ k) * 64, 64)
        w_rows[pl.ds(at, 64)] = got[k][:64, :QKV]
        wo_rows[pl.ds(at, 64)] = got[k][:64, QKV:]
        tail = jnp.where(row == k, got[k][64:, :QKV].astype(f32), tail)
    w_rows[ROWS:] = tail.astype(bf16)


def sum_kernel(*refs):
    refs[-1][...] = sum(r[...].astype(f32) for r in refs[:-1]).astype(bf16)


def split_kernel(place, down, up, own, wo_sum, *refs):
    outs, total = refs[:SIDE], refs[SIDE]
    qkv = down[...].astype(f32) + up[...].astype(f32) + own[...].astype(f32)
    total[:, :QKV] = qkv.T
    total[:, QKV:] = jnp.concatenate([wo_sum[:ROWS], wo_sum[ROWS:]], axis=1).T
    for k in range(SIDE):
        at = pl.multiple_of((place[1] ^ k) * 64, 64)
        outs[k][...] = total[pl.ds(at, 64)].astype(bf16)


def step_kernel(place, momentum, *refs):
    got, (new_m, sent, by_head) = refs[:SIDE], refs[SIDE:]
    for k in range(SIDE):
        by_head[place[1] ^ k] = got[k][...]
    for lo, n, to in ((0, 256, 0), (256, 64, 1024), (320, 64, 1280), (384, 256, 1536)):
        grad = jnp.concatenate([by_head[j, :, lo : lo + n] for j in range(SIDE)], axis=1)
        at = slice(to, to + SIDE * n)
        m = BETA * momentum[:, at] + grad.astype(f32)
        new_m[:, at] = m
        sent[:, at] = m.astype(bf16)


def mean_kernel(w, m, other, partner, out_w, out_m):
    mean_m = 0.5 * (m[...] + other[...].astype(f32))
    out_m[...] = mean_m
    out_w[...] = 0.5 * (w[...] + partner[...].astype(f32)) - RATE * mean_m


def plane_at(info, offset):
    return lax.rem(info[0] + (offset % PLANES), PLANES)


def lanes(shape):
    return lax.broadcasted_iota(jnp.int32, shape, len(shape) - 1)


def proj_kernel(place, cos, sin, wo_rows, *refs):
    parts, blocks = refs[:SIDE], refs[SIDE : SIDE + PLANES]
    normed, q_out, kv_out, start, info = refs[SIDE + PLANES :]
    for k in range(SIDE):
        at = pl.multiple_of((place[1] ^ k) * 128, 128)
        normed[pl.ds(at, 128)] = parts[k][...]
    total = jnp.zeros((TOKENS, QKV), f32)
    for o in range(PLANES):
        at = pl.multiple_of(plane_at(place, o) * ROWS, ROWS)
        total = total + dot(normed[:, pl.ds(at, ROWS)], blocks[o][:ROWS])

    tails = sum(b[ROWS : ROWS + 16].astype(f32)[:SIDE, :128] for b in blocks)
    lane = lanes(tails.shape)
    second = jnp.sum(jnp.where(lane == 0, tails, 0.0)).astype(jnp.int32)
    third = second + jnp.sum(jnp.where(lane == 1, tails, 0.0)).astype(jnp.int32)

    def start_of(t):
        return jnp.where(t >= third, third, jnp.where(t >= second, second, 0))

    start[...] = start_of(positions(place))
    info[0] = place[0]
    info[1] = start_of(place[0] * TOKENS)
    info[2] = start_of(place[0] * TOKENS + TOKENS - 1)

    lane = lanes((TOKENS, 128))
    first = lax.rem(lane, HEAD_SIZE) < HEAD_SIZE // 2
    low = lane < HEAD_SIZE
    c, s = cos[...], sin[...]

    def turned(u):
        return jnp.where(first, pltpu.roll(u, 96, 1), pltpu.roll(u, 32, 1))

    for pair in range(2):
        u = total[:, 128 * pair : 128 * pair + 128]
        u = (u * c + turned(u) * s) * (1.0 / math.sqrt(HEAD_SIZE))
        q_out[2 * pair] = jnp.where(low, u, 0.0).astype(bf16)
        q_out[2 * pair + 1] = jnp.where(low, pltpu.roll(u, 64, 1), 0.0).astype(bf16)
    u = total[:, 256:]
    kv_out[:TOKENS] = jnp.where(low, u * c + turned(u) * s, u).astype(bf16)
    kv_out[TOKENS : TOKENS + ROWS] = wo_rows[:, :128]
    kv_out[TOKENS + ROWS :] = wo_rows[:, 128:]


def masked(s, src, qpos, start):
    kpos = src * TOKENS + lax.broadcasted_iota(jnp.int32, (TOKENS, TOKENS), 0)
    return jnp.where((kpos <= qpos) & (kpos >= start), s, MASK_FILL)


def on_blocks(info, offsets, body):
    def step(i, carry):
        src = plane_at(info, offsets[0])
        for n, o in enumerate(offsets[1:], 1):
            src = jnp.where(i == n, plane_at(info, o), src)
        base = src * TOKENS
        seen = (src <= info[0]) & (base + TOKENS > info[1])
        edge = (src == info[0]) | (base < info[2])

        @pl.when(seen & edge)
        def _():
            body(i, src, True)

        if offsets != (0,):

            @pl.when(seen & jnp.logical_not(edge))
            def _():
                body(i, src, False)

        return carry

    lax.fori_loop(0, len(offsets), step, 0)


def for_heads(body):
    def step(h, carry):
        body(h, pl.ds(pl.multiple_of(h * HEAD_SIZE, HEAD_SIZE), HEAD_SIZE))
        return carry

    lax.fori_loop(0, REPEAT, step, 0)


def positions(info):
    return info[0] * TOKENS + lax.broadcasted_iota(jnp.int32, (1, TOKENS), 1)


def fwd_blocks(info, offsets, q, kvs, start, rows, acc, kv, value_t):
    for i, ref in enumerate(kvs):
        kv[i] = ref[:TOKENS]

    def block(i, src, mask):
        value_t[...] = kv[i].T[HEAD_SIZE:]

        def head(h, at):
            s = dot(kv[i], q[h], NT)
            if mask:
                s = masked(s, src, positions(info), start[...])
            old = rows[h]
            top = jnp.maximum(old, jnp.max(s, axis=0, keepdims=True))
            p = jnp.exp(s - top)
            fade = jnp.exp(old - top)
            rows[h] = top
            rows[4 + h] = rows[4 + h] * fade + jnp.sum(p, axis=0, keepdims=True)
            acc[at] = acc[at] * fade + dot(value_t[...], p.astype(bf16))

        for_heads(head)

    on_blocks(info, offsets, block)


def fwd_scratch(n):
    return [pltpu.VMEM((n, TOKENS, 128), bf16), pltpu.VMEM((HEAD_SIZE, TOKENS), bf16)]


def fwd_kernel(offsets, info, q, start, *refs):
    n = len(offsets)
    kvs, refs = refs[:n], refs[n:]
    if offsets[0] == 0:
        rows, acc, *scratch = refs
        rows[0:4] = jnp.full((4, 1, TOKENS), TOP_START, f32)
        rows[4:8] = jnp.zeros((4, 1, TOKENS), f32)
        acc[...] = jnp.zeros(acc.shape, f32)
    else:
        rows_in, acc_in, rows, acc, *scratch = refs
        rows[...] = rows_in[...]
        acc[...] = acc_in[...]
    fwd_blocks(info, offsets, q, kvs, start, rows, acc, *scratch)


def out_block(ref):
    return jnp.concatenate([ref[TOKENS : TOKENS + ROWS], ref[TOKENS + ROWS :]], axis=1)


def mid_kernel(info, place, q, start, kv, rows_in, acc_in, *refs):
    parts, blocks, refs = refs[:SIDE], refs[SIDE : SIDE + PLANES], refs[SIDE + PLANES :]
    mixed_t, d_out, back_rows, w_out = refs[:4]
    grads, (rows, acc, cot, *scratch) = refs[4 : 4 + PLANES], refs[4 + PLANES :]
    rows[...] = rows_in[...]
    acc[...] = acc_in[...]
    fwd_blocks(info, (-4,), q, (kv,), start, rows, acc, *scratch)
    for k in range(SIDE):
        at = pl.multiple_of((place[1] ^ k) * 128, 128)
        cot[pl.ds(at, 128)] = parts[k][...]
    for o in range(PLANES):
        at = pl.multiple_of(plane_at(info, o) * ROWS, ROWS)
        w_out[pl.ds(at, ROWS)] = out_block(blocks[o])
    d_mixed = dot(cot[...], w_out[...]).astype(bf16).astype(f32)
    inverse = jnp.concatenate([1.0 / rows[4 + h] for h in range(REPEAT)], axis=0)
    back_rows[0:4] = rows[0:4]
    for h in range(REPEAT):
        at = slice(64 * h, 64 * h + 64)
        mixed_t[at] = (acc[at] * inverse[h : h + 1]).astype(bf16)
    mt = mixed_t[...]
    prod = d_mixed.T * mt.astype(f32)
    for h in range(REPEAT):
        back_rows[4 + h] = inverse[h : h + 1] * jnp.sum(
            prod[64 * h : 64 * h + 64], axis=0, keepdims=True
        )
    by_row = jnp.concatenate([inverse, inverse], axis=0).T
    high = lanes((TOKENS, 128)) >= HEAD_SIZE
    for pair in range(2):
        u = d_mixed[:, 128 * pair : 128 * pair + 128]
        scale = [by_row[:, 2 * pair + i : 2 * pair + i + 1] for i in range(2)]
        u = u * jnp.where(high, scale[1], scale[0])
        d_out[2 * pair] = jnp.where(high, pltpu.roll(u, 64, 1), 0.0).astype(bf16)
        d_out[2 * pair + 1] = jnp.where(high, u, 0.0).astype(bf16)
    for o in range(PLANES):
        at = pl.multiple_of(plane_at(info, o) * ROWS, ROWS)
        term = dot(mt, cot[:, pl.ds(at, ROWS)]).astype(bf16)
        grads[o][:ROWS] = term[:, :128]
        grads[o][ROWS:] = term[:, 128:]


def attn_kernel(place, mixed_t, w_out, kept, sent, mixed):
    mixed[...] = mixed_t[...].astype(f32).T
    for k in range(SIDE):
        at = pl.multiple_of((place[1] ^ k) * 128, 128)
        out = sent if k % 2 else kept
        out[k // 2] = dot(mixed[pl.ds(at, 128)].astype(bf16), w_out[...], NT).astype(bf16)


def cores_kernel(a, b, own, across):
    own[...] = (a[0].astype(f32) + b[0].astype(f32)).astype(bf16)
    across[...] = (a[1].astype(f32) + b[1].astype(f32)).astype(bf16)


def bwd_blocks(info, offsets, q, d_out, rows, kvs, start, acc, sums, kv, key_t):
    for i, ref in enumerate(kvs):
        kv[i] = ref[:TOKENS]
        sums[i] = jnp.zeros((TOKENS, 128), f32)

    def block(i, src, mask):
        key_t[...] = kv[i].T[:HEAD_SIZE]

        def head(h, at):
            s = dot(kv[i], q[h], NT)
            if mask:
                s = masked(s, src, positions(info), start[...])
            p = jnp.exp(s - rows[h])
            dp = dot(kv[i], d_out[h], NT)
            ds = (p * (dp - rows[4 + h])).astype(bf16)
            sums[i] = sums[i] + (dot(p.astype(bf16), d_out[h]) + dot(ds, q[h]))
            acc[at] = acc[at] + dot(key_t[...], ds)

        for_heads(head)

    on_blocks(info, offsets, block)


def bwd_scratch(n):
    return [pltpu.VMEM((n, TOKENS, 128), f32)] + fwd_scratch(n)


def bwd_kernel(offsets, info, q, d_out, rows, start, *refs):
    n = len(offsets)
    kvs, wo_terms, refs, scratch = refs[:n], refs[n : 2 * n], refs[2 * n : -3], refs[-3:]
    acc, outs = refs[-n - 1], refs[-n:]
    acc[...] = refs[0][...] if len(refs) > n + 1 else jnp.zeros(acc.shape, f32)
    bwd_blocks(info, offsets, q, d_out, rows, kvs, start, acc, *scratch)
    for i in range(n):
        outs[i][:TOKENS] = scratch[0][i].astype(bf16)
        outs[i][TOKENS:] = wo_terms[i][...]


def turn_back(u, c, s, out, at, scale):
    one, two = u[:32], u[32:]
    out[at : at + 32] = ((one * c + two * s) * scale).astype(bf16)
    out[at + 32 : at + 64] = ((two * c - one * s) * scale).astype(bf16)


def own_kernel(
    info, q, d_out, rows, start, kv, acc_in, cos_t, sin_t, normed,
    out, grads, acc, d_t, *scratch,
):
    acc[...] = acc_in[...]
    bwd_blocks(info, (0,), q, d_out, rows, (kv,), start, acc, *scratch)
    out[...] = scratch[0][0]
    c, s = cos_t[...], sin_t[...]
    for h in range(REPEAT):
        turn_back(acc[64 * h : 64 * h + 64], c, s, d_t, 64 * h, 1.0 / math.sqrt(HEAD_SIZE))
    for o in range(PLANES):
        at = pl.multiple_of(plane_at(info, o) * ROWS, ROWS)
        grads[o] = dot(d_t[...], normed[:, pl.ds(at, ROWS)]).astype(bf16)


def last_kernel(info, own, wo_own, got_a, got_b, cos_t, sin_t, normed, q_grads, *refs):
    wo_sum, grads, d_t = refs[0], refs[1 : 1 + PLANES], refs[1 + PLANES]
    got = got_a[...].astype(f32) + got_b[...].astype(f32)
    kv_t = (got[:TOKENS] + own[...]).T
    wo_sum[...] = got[TOKENS:] + wo_own[...].astype(f32)
    turn_back(kv_t[:64], cos_t[...], sin_t[...], d_t, 0, 1.0)
    d_t[64:128] = kv_t[64:].astype(bf16)
    for o in range(PLANES):
        at = pl.multiple_of(plane_at(info, o) * ROWS, ROWS)
        grads[o][:WO] = q_grads[o]
        grads[o][WO:] = dot(d_t[...], normed[:, pl.ds(at, ROWS)]).astype(bf16)


def on_device(hidden, gain, weights, momentum, cotangent, segment, distance):
    rank = lax.axis_index("fsdp")
    plane, own = rank // SIDE, rank % SIDE
    old_w, old_m = weights[0], momentum[0]
    place = jnp.stack([plane, own]).astype(jnp.int32)

    tie = lax.optimization_barrier

    half = HEAD_SIZE // 2
    tokens = plane * TOKENS + jnp.arange(TOKENS, dtype=jnp.int32)
    freq = jnp.power(THETA, -jnp.arange(half, dtype=f32) * 2.0 / HEAD_SIZE)
    angle = tokens.astype(f32)[:, None] * freq[None, :]
    cosine, sine = jnp.cos(angle), jnp.sin(angle)
    cos_rows = jnp.concatenate([cosine] * 4, axis=1)
    sin_rows = jnp.concatenate([-sine, sine] * 2, axis=1)
    cos_t, sin_t = cosine.T, sine.T

    normed, rounded, *sent = call(
        prep_kernel,
        (shape(128, 2048), shape(*old_w.shape)) + (shape(80, QKV + WO),) * SIDE,
        (place, hidden[0], gain, old_w, segment),
        scratch=[
            pltpu.VMEM((SIDE, 80, QKV + WO), bf16),
            pltpu.VMEM((128, 2048), bf16),
            pltpu.VMEM(gain.shape, f32),
            pltpu.VMEM(old_w.shape, f32),
            pltpu.VMEM(segment.shape, jnp.int32),
            pltpu.SemaphoreType.DMA((4,)),
        ],
        space=pl.ANY,
        mib=60,
    )
    got = [sent[0]] + [beside(sent[k], k) for k in range(1, SIDE)]
    w_rows, wo_rows = call(join_kernel, (shape(ROWS + 16, QKV), shape(ROWS, WO)), (place, *got))
    w_rows, cos_rows, sin_rows, cos_t, sin_t = tie((w_rows, cos_rows, sin_rows, cos_t, sin_t))

    groups = lax.axis_size("group")
    bits = groups.bit_length() - 1
    bit = jnp.remainder(distance[0], bits)

    def swap(x):
        def by(b):
            return lambda x: lax.ppermute(x, "group", [(i, i ^ 1 << b) for i in range(groups)])

        return lax.switch(bit, [by(b) for b in range(bits)], x)

    rounded, _ = tie((rounded, w_rows))
    w_qkv, across, partner = ring_gather(w_rows, beside(normed, 2), swap(rounded))
    parts = [normed, beside(normed, 1), across, beside(across, 1)]

    state_shape = (shape(8, 1, TOKENS, dtype=f32), shape(256, TOKENS, dtype=f32))
    head_shape = shape(REPEAT, TOKENS, 128)
    sent_shape = shape(2 * TOKENS, 128)
    score = 2 * REPEAT * TOKENS * TOKENS * 128

    normed, q, kv, start, info = call(
        proj_kernel,
        (shape(TOKENS, 2048), head_shape, sent_shape, shape(1, TOKENS, dtype=jnp.int32), INFO),
        (place, cos_rows, sin_rows, wo_rows, *parts, *w_qkv),
        (2 * TOKENS * 2048 * QKV, 8 << 20, 0),
    )

    cot, _ = lax.optimization_barrier((cotangent[0], q))
    across = beside(cot, 2)
    cots = [cot, beside(cot, 1), across, beside(across, 1)]
    def forward_step(offsets, state):
        n = len(offsets)
        return call(
            functools.partial(fwd_kernel, offsets),
            state_shape,
            (info, q, start, *[kvs[o] for o in offsets], *state),
            (2 * n * score, 2 << 20, n << 20),
            scratch=fwd_scratch(n),
            alias={3 + n: 0, 4 + n: 1} if state else None,
        )

    kvs = {0: kv, -1: along(kv, 1), 1: along(kv, -1)}
    state = forward_step((0,), ())
    for s in (1, 2, 3):
        down, up, *state = tie((kvs[-s], kvs[s], *state))
        kvs[-s - 1] = along(down, 1)
        if s < 3:
            kvs[s + 1] = along(up, -1)
        state = forward_step((-s, s), state)
    kvs = [kvs[o - PLANES if o >= PLANES // 2 else o] for o in range(PLANES)]

    mixed_t, d_out, back_rows, w_out, *wo_grads = call(
        mid_kernel,
        (shape(256, TOKENS), head_shape, state_shape[0], shape(2048, WO))
        + (shape(TOKENS, 128),) * PLANES,
        (info, place, q, start, kvs[4], *state, *cots, *kvs),
        (2 * score + 4 * TOKENS * 2048 * WO, 8 << 20, 1 << 20),
        scalars=2,
        scratch=[pltpu.VMEM((8, 1, TOKENS), f32), pltpu.VMEM((256, TOKENS), f32)]
        + [pltpu.VMEM((TOKENS, 2048), bf16)]
        + fwd_scratch(1),
        mib=16,
    )

    common = (info, q, d_out, back_rows, start)

    def back_step(offsets, acc):
        n = len(offsets)
        args = common + tuple(x[o % PLANES] for x in (kvs, wo_grads) for o in offsets)
        return call(
            functools.partial(bwd_kernel, offsets),
            (state_shape[1],) + (sent_shape,) * n,
            args if acc is None else args + (acc,),
            (5 * n * score, 3 << 20, n << 20),
            scratch=bwd_scratch(n),
            alias=None if acc is None else {len(args): 0},
        )

    acc, down, up = back_step((-4, 3), None)
    kept, sent = call(
        attn_kernel,
        (shape(2, TOKENS // SIDE, 2048),) * 2,
        (place, mixed_t, w_out),
        (2 * TOKENS * 2048 * WO, 4 << 20, 0),
        scratch=[pltpu.VMEM((TOKENS, WO), f32)],
    )
    acc, kept = tie((acc, kept))
    token_block = shape(TOKENS // SIDE, 2048)
    attn, across = call(cores_kernel, (token_block,) * 2, (kept, beside(sent, 1)), scalars=0)
    down, up = along(down, -1), along(up, 1)
    for offsets in ((-3, 2), (-2, 1)):
        acc, *terms = back_step(offsets, acc)
        down, up = add(down, terms[0]), add(up, terms[1])
        acc, _, _, across = tie((acc, down, up, across))
        down, up = along(down, -1), along(up, 1)
    across = beside(across, 2)
    acc, term = back_step((-1,), acc)
    down = add(down, term)
    acc, _ = tie((acc, down))
    down = along(down, -1)
    own_kv, q_grads = call(
        own_kernel,
        (shape(TOKENS, 128, dtype=f32), shape(PLANES, WO, ROWS)),
        (*common, kvs[0], acc, cos_t, sin_t, normed),
        (5 * score + 2 * TOKENS * 2048 * WO, 5 << 20, 1 << 20),
        scratch=[pltpu.VMEM((256, TOKENS), f32), pltpu.VMEM((WO, TOKENS), bf16)] + bwd_scratch(1),
    )
    attn = add(attn, across)
    own_kv, attn = tie((own_kv, attn))
    wo_sum, *grads = call(
        last_kernel,
        (shape(TOKENS, 128, dtype=f32),) + (shape(QKV, ROWS),) * PLANES,
        (info, own_kv, wo_grads[0], down, up, cos_t, sin_t, normed, q_grads),
        (2 * TOKENS * 2048 * 128, 6 << 20, 0),
        scratch=[pltpu.VMEM((128, TOKENS), bf16)],
    )
    down, up = ring_scatter(grads)
    sent = call(
        split_kernel,
        (shape(64, QKV + WO),) * SIDE,
        (place, down, up, grads[0], wo_sum),
        scratch=[pltpu.VMEM((ROWS, QKV + WO), f32)],
    )
    got = [sent[0]] + [beside(sent[k], k) for k in range(1, SIDE)]
    whole = shape(*old_w.shape, dtype=f32)
    new_m, sent = call(
        step_kernel,
        (whole, shape(*old_w.shape)),
        (place, old_m, *got),
        scratch=[pltpu.VMEM((SIDE, 64, QKV + WO), bf16)],
    )
    out_w, out_m = call(
        mean_kernel, (whole, whole), (old_w, new_m, swap(sent), partner), scalars=0
    )
    return (attn[None], out_w[None], out_m[None])


def solution(mesh):
    return jax.shard_map(
        on_device,
        mesh=mesh,
        in_specs=(
            P("group", "fsdp", None),
            P("group", None),
            P("group", "fsdp", None),
            P("group", "fsdp", None),
            P("group", "fsdp", None),
            P("group", "fsdp"),
            P(),
        ),
        out_specs=(P("group", "fsdp", None), P("group", "fsdp", None), P("group", "fsdp", None)),
        check_vma=False,
    )
```

```python
import functools
import math

import jax
import jax.numpy as jnp
from jax import lax
from jax.experimental import pallas as pl
from jax.experimental.pallas import tpu as pltpu
from jax.sharding import PartitionSpec as P

QUERY_HEADS = 16
KEY_VALUE_HEADS = 4
HEAD_SIZE = 64
REPEAT = QUERY_HEADS // KEY_VALUE_HEADS

EPS = 1e-05
BETA = 0.9
RATE = 0.01
THETA = 500000.0
MASK_FILL = -1e30
TOP_START = -1e20

PLANES = 8
SIDE = 4
TOKENS = 512
ROWS = 256
QKV = 384
WO = 256
NT = (((1,), (1,)), ((), ()))
NN = (((1,), (0,)), ((), ()))

f32 = jnp.float32
bf16 = jnp.bfloat16


def dot(a, b, dims=NN):
    return lax.dot_general(a, b, dims, preferred_element_type=f32)


def along(x, step):
    n = PLANES * SIDE
    return lax.ppermute(x, "fsdp", [(i, (i + SIDE * step) % n) for i in range(n)])


def beside(x, mask):
    return lax.ppermute(x, "fsdp", [(i, i ^ mask) for i in range(PLANES * SIDE)])


def ring_gather(x, second):
    got = [None] * PLANES
    got[0] = x
    down = up = x
    for s in range(1, PLANES // 2 + 1):
        down = along(down, 1)
        if s < PLANES // 2:
            up = along(up, -1)
            if s == 2:
                up, second = lax.optimization_barrier((up, second))
            got[s] = up
        got[-s % PLANES] = down
    return got, second


def call(kernel, outs, args, cost=(1 << 20, 1 << 20, 0), scalars=1, scratch=(), alias=None, mib=8, space=pltpu.VMEM):
    flops, bytes_, exps = cost
    vmem, smem = (pl.BlockSpec(memory_space=m) for m in (pltpu.VMEM, pltpu.SMEM))
    return pl.pallas_call(
        kernel,
        out_shape=tuple(outs),
        in_specs=[smem] * scalars + [pl.BlockSpec(memory_space=space)] * (len(args) - scalars),
        out_specs=tuple(smem if o.shape == INFO.shape else vmem for o in outs),
        scratch_shapes=scratch,
        input_output_aliases=alias or {},
        compiler_params=pltpu.CompilerParams(vmem_limit_bytes=mib * 1024 * 1024),
        cost_estimate=pl.CostEstimate(flops=flops, bytes_accessed=bytes_, transcendentals=exps),
    )(*args)


def shape(*dims, dtype=bf16):
    return jax.ShapeDtypeStruct(dims, dtype)


INFO = shape(3, dtype=jnp.int32)


def add(got, term):
    return call(sum_kernel, (shape(*term.shape),), (got, term), scalars=0, mib=4)[0]


def ring_scatter(terms):
    down, up = along(terms[4], -1), along(terms[3], 1)
    for s in (2, 1):
        down, up = along(add(down, terms[-s - 1]), -1), along(add(up, terms[s]), 1)
    return along(add(down, terms[-1]), -1), up


def prep_kernel(place, *refs):
    sources, normed, rounded, refs = refs[:4], refs[4], refs[5], refs[6:]
    outs, sent, sems = refs[:SIDE], refs[SIDE], refs[-1]
    hidden, gain, weights, seg = refs[SIDE + 1 : SIDE + 5]
    copies = [
        pltpu.make_async_copy(source, to, sems.at[i])
        for i, (source, to) in enumerate(zip(sources, (hidden, gain, weights, seg)))
    ]
    for c in copies:
        c.start()
    for c in copies:
        c.wait()
    rounded[...] = weights[...].astype(bf16)
    x = hidden[...].astype(f32)
    scale = lax.rsqrt(jnp.mean(x * x, axis=1, keepdims=True) + EPS)
    normed[...] = (x * scale * gain[...]).astype(bf16)
    documents = seg[...]
    first, second = (jnp.sum((documents == d).astype(f32)) for d in range(2))
    lane = lanes((16, QKV + WO))
    counts = jnp.where(lane == 0, first, jnp.where(lane == 1, second, 0.0)).astype(bf16)
    for j in range(SIDE):
        cuts = [(256 * j, 256), (1024 + 64 * j, 64), (1280 + 64 * j, 64), (1536 + 256 * j, 256)]
        block = jnp.concatenate([weights[:, at : at + n] for at, n in cuts], axis=1)
        sent[j, :64] = block.astype(bf16)
        sent[j, 64:] = counts
    for k in range(SIDE):
        outs[k][...] = sent[place[1] ^ k]


def join_kernel(place, *refs):
    got, (w_rows, wo_rows) = refs[:SIDE], refs[SIDE:]
    row = lax.broadcasted_iota(jnp.int32, (16, QKV), 0)
    tail = jnp.zeros((16, QKV), f32)
    for k in range(SIDE):
        at = pl.multiple_of((place[1] ^ k) * 64, 64)
        w_rows[pl.ds(at, 64)] = got[k][:64, :QKV]
        wo_rows[pl.ds(at, 64)] = got[k][:64, QKV:]
        tail = jnp.where(row == k, got[k][64:, :QKV].astype(f32), tail)
    w_rows[ROWS:] = tail.astype(bf16)


def sum_kernel(*refs):
    refs[-1][...] = sum(r[...].astype(f32) for r in refs[:-1]).astype(bf16)


def split_kernel(place, down, up, own, wo_sum, *refs):
    outs, total = refs[:SIDE], refs[SIDE]
    qkv = down[...].astype(f32) + up[...].astype(f32) + own[...].astype(f32)
    total[:, :QKV] = qkv.T
    total[:, QKV:] = jnp.concatenate([wo_sum[:ROWS], wo_sum[ROWS:]], axis=1).T
    for k in range(SIDE):
        at = pl.multiple_of((place[1] ^ k) * 64, 64)
        outs[k][...] = total[pl.ds(at, 64)].astype(bf16)


def step_kernel(place, momentum, *refs):
    got, (new_m, sent, by_head) = refs[:SIDE], refs[SIDE:]
    for k in range(SIDE):
        by_head[place[1] ^ k] = got[k][...]
    for lo, n, to in ((0, 256, 0), (256, 64, 1024), (320, 64, 1280), (384, 256, 1536)):
        grad = jnp.concatenate([by_head[j, :, lo : lo + n] for j in range(SIDE)], axis=1)
        at = slice(to, to + SIDE * n)
        m = BETA * momentum[:, at] + grad.astype(f32)
        new_m[:, at] = m
        sent[:, at] = m.astype(bf16)


def mean_kernel(bit, w, m, other, *refs):
    partners, (out_w, out_m) = refs[:-2], refs[-2:]
    mean_m = 0.5 * (m[...] + other[...].astype(f32))
    out_m[...] = mean_m
    for b, partner in enumerate(partners):

        @pl.when(bit[0] == b)
        def _():
            out_w[...] = 0.5 * (w[...] + partner[...].astype(f32)) - RATE * mean_m


def plane_at(info, offset):
    return lax.rem(info[0] + (offset % PLANES), PLANES)


def lanes(shape):
    return lax.broadcasted_iota(jnp.int32, shape, len(shape) - 1)


def proj_kernel(place, cos, sin, wo_rows, *refs):
    parts, blocks = refs[:SIDE], refs[SIDE : SIDE + PLANES]
    normed, q_out, kv_out, start, info = refs[SIDE + PLANES :]
    for k in range(SIDE):
        at = pl.multiple_of((place[1] ^ k) * 128, 128)
        normed[pl.ds(at, 128)] = parts[k][...]
    total = jnp.zeros((TOKENS, QKV), f32)
    for o in range(PLANES):
        at = pl.multiple_of(plane_at(place, o) * ROWS, ROWS)
        total = total + dot(normed[:, pl.ds(at, ROWS)], blocks[o][:ROWS])

    tails = sum(b[ROWS : ROWS + 16].astype(f32)[:SIDE, :128] for b in blocks)
    lane = lanes(tails.shape)
    second = jnp.sum(jnp.where(lane == 0, tails, 0.0)).astype(jnp.int32)
    third = second + jnp.sum(jnp.where(lane == 1, tails, 0.0)).astype(jnp.int32)

    def start_of(t):
        return jnp.where(t >= third, third, jnp.where(t >= second, second, 0))

    start[...] = start_of(positions(place))
    info[0] = place[0]
    info[1] = start_of(place[0] * TOKENS)
    info[2] = start_of(place[0] * TOKENS + TOKENS - 1)

    lane = lanes((TOKENS, 128))
    first = lax.rem(lane, HEAD_SIZE) < HEAD_SIZE // 2
    low = lane < HEAD_SIZE
    c, s = cos[...], sin[...]

    def turned(u):
        return jnp.where(first, pltpu.roll(u, 96, 1), pltpu.roll(u, 32, 1))

    for pair in range(2):
        u = total[:, 128 * pair : 128 * pair + 128]
        u = (u * c + turned(u) * s) * (1.0 / math.sqrt(HEAD_SIZE))
        q_out[2 * pair] = jnp.where(low, u, 0.0).astype(bf16)
        q_out[2 * pair + 1] = jnp.where(low, pltpu.roll(u, 64, 1), 0.0).astype(bf16)
    u = total[:, 256:]
    kv_out[:TOKENS] = jnp.where(low, u * c + turned(u) * s, u).astype(bf16)
    kv_out[TOKENS : TOKENS + ROWS] = wo_rows[:, :128]
    kv_out[TOKENS + ROWS :] = wo_rows[:, 128:]


def masked(s, src, qpos, start):
    kpos = src * TOKENS + lax.broadcasted_iota(jnp.int32, (TOKENS, TOKENS), 0)
    return jnp.where((kpos <= qpos) & (kpos >= start), s, MASK_FILL)


def on_blocks(info, offsets, body):
    def step(i, carry):
        src = plane_at(info, offsets[0])
        for n, o in enumerate(offsets[1:], 1):
            src = jnp.where(i == n, plane_at(info, o), src)
        base = src * TOKENS
        seen = (src <= info[0]) & (base + TOKENS > info[1])
        edge = (src == info[0]) | (base < info[2])

        @pl.when(seen & edge)
        def _():
            body(i, src, True)

        if offsets != (0,):

            @pl.when(seen & jnp.logical_not(edge))
            def _():
                body(i, src, False)

        return carry

    lax.fori_loop(0, len(offsets), step, 0)


def for_heads(body):
    def step(h, carry):
        body(h, pl.ds(pl.multiple_of(h * HEAD_SIZE, HEAD_SIZE), HEAD_SIZE))
        return carry

    lax.fori_loop(0, REPEAT, step, 0)


def positions(info):
    return info[0] * TOKENS + lax.broadcasted_iota(jnp.int32, (1, TOKENS), 1)


def fwd_blocks(info, offsets, q, kvs, start, rows, acc, kv, value_t):
    for i, ref in enumerate(kvs):
        kv[i] = ref[:TOKENS]

    def block(i, src, mask):
        value_t[...] = kv[i].T[HEAD_SIZE:]

        def head(h, at):
            s = dot(kv[i], q[h], NT)
            if mask:
                s = masked(s, src, positions(info), start[...])
            old = rows[h]
            top = jnp.maximum(old, jnp.max(s, axis=0, keepdims=True))
            p = jnp.exp(s - top)
            fade = jnp.exp(old - top)
            rows[h] = top
            rows[4 + h] = rows[4 + h] * fade + jnp.sum(p, axis=0, keepdims=True)
            acc[at] = acc[at] * fade + dot(value_t[...], p.astype(bf16))

        for_heads(head)

    on_blocks(info, offsets, block)


def fwd_scratch(n):
    return [pltpu.VMEM((n, TOKENS, 128), bf16), pltpu.VMEM((HEAD_SIZE, TOKENS), bf16)]


def fwd_kernel(offsets, info, q, start, *refs):
    n = len(offsets)
    kvs, refs = refs[:n], refs[n:]
    if offsets[0] == 0:
        rows, acc, *scratch = refs
        rows[0:4] = jnp.full((4, 1, TOKENS), TOP_START, f32)
        rows[4:8] = jnp.zeros((4, 1, TOKENS), f32)
        acc[...] = jnp.zeros(acc.shape, f32)
    else:
        rows_in, acc_in, rows, acc, *scratch = refs
        rows[...] = rows_in[...]
        acc[...] = acc_in[...]
    fwd_blocks(info, offsets, q, kvs, start, rows, acc, *scratch)


def out_block(ref):
    return jnp.concatenate([ref[TOKENS : TOKENS + ROWS], ref[TOKENS + ROWS :]], axis=1)


def mid_kernel(info, place, q, start, kv, rows_in, acc_in, *refs):
    parts, blocks, refs = refs[:SIDE], refs[SIDE : SIDE + PLANES], refs[SIDE + PLANES :]
    mixed_t, d_out, back_rows, w_out = refs[:4]
    grads, (rows, acc, cot, *scratch) = refs[4 : 4 + PLANES], refs[4 + PLANES :]
    rows[...] = rows_in[...]
    acc[...] = acc_in[...]
    fwd_blocks(info, (-4,), q, (kv,), start, rows, acc, *scratch)
    for k in range(SIDE):
        at = pl.multiple_of((place[1] ^ k) * 128, 128)
        cot[pl.ds(at, 128)] = parts[k][...]
    for o in range(PLANES):
        at = pl.multiple_of(plane_at(info, o) * ROWS, ROWS)
        w_out[pl.ds(at, ROWS)] = out_block(blocks[o])
    d_mixed = dot(cot[...], w_out[...]).astype(bf16).astype(f32)
    inverse = jnp.concatenate([1.0 / rows[4 + h] for h in range(REPEAT)], axis=0)
    back_rows[0:4] = rows[0:4]
    for h in range(REPEAT):
        at = slice(64 * h, 64 * h + 64)
        mixed_t[at] = (acc[at] * inverse[h : h + 1]).astype(bf16)
    mt = mixed_t[...]
    prod = d_mixed.T * mt.astype(f32)
    for h in range(REPEAT):
        back_rows[4 + h] = inverse[h : h + 1] * jnp.sum(
            prod[64 * h : 64 * h + 64], axis=0, keepdims=True
        )
    by_row = jnp.concatenate([inverse, inverse], axis=0).T
    high = lanes((TOKENS, 128)) >= HEAD_SIZE
    for pair in range(2):
        u = d_mixed[:, 128 * pair : 128 * pair + 128]
        scale = [by_row[:, 2 * pair + i : 2 * pair + i + 1] for i in range(2)]
        u = u * jnp.where(high, scale[1], scale[0])
        d_out[2 * pair] = jnp.where(high, pltpu.roll(u, 64, 1), 0.0).astype(bf16)
        d_out[2 * pair + 1] = jnp.where(high, u, 0.0).astype(bf16)
    for o in range(PLANES):
        at = pl.multiple_of(plane_at(info, o) * ROWS, ROWS)
        term = dot(mt, cot[:, pl.ds(at, ROWS)]).astype(bf16)
        grads[o][:ROWS] = term[:, :128]
        grads[o][ROWS:] = term[:, 128:]


def attn_kernel(place, mixed_t, w_out, kept, sent, mixed):
    mixed[...] = mixed_t[...].astype(f32).T
    for k in range(SIDE):
        at = pl.multiple_of((place[1] ^ k) * 128, 128)
        out = sent if k % 2 else kept
        out[k // 2] = dot(mixed[pl.ds(at, 128)].astype(bf16), w_out[...], NT).astype(bf16)


def cores_kernel(a, b, own, across):
    own[...] = (a[0].astype(f32) + b[0].astype(f32)).astype(bf16)
    across[...] = (a[1].astype(f32) + b[1].astype(f32)).astype(bf16)


def bwd_blocks(info, offsets, q, d_out, rows, kvs, start, acc, sums, kv, key_t):
    for i, ref in enumerate(kvs):
        kv[i] = ref[:TOKENS]
        sums[i] = jnp.zeros((TOKENS, 128), f32)

    def block(i, src, mask):
        key_t[...] = kv[i].T[:HEAD_SIZE]

        def head(h, at):
            s = dot(kv[i], q[h], NT)
            if mask:
                s = masked(s, src, positions(info), start[...])
            p = jnp.exp(s - rows[h])
            dp = dot(kv[i], d_out[h], NT)
            ds = (p * (dp - rows[4 + h])).astype(bf16)
            sums[i] = sums[i] + (dot(p.astype(bf16), d_out[h]) + dot(ds, q[h]))
            acc[at] = acc[at] + dot(key_t[...], ds)

        for_heads(head)

    on_blocks(info, offsets, block)


def bwd_scratch(n):
    return [pltpu.VMEM((n, TOKENS, 128), f32)] + fwd_scratch(n)


def bwd_kernel(offsets, info, q, d_out, rows, start, *refs):
    n = len(offsets)
    kvs, wo_terms, refs, scratch = refs[:n], refs[n : 2 * n], refs[2 * n : -3], refs[-3:]
    acc, outs = refs[-n - 1], refs[-n:]
    acc[...] = refs[0][...] if len(refs) > n + 1 else jnp.zeros(acc.shape, f32)
    bwd_blocks(info, offsets, q, d_out, rows, kvs, start, acc, *scratch)
    for i in range(n):
        outs[i][:TOKENS] = scratch[0][i].astype(bf16)
        outs[i][TOKENS:] = wo_terms[i][...]


def turn_back(u, c, s, out, at, scale):
    one, two = u[:32], u[32:]
    out[at : at + 32] = ((one * c + two * s) * scale).astype(bf16)
    out[at + 32 : at + 64] = ((two * c - one * s) * scale).astype(bf16)


def own_kernel(
    info, q, d_out, rows, start, kv, acc_in, cos_t, sin_t, normed,
    out, grads, acc, d_t, *scratch,
):
    acc[...] = acc_in[...]
    bwd_blocks(info, (0,), q, d_out, rows, (kv,), start, acc, *scratch)
    out[...] = scratch[0][0]
    c, s = cos_t[...], sin_t[...]
    for h in range(REPEAT):
        turn_back(acc[64 * h : 64 * h + 64], c, s, d_t, 64 * h, 1.0 / math.sqrt(HEAD_SIZE))
    for o in range(PLANES):
        at = pl.multiple_of(plane_at(info, o) * ROWS, ROWS)
        grads[o] = dot(d_t[...], normed[:, pl.ds(at, ROWS)]).astype(bf16)


def last_kernel(info, own, wo_own, got_a, got_b, cos_t, sin_t, normed, q_grads, *refs):
    wo_sum, grads, d_t = refs[0], refs[1 : 1 + PLANES], refs[1 + PLANES]
    got = got_a[...].astype(f32) + got_b[...].astype(f32)
    kv_t = (got[:TOKENS] + own[...]).T
    wo_sum[...] = got[TOKENS:] + wo_own[...].astype(f32)
    turn_back(kv_t[:64], cos_t[...], sin_t[...], d_t, 0, 1.0)
    d_t[64:128] = kv_t[64:].astype(bf16)
    for o in range(PLANES):
        at = pl.multiple_of(plane_at(info, o) * ROWS, ROWS)
        grads[o][:WO] = q_grads[o]
        grads[o][WO:] = dot(d_t[...], normed[:, pl.ds(at, ROWS)]).astype(bf16)


def on_device(hidden, gain, weights, momentum, cotangent, segment, distance):
    rank = lax.axis_index("fsdp")
    plane, own = rank // SIDE, rank % SIDE
    old_w, old_m = weights[0], momentum[0]
    place = jnp.stack([plane, own]).astype(jnp.int32)

    tie = lax.optimization_barrier

    half = HEAD_SIZE // 2
    tokens = plane * TOKENS + jnp.arange(TOKENS, dtype=jnp.int32)
    freq = jnp.power(THETA, -jnp.arange(half, dtype=f32) * 2.0 / HEAD_SIZE)
    angle = tokens.astype(f32)[:, None] * freq[None, :]
    cosine, sine = jnp.cos(angle), jnp.sin(angle)
    cos_rows = jnp.concatenate([cosine] * 4, axis=1)
    sin_rows = jnp.concatenate([-sine, sine] * 2, axis=1)
    cos_t, sin_t = cosine.T, sine.T

    normed, rounded, *sent = call(
        prep_kernel,
        (shape(128, 2048), shape(*old_w.shape)) + (shape(80, QKV + WO),) * SIDE,
        (place, hidden[0], gain, old_w, segment),
        scratch=[
            pltpu.VMEM((SIDE, 80, QKV + WO), bf16),
            pltpu.VMEM((128, 2048), bf16),
            pltpu.VMEM(gain.shape, f32),
            pltpu.VMEM(old_w.shape, f32),
            pltpu.VMEM(segment.shape, jnp.int32),
            pltpu.SemaphoreType.DMA((4,)),
        ],
        space=pl.ANY,
        mib=60,
    )
    got = [sent[0]] + [beside(sent[k], k) for k in range(1, SIDE)]
    w_rows, wo_rows = call(join_kernel, (shape(ROWS + 16, QKV), shape(ROWS, WO)), (place, *got))
    w_rows, cos_rows, sin_rows, cos_t, sin_t = tie((w_rows, cos_rows, sin_rows, cos_t, sin_t))

    groups = lax.axis_size("group")
    bits = groups.bit_length() - 1
    bit = jnp.remainder(distance, bits).astype(jnp.int32)

    def swap(b, x):
        return lax.ppermute(x, "group", [(i, i ^ 1 << b) for i in range(groups)])

    w_qkv, across = ring_gather(w_rows, beside(normed, 2))
    parts = [normed, beside(normed, 1), across, beside(across, 1)]

    state_shape = (shape(8, 1, TOKENS, dtype=f32), shape(256, TOKENS, dtype=f32))
    head_shape = shape(REPEAT, TOKENS, 128)
    sent_shape = shape(2 * TOKENS, 128)
    score = 2 * REPEAT * TOKENS * TOKENS * 128

    normed, q, kv, start, info = call(
        proj_kernel,
        (shape(TOKENS, 2048), head_shape, sent_shape, shape(1, TOKENS, dtype=jnp.int32), INFO),
        (place, cos_rows, sin_rows, wo_rows, *parts, *w_qkv),
        (2 * TOKENS * 2048 * QKV, 8 << 20, 0),
    )

    cot, _ = lax.optimization_barrier((cotangent[0], q))
    across = beside(cot, 2)
    cots = [cot, beside(cot, 1), across, beside(across, 1)]
    cots[0], *partners = tie((cots[0], *[swap(b, rounded) for b in range(bits)]))
    def forward_step(offsets, state):
        n = len(offsets)
        return call(
            functools.partial(fwd_kernel, offsets),
            state_shape,
            (info, q, start, *[kvs[o] for o in offsets], *state),
            (2 * n * score, 2 << 20, n << 20),
            scratch=fwd_scratch(n),
            alias={3 + n: 0, 4 + n: 1} if state else None,
        )

    kvs = {0: kv, -1: along(kv, 1), 1: along(kv, -1)}
    state = forward_step((0,), ())
    for s in (1, 2, 3):
        kvs[-s - 1] = along(tie((kvs[-s], state[0]))[0], 1)
        if s < 3:
            kvs[s + 1] = along(tie((kvs[s], state[0]))[0], -1)
        state = forward_step((-s, s), state)
    kvs = [kvs[o - PLANES if o >= PLANES // 2 else o] for o in range(PLANES)]

    mixed_t, d_out, back_rows, w_out, *wo_grads = call(
        mid_kernel,
        (shape(256, TOKENS), head_shape, state_shape[0], shape(2048, WO))
        + (shape(TOKENS, 128),) * PLANES,
        (info, place, q, start, kvs[4], *state, *cots, *kvs),
        (2 * score + 4 * TOKENS * 2048 * WO, 8 << 20, 1 << 20),
        scalars=2,
        scratch=[pltpu.VMEM((8, 1, TOKENS), f32), pltpu.VMEM((256, TOKENS), f32)]
        + [pltpu.VMEM((TOKENS, 2048), bf16)]
        + fwd_scratch(1),
        mib=16,
    )

    common = (info, q, d_out, back_rows, start)

    def back_step(offsets, acc):
        n = len(offsets)
        args = common + tuple(x[o % PLANES] for x in (kvs, wo_grads) for o in offsets)
        return call(
            functools.partial(bwd_kernel, offsets),
            (state_shape[1],) + (sent_shape,) * n,
            args if acc is None else args + (acc,),
            (5 * n * score, 3 << 20, n << 20),
            scratch=bwd_scratch(n),
            alias=None if acc is None else {len(args): 0},
        )

    acc, down, up = back_step((-4, 3), None)
    kept, sent = call(
        attn_kernel,
        (shape(2, TOKENS // SIDE, 2048),) * 2,
        (place, mixed_t, w_out),
        (2 * TOKENS * 2048 * WO, 4 << 20, 0),
        scratch=[pltpu.VMEM((TOKENS, WO), f32)],
    )
    acc, kept = tie((acc, kept))
    token_block = shape(TOKENS // SIDE, 2048)
    attn, across = call(cores_kernel, (token_block,) * 2, (kept, beside(sent, 1)), scalars=0)
    down, up = along(down, -1), along(up, 1)
    for offsets in ((-3, 2), (-2, 1)):
        acc, *terms = back_step(offsets, acc)
        down, up = add(down, terms[0]), add(up, terms[1])
        acc, _, _, across = tie((acc, down, up, across))
        down, up = along(down, -1), along(up, 1)
    across = beside(across, 2)
    acc, term = back_step((-1,), acc)
    down = add(down, term)
    acc, _ = tie((acc, down))
    down = along(down, -1)
    own_kv, q_grads = call(
        own_kernel,
        (shape(TOKENS, 128, dtype=f32), shape(PLANES, WO, ROWS)),
        (*common, kvs[0], acc, cos_t, sin_t, normed),
        (5 * score + 2 * TOKENS * 2048 * WO, 5 << 20, 1 << 20),
        scratch=[pltpu.VMEM((256, TOKENS), f32), pltpu.VMEM((WO, TOKENS), bf16)] + bwd_scratch(1),
    )
    attn = add(attn, across)
    own_kv, attn = tie((own_kv, attn))
    wo_sum, *grads = call(
        last_kernel,
        (shape(TOKENS, 128, dtype=f32),) + (shape(QKV, ROWS),) * PLANES,
        (info, own_kv, wo_grads[0], down, up, cos_t, sin_t, normed, q_grads),
        (2 * TOKENS * 2048 * 128, 6 << 20, 0),
        scratch=[pltpu.VMEM((128, TOKENS), bf16)],
    )
    down, up = ring_scatter(grads)
    sent = call(
        split_kernel,
        (shape(64, QKV + WO),) * SIDE,
        (place, down, up, grads[0], wo_sum),
        scratch=[pltpu.VMEM((ROWS, QKV + WO), f32)],
    )
    got = [sent[0]] + [beside(sent[k], k) for k in range(1, SIDE)]
    whole = shape(*old_w.shape, dtype=f32)
    new_m, sent = call(
        step_kernel,
        (whole, shape(*old_w.shape)),
        (place, old_m, *got),
        scratch=[pltpu.VMEM((SIDE, 64, QKV + WO), bf16)],
    )
    other = lax.switch(bit[0], [functools.partial(swap, b) for b in range(bits)], sent)
    out_w, out_m = call(mean_kernel, (whole, whole), (bit, old_w, new_m, other, *partners))
    return (attn[None], out_w[None], out_m[None])


def solution(mesh):
    return jax.shard_map(
        on_device,
        mesh=mesh,
        in_specs=(
            P("group", "fsdp", None),
            P("group", None),
            P("group", "fsdp", None),
            P("group", "fsdp", None),
            P("group", "fsdp", None),
            P("group", "fsdp"),
            P(),
        ),
        out_specs=(P("group", "fsdp", None), P("group", "fsdp", None), P("group", "fsdp", None)),
        check_vma=False,
    )
```

```python
import functools
import math

import jax
import jax.numpy as jnp
from jax import lax
from jax.experimental import pallas as pl
from jax.experimental.pallas import tpu as pltpu
from jax.sharding import PartitionSpec as P

QUERY_HEADS = 16
KEY_VALUE_HEADS = 4
HEAD_SIZE = 64
REPEAT = QUERY_HEADS // KEY_VALUE_HEADS

EPS = 1e-05
BETA = 0.9
RATE = 0.01
THETA = 500000.0
MASK_FILL = -1e30
TOP_START = -1e20

PLANES = 8
SIDE = 4
TOKENS = 512
ROWS = 256
QKV = 384
WO = 256
NT = (((1,), (1,)), ((), ()))
NN = (((1,), (0,)), ((), ()))

f32 = jnp.float32
bf16 = jnp.bfloat16


def dot(a, b, dims=NN):
    return lax.dot_general(a, b, dims, preferred_element_type=f32)


def along(x, step):
    n = PLANES * SIDE
    return lax.ppermute(x, "fsdp", [(i, (i + SIDE * step) % n) for i in range(n)])


def beside(x, mask):
    return lax.ppermute(x, "fsdp", [(i, i ^ mask) for i in range(PLANES * SIDE)])


def ring_gather(x, second):
    got = [None] * PLANES
    got[0] = x
    down = up = x
    for s in range(1, PLANES // 2 + 1):
        down = along(down, 1)
        if s < PLANES // 2:
            up = along(up, -1)
            if s == 2:
                up, second = lax.optimization_barrier((up, second))
            got[s] = up
        got[-s % PLANES] = down
    return got, second


def call(kernel, outs, args, cost=(1 << 20, 1 << 20, 0), scalars=1, scratch=(), alias=None, mib=8, space=pltpu.VMEM):
    flops, bytes_, exps = cost
    vmem, smem = (pl.BlockSpec(memory_space=m) for m in (pltpu.VMEM, pltpu.SMEM))
    return pl.pallas_call(
        kernel,
        out_shape=tuple(outs),
        in_specs=[smem] * scalars + [pl.BlockSpec(memory_space=space)] * (len(args) - scalars),
        out_specs=tuple(smem if o.shape == INFO.shape else vmem for o in outs),
        scratch_shapes=scratch,
        input_output_aliases=alias or {},
        compiler_params=pltpu.CompilerParams(vmem_limit_bytes=mib * 1024 * 1024),
        cost_estimate=pl.CostEstimate(flops=flops, bytes_accessed=bytes_, transcendentals=exps),
    )(*args)


def shape(*dims, dtype=bf16):
    return jax.ShapeDtypeStruct(dims, dtype)


INFO = shape(3, dtype=jnp.int32)


def add(got, term):
    return call(sum_kernel, (shape(*term.shape),), (got, term), scalars=0, mib=4)[0]


def ring_scatter(terms):
    down, up = along(terms[4], -1), along(terms[3], 1)
    for s in (2, 1):
        down, up = along(add(down, terms[-s - 1]), -1), along(add(up, terms[s]), 1)
    return along(add(down, terms[-1]), -1), up


def prep_kernel(place, *refs):
    sources, normed, rounded, refs = refs[:4], refs[4], refs[5], refs[6:]
    outs, sent, sems = refs[:SIDE], refs[SIDE], refs[-1]
    hidden, gain, weights, seg = refs[SIDE + 1 : SIDE + 5]
    copies = [
        pltpu.make_async_copy(source, to, sems.at[i])
        for i, (source, to) in enumerate(zip(sources, (hidden, gain, weights, seg)))
    ]
    for c in copies:
        c.start()
    for c in copies:
        c.wait()
    rounded[...] = weights[...].astype(bf16)
    x = hidden[...].astype(f32)
    scale = lax.rsqrt(jnp.mean(x * x, axis=1, keepdims=True) + EPS)
    normed[...] = (x * scale * gain[...]).astype(bf16)
    documents = seg[...]
    first, second = (jnp.sum((documents == d).astype(f32)) for d in range(2))
    lane = lanes((16, QKV + WO))
    counts = jnp.where(lane == 0, first, jnp.where(lane == 1, second, 0.0)).astype(bf16)
    for j in range(SIDE):
        cuts = [(256 * j, 256), (1024 + 64 * j, 64), (1280 + 64 * j, 64), (1536 + 256 * j, 256)]
        block = jnp.concatenate([weights[:, at : at + n] for at, n in cuts], axis=1)
        sent[j, :64] = block.astype(bf16)
        sent[j, 64:] = counts
    for k in range(SIDE):
        outs[k][...] = sent[place[1] ^ k]


def join_kernel(place, *refs):
    got, (w_rows, wo_rows) = refs[:SIDE], refs[SIDE:]
    row = lax.broadcasted_iota(jnp.int32, (16, QKV), 0)
    tail = jnp.zeros((16, QKV), f32)
    for k in range(SIDE):
        at = pl.multiple_of((place[1] ^ k) * 64, 64)
        w_rows[pl.ds(at, 64)] = got[k][:64, :QKV]
        wo_rows[pl.ds(at, 64)] = got[k][:64, QKV:]
        tail = jnp.where(row == k, got[k][64:, :QKV].astype(f32), tail)
    w_rows[ROWS:] = tail.astype(bf16)


def sum_kernel(*refs):
    refs[-1][...] = sum(r[...].astype(f32) for r in refs[:-1]).astype(bf16)


def split_kernel(place, down, up, own, wo_sum, *refs):
    outs, total = refs[:SIDE], refs[SIDE]
    qkv = down[...].astype(f32) + up[...].astype(f32) + own[...].astype(f32)
    total[:, :QKV] = qkv.T
    total[:, QKV:] = jnp.concatenate([wo_sum[:ROWS], wo_sum[ROWS:]], axis=1).T
    for k in range(SIDE):
        at = pl.multiple_of((place[1] ^ k) * 64, 64)
        outs[k][...] = total[pl.ds(at, 64)].astype(bf16)


def step_kernel(place, momentum, *refs):
    got, (new_m, sent, by_head) = refs[:SIDE], refs[SIDE:]
    for k in range(SIDE):
        by_head[place[1] ^ k] = got[k][...]
    for lo, n, to in ((0, 256, 0), (256, 64, 1024), (320, 64, 1280), (384, 256, 1536)):
        grad = jnp.concatenate([by_head[j, :, lo : lo + n] for j in range(SIDE)], axis=1)
        at = slice(to, to + SIDE * n)
        m = BETA * momentum[:, at] + grad.astype(f32)
        new_m[:, at] = m
        sent[:, at] = m.astype(bf16)


def mean_kernel(bit, w, m, other, *refs):
    partners, (out_w, out_m) = refs[:-2], refs[-2:]
    mean_m = 0.5 * (m[...] + other[...].astype(f32))
    out_m[...] = mean_m
    for b, partner in enumerate(partners):

        @pl.when(bit[0] == b)
        def _():
            out_w[...] = 0.5 * (w[...] + partner[...].astype(f32)) - RATE * mean_m


def plane_at(info, offset):
    return lax.rem(info[0] + (offset % PLANES), PLANES)


def lanes(shape):
    return lax.broadcasted_iota(jnp.int32, shape, len(shape) - 1)


def proj_kernel(place, cos, sin, wo_rows, *refs):
    parts, blocks = refs[:SIDE], refs[SIDE : SIDE + PLANES]
    normed, q_out, kv_out, start, info = refs[SIDE + PLANES :]
    for k in range(SIDE):
        at = pl.multiple_of((place[1] ^ k) * 128, 128)
        normed[pl.ds(at, 128)] = parts[k][...]
    total = jnp.zeros((TOKENS, QKV), f32)
    for o in range(PLANES):
        at = pl.multiple_of(plane_at(place, o) * ROWS, ROWS)
        total = total + dot(normed[:, pl.ds(at, ROWS)], blocks[o][:ROWS])

    tails = sum(b[ROWS : ROWS + 16].astype(f32)[:SIDE, :128] for b in blocks)
    lane = lanes(tails.shape)
    second = jnp.sum(jnp.where(lane == 0, tails, 0.0)).astype(jnp.int32)
    third = second + jnp.sum(jnp.where(lane == 1, tails, 0.0)).astype(jnp.int32)

    def start_of(t):
        return jnp.where(t >= third, third, jnp.where(t >= second, second, 0))

    start[...] = start_of(positions(place))
    info[0] = place[0]
    info[1] = start_of(place[0] * TOKENS)
    info[2] = start_of(place[0] * TOKENS + TOKENS - 1)

    lane = lanes((TOKENS, 128))
    first = lax.rem(lane, HEAD_SIZE) < HEAD_SIZE // 2
    low = lane < HEAD_SIZE
    c, s = cos[...], sin[...]

    def turned(u):
        return jnp.where(first, pltpu.roll(u, 96, 1), pltpu.roll(u, 32, 1))

    for pair in range(2):
        u = total[:, 128 * pair : 128 * pair + 128]
        u = (u * c + turned(u) * s) * (1.0 / math.sqrt(HEAD_SIZE))
        q_out[2 * pair] = jnp.where(low, u, 0.0).astype(bf16)
        q_out[2 * pair + 1] = jnp.where(low, pltpu.roll(u, 64, 1), 0.0).astype(bf16)
    u = total[:, 256:]
    kv_out[:TOKENS] = jnp.where(low, u * c + turned(u) * s, u).astype(bf16)
    kv_out[TOKENS : TOKENS + ROWS] = wo_rows[:, :128]
    kv_out[TOKENS + ROWS :] = wo_rows[:, 128:]


def masked(s, src, qpos, start):
    kpos = src * TOKENS + lax.broadcasted_iota(jnp.int32, (TOKENS, TOKENS), 0)
    return jnp.where((kpos <= qpos) & (kpos >= start), s, MASK_FILL)


def on_blocks(info, offsets, body):
    def step(i, carry):
        src = plane_at(info, offsets[0])
        for n, o in enumerate(offsets[1:], 1):
            src = jnp.where(i == n, plane_at(info, o), src)
        base = src * TOKENS
        seen = (src <= info[0]) & (base + TOKENS > info[1])
        edge = (src == info[0]) | (base < info[2])

        @pl.when(seen & edge)
        def _():
            body(i, src, True)

        if offsets != (0,):

            @pl.when(seen & jnp.logical_not(edge))
            def _():
                body(i, src, False)

        return carry

    lax.fori_loop(0, len(offsets), step, 0)


def for_heads(body):
    def step(h, carry):
        body(h, pl.ds(pl.multiple_of(h * HEAD_SIZE, HEAD_SIZE), HEAD_SIZE))
        return carry

    lax.fori_loop(0, REPEAT, step, 0)


def positions(info):
    return info[0] * TOKENS + lax.broadcasted_iota(jnp.int32, (1, TOKENS), 1)


def fwd_blocks(info, offsets, q, kvs, start, rows, acc, kv, value_t):
    for i, ref in enumerate(kvs):
        kv[i] = ref[:TOKENS]

    def block(i, src, mask):
        value_t[...] = kv[i].T[HEAD_SIZE:]

        def head(h, at):
            s = dot(kv[i], q[h], NT)
            if mask:
                s = masked(s, src, positions(info), start[...])
            old = rows[h]
            top = jnp.maximum(old, jnp.max(s, axis=0, keepdims=True))
            p = jnp.exp(s - top)
            fade = jnp.exp(old - top)
            rows[h] = top
            rows[4 + h] = rows[4 + h] * fade + jnp.sum(p, axis=0, keepdims=True)
            acc[at] = acc[at] * fade + dot(value_t[...], p.astype(bf16))

        for_heads(head)

    on_blocks(info, offsets, block)


def fwd_scratch(n):
    return [pltpu.VMEM((n, TOKENS, 128), bf16), pltpu.VMEM((HEAD_SIZE, TOKENS), bf16)]


def fwd_kernel(offsets, info, q, start, *refs):
    n = len(offsets)
    kvs, refs = refs[:n], refs[n:]
    if offsets[0] == 0:
        rows, acc, *scratch = refs
        rows[0:4] = jnp.full((4, 1, TOKENS), TOP_START, f32)
        rows[4:8] = jnp.zeros((4, 1, TOKENS), f32)
        acc[...] = jnp.zeros(acc.shape, f32)
    else:
        rows_in, acc_in, rows, acc, *scratch = refs
        rows[...] = rows_in[...]
        acc[...] = acc_in[...]
    fwd_blocks(info, offsets, q, kvs, start, rows, acc, *scratch)


def out_block(ref):
    return jnp.concatenate([ref[TOKENS : TOKENS + ROWS], ref[TOKENS + ROWS :]], axis=1)


def mid_kernel(info, place, q, start, kv, rows_in, acc_in, *refs):
    parts, blocks, refs = refs[:SIDE], refs[SIDE : SIDE + PLANES], refs[SIDE + PLANES :]
    mixed_t, d_out, back_rows, w_out = refs[:4]
    grads, (rows, acc, cot, *scratch) = refs[4 : 4 + PLANES], refs[4 + PLANES :]
    rows[...] = rows_in[...]
    acc[...] = acc_in[...]
    fwd_blocks(info, (-4,), q, (kv,), start, rows, acc, *scratch)
    for k in range(SIDE):
        at = pl.multiple_of((place[1] ^ k) * 128, 128)
        cot[pl.ds(at, 128)] = parts[k][...]
    for o in range(PLANES):
        at = pl.multiple_of(plane_at(info, o) * ROWS, ROWS)
        w_out[pl.ds(at, ROWS)] = out_block(blocks[o])
    d_mixed = dot(cot[...], w_out[...]).astype(bf16).astype(f32)
    inverse = jnp.concatenate([1.0 / rows[4 + h] for h in range(REPEAT)], axis=0)
    back_rows[0:4] = rows[0:4]
    for h in range(REPEAT):
        at = slice(64 * h, 64 * h + 64)
        mixed_t[at] = (acc[at] * inverse[h : h + 1]).astype(bf16)
    mt = mixed_t[...]
    prod = d_mixed.T * mt.astype(f32)
    for h in range(REPEAT):
        back_rows[4 + h] = inverse[h : h + 1] * jnp.sum(
            prod[64 * h : 64 * h + 64], axis=0, keepdims=True
        )
    by_row = jnp.concatenate([inverse, inverse], axis=0).T
    high = lanes((TOKENS, 128)) >= HEAD_SIZE
    for pair in range(2):
        u = d_mixed[:, 128 * pair : 128 * pair + 128]
        scale = [by_row[:, 2 * pair + i : 2 * pair + i + 1] for i in range(2)]
        u = u * jnp.where(high, scale[1], scale[0])
        d_out[2 * pair] = jnp.where(high, pltpu.roll(u, 64, 1), 0.0).astype(bf16)
        d_out[2 * pair + 1] = jnp.where(high, u, 0.0).astype(bf16)
    for o in range(PLANES):
        at = pl.multiple_of(plane_at(info, o) * ROWS, ROWS)
        term = dot(mt, cot[:, pl.ds(at, ROWS)]).astype(bf16)
        grads[o][:ROWS] = term[:, :128]
        grads[o][ROWS:] = term[:, 128:]


def attn_kernel(place, mixed_t, w_out, kept, sent, mixed):
    mixed[...] = mixed_t[...].astype(f32).T
    for k in range(SIDE):
        at = pl.multiple_of((place[1] ^ k) * 128, 128)
        out = sent if k % 2 else kept
        out[k // 2] = dot(mixed[pl.ds(at, 128)].astype(bf16), w_out[...], NT).astype(bf16)


def cores_kernel(a, b, own, across):
    own[...] = (a[0].astype(f32) + b[0].astype(f32)).astype(bf16)
    across[...] = (a[1].astype(f32) + b[1].astype(f32)).astype(bf16)


def bwd_blocks(info, offsets, q, d_out, rows, kvs, start, acc, sums, kv, key_t):
    for i, ref in enumerate(kvs):
        kv[i] = ref[:TOKENS]
        sums[i] = jnp.zeros((TOKENS, 128), f32)

    def block(i, src, mask):
        key_t[...] = kv[i].T[:HEAD_SIZE]

        def head(h, at):
            s = dot(kv[i], q[h], NT)
            if mask:
                s = masked(s, src, positions(info), start[...])
            p = jnp.exp(s - rows[h])
            dp = dot(kv[i], d_out[h], NT)
            ds = (p * (dp - rows[4 + h])).astype(bf16)
            sums[i] = sums[i] + (dot(p.astype(bf16), d_out[h]) + dot(ds, q[h]))
            acc[at] = acc[at] + dot(key_t[...], ds)

        for_heads(head)

    on_blocks(info, offsets, block)


def bwd_scratch(n):
    return [pltpu.VMEM((n, TOKENS, 128), f32)] + fwd_scratch(n)


def bwd_kernel(offsets, info, q, d_out, rows, start, *refs):
    n = len(offsets)
    kvs, wo_terms, refs, scratch = refs[:n], refs[n : 2 * n], refs[2 * n : -3], refs[-3:]
    acc, outs = refs[-n - 1], refs[-n:]
    acc[...] = refs[0][...] if len(refs) > n + 1 else jnp.zeros(acc.shape, f32)
    bwd_blocks(info, offsets, q, d_out, rows, kvs, start, acc, *scratch)
    for i in range(n):
        outs[i][:TOKENS] = scratch[0][i].astype(bf16)
        outs[i][TOKENS:] = wo_terms[i][...]


def turn_back(u, c, s, out, at, scale):
    one, two = u[:32], u[32:]
    out[at : at + 32] = ((one * c + two * s) * scale).astype(bf16)
    out[at + 32 : at + 64] = ((two * c - one * s) * scale).astype(bf16)


def own_kernel(
    info, q, d_out, rows, start, kv, acc_in, cos_t, sin_t, normed,
    out, grads, acc, d_t, *scratch,
):
    acc[...] = acc_in[...]
    bwd_blocks(info, (0,), q, d_out, rows, (kv,), start, acc, *scratch)
    out[...] = scratch[0][0]
    c, s = cos_t[...], sin_t[...]
    for h in range(REPEAT):
        turn_back(acc[64 * h : 64 * h + 64], c, s, d_t, 64 * h, 1.0 / math.sqrt(HEAD_SIZE))
    for o in range(PLANES):
        at = pl.multiple_of(plane_at(info, o) * ROWS, ROWS)
        grads[o] = dot(d_t[...], normed[:, pl.ds(at, ROWS)]).astype(bf16)


def last_kernel(info, own, wo_own, got_a, got_b, cos_t, sin_t, normed, q_grads, *refs):
    wo_sum, grads, d_t = refs[0], refs[1 : 1 + PLANES], refs[1 + PLANES]
    got = got_a[...].astype(f32) + got_b[...].astype(f32)
    kv_t = (got[:TOKENS] + own[...]).T
    wo_sum[...] = got[TOKENS:] + wo_own[...].astype(f32)
    turn_back(kv_t[:64], cos_t[...], sin_t[...], d_t, 0, 1.0)
    d_t[64:128] = kv_t[64:].astype(bf16)
    for o in range(PLANES):
        at = pl.multiple_of(plane_at(info, o) * ROWS, ROWS)
        grads[o][:WO] = q_grads[o]
        grads[o][WO:] = dot(d_t[...], normed[:, pl.ds(at, ROWS)]).astype(bf16)


def on_device(hidden, gain, weights, momentum, cotangent, segment, distance):
    rank = lax.axis_index("fsdp")
    plane, own = rank // SIDE, rank % SIDE
    old_w, old_m = weights[0], momentum[0]
    place = jnp.stack([plane, own]).astype(jnp.int32)

    tie = lax.optimization_barrier

    half = HEAD_SIZE // 2
    tokens = plane * TOKENS + jnp.arange(TOKENS, dtype=jnp.int32)
    freq = jnp.power(THETA, -jnp.arange(half, dtype=f32) * 2.0 / HEAD_SIZE)
    angle = tokens.astype(f32)[:, None] * freq[None, :]
    cosine, sine = jnp.cos(angle), jnp.sin(angle)
    cos_rows = jnp.concatenate([cosine] * 4, axis=1)
    sin_rows = jnp.concatenate([-sine, sine] * 2, axis=1)
    cos_t, sin_t = cosine.T, sine.T

    normed, rounded, *sent = call(
        prep_kernel,
        (shape(128, 2048), shape(*old_w.shape)) + (shape(80, QKV + WO),) * SIDE,
        (place, hidden[0], gain, old_w, segment),
        scratch=[
            pltpu.VMEM((SIDE, 80, QKV + WO), bf16),
            pltpu.VMEM((128, 2048), bf16),
            pltpu.VMEM(gain.shape, f32),
            pltpu.VMEM(old_w.shape, f32),
            pltpu.VMEM(segment.shape, jnp.int32),
            pltpu.SemaphoreType.DMA((4,)),
        ],
        space=pl.ANY,
        mib=60,
    )
    got = [sent[0]] + [beside(sent[k], k) for k in range(1, SIDE)]
    w_rows, wo_rows = call(join_kernel, (shape(ROWS + 16, QKV), shape(ROWS, WO)), (place, *got))
    w_rows, cos_rows, sin_rows, cos_t, sin_t = tie((w_rows, cos_rows, sin_rows, cos_t, sin_t))

    groups = lax.axis_size("group")
    bits = groups.bit_length() - 1
    bit = jnp.remainder(distance, bits).astype(jnp.int32)

    def swap(b, x):
        return lax.ppermute(x, "group", [(i, i ^ 1 << b) for i in range(groups)])

    w_qkv, across = ring_gather(w_rows, beside(normed, 2))
    parts = [normed, beside(normed, 1), across, beside(across, 1)]
    parts[0], *partners = tie((parts[0], *[swap(b, rounded) for b in range(bits)]))

    state_shape = (shape(8, 1, TOKENS, dtype=f32), shape(256, TOKENS, dtype=f32))
    head_shape = shape(REPEAT, TOKENS, 128)
    sent_shape = shape(2 * TOKENS, 128)
    score = 2 * REPEAT * TOKENS * TOKENS * 128

    normed, q, kv, start, info = call(
        proj_kernel,
        (shape(TOKENS, 2048), head_shape, sent_shape, shape(1, TOKENS, dtype=jnp.int32), INFO),
        (place, cos_rows, sin_rows, wo_rows, *parts, *w_qkv),
        (2 * TOKENS * 2048 * QKV, 8 << 20, 0),
    )

    cot, _ = lax.optimization_barrier((cotangent[0], q))
    across = beside(cot, 2)
    cots = [cot, beside(cot, 1), across, beside(across, 1)]
    def forward_step(offsets, state):
        n = len(offsets)
        return call(
            functools.partial(fwd_kernel, offsets),
            state_shape,
            (info, q, start, *[kvs[o] for o in offsets], *state),
            (2 * n * score, 2 << 20, n << 20),
            scratch=fwd_scratch(n),
            alias={3 + n: 0, 4 + n: 1} if state else None,
        )

    kvs = {0: kv, -1: along(kv, 1), 1: along(kv, -1)}
    state = forward_step((0,), ())
    for s in (1, 2, 3):
        kvs[-s - 1] = along(tie((kvs[-s], state[0]))[0], 1)
        if s < 3:
            kvs[s + 1] = along(tie((kvs[s], state[0]))[0], -1)
        state = forward_step((-s, s), state)
    kvs = [kvs[o - PLANES if o >= PLANES // 2 else o] for o in range(PLANES)]

    mixed_t, d_out, back_rows, w_out, *wo_grads = call(
        mid_kernel,
        (shape(256, TOKENS), head_shape, state_shape[0], shape(2048, WO))
        + (shape(TOKENS, 128),) * PLANES,
        (info, place, q, start, kvs[4], *state, *cots, *kvs),
        (2 * score + 4 * TOKENS * 2048 * WO, 8 << 20, 1 << 20),
        scalars=2,
        scratch=[pltpu.VMEM((8, 1, TOKENS), f32), pltpu.VMEM((256, TOKENS), f32)]
        + [pltpu.VMEM((TOKENS, 2048), bf16)]
        + fwd_scratch(1),
        mib=16,
    )

    common = (info, q, d_out, back_rows, start)

    def back_step(offsets, acc):
        n = len(offsets)
        args = common + tuple(x[o % PLANES] for x in (kvs, wo_grads) for o in offsets)
        return call(
            functools.partial(bwd_kernel, offsets),
            (state_shape[1],) + (sent_shape,) * n,
            args if acc is None else args + (acc,),
            (5 * n * score, 3 << 20, n << 20),
            scratch=bwd_scratch(n),
            alias=None if acc is None else {len(args): 0},
        )

    acc, down, up = back_step((-4, 3), None)
    kept, sent = call(
        attn_kernel,
        (shape(2, TOKENS // SIDE, 2048),) * 2,
        (place, mixed_t, w_out),
        (2 * TOKENS * 2048 * WO, 4 << 20, 0),
        scratch=[pltpu.VMEM((TOKENS, WO), f32)],
    )
    acc, kept = tie((acc, kept))
    token_block = shape(TOKENS // SIDE, 2048)
    attn, across = call(cores_kernel, (token_block,) * 2, (kept, beside(sent, 1)), scalars=0)
    down, up = along(down, -1), along(up, 1)
    for offsets in ((-3, 2), (-2, 1)):
        acc, *terms = back_step(offsets, acc)
        down, up = add(down, terms[0]), add(up, terms[1])
        acc, _, _, across = tie((acc, down, up, across))
        down, up = along(down, -1), along(up, 1)
    across = beside(across, 2)
    acc, term = back_step((-1,), acc)
    down = add(down, term)
    acc, _ = tie((acc, down))
    down = along(down, -1)
    own_kv, q_grads = call(
        own_kernel,
        (shape(TOKENS, 128, dtype=f32), shape(PLANES, WO, ROWS)),
        (*common, kvs[0], acc, cos_t, sin_t, normed),
        (5 * score + 2 * TOKENS * 2048 * WO, 5 << 20, 1 << 20),
        scratch=[pltpu.VMEM((256, TOKENS), f32), pltpu.VMEM((WO, TOKENS), bf16)] + bwd_scratch(1),
    )
    attn = add(attn, across)
    own_kv, attn = tie((own_kv, attn))
    wo_sum, *grads = call(
        last_kernel,
        (shape(TOKENS, 128, dtype=f32),) + (shape(QKV, ROWS),) * PLANES,
        (info, own_kv, wo_grads[0], down, up, cos_t, sin_t, normed, q_grads),
        (2 * TOKENS * 2048 * 128, 6 << 20, 0),
        scratch=[pltpu.VMEM((128, TOKENS), bf16)],
    )
    down, up = ring_scatter(grads)
    sent = call(
        split_kernel,
        (shape(64, QKV + WO),) * SIDE,
        (place, down, up, grads[0], wo_sum),
        scratch=[pltpu.VMEM((ROWS, QKV + WO), f32)],
    )
    got = [sent[0]] + [beside(sent[k], k) for k in range(1, SIDE)]
    whole = shape(*old_w.shape, dtype=f32)
    new_m, sent = call(
        step_kernel,
        (whole, shape(*old_w.shape)),
        (place, old_m, *got),
        scratch=[pltpu.VMEM((SIDE, 64, QKV + WO), bf16)],
    )
    other = lax.switch(bit[0], [functools.partial(swap, b) for b in range(bits)], sent)
    out_w, out_m = call(mean_kernel, (whole, whole), (bit, old_w, new_m, other, *partners))
    return (attn[None], out_w[None], out_m[None])


def solution(mesh):
    return jax.shard_map(
        on_device,
        mesh=mesh,
        in_specs=(
            P("group", "fsdp", None),
            P("group", None),
            P("group", "fsdp", None),
            P("group", "fsdp", None),
            P("group", "fsdp", None),
            P("group", "fsdp"),
            P(),
        ),
        out_specs=(P("group", "fsdp", None), P("group", "fsdp", None), P("group", "fsdp", None)),
        check_vma=False,
    )
```
